128 devices in a mesh: dom: 32 (over z, x, core), rep: 4 (over y).
Axes of the slice: x: 4, y: 4, z: 4, core: 2. Of those that a mesh axis runs over, the one named last changes fastest.
Arguments:
- features: bfloat16 [98304, 512], P('dom', 'rep'), may hold values from -6 to 6
- stale_features: bfloat16 [98304, 512], P('dom', 'rep'), may hold values from -6 to 6
- grad_output: bfloat16 [98304, 512], P('dom', 'rep'), may hold values from -6 to 6
- w_neigh: bfloat16 [512, 512], replicated, may hold values from -0.25 to 0.25
- w_self: bfloat16 [512, 512], replicated, may hold values from -0.25 to 0.25
- adj_tiles: bfloat16 [32, 24, 20, 128, 128], P('dom'), may hold values from -0.125 to 0.125
- tile_cols: int32 [32, 24, 20], P('dom'), may hold values from 0 to 119
- send_idx: int32 [32, 32, 384], P('dom'), may hold values from 0 to 3071
- counts: int32 [32, 32], P('dom'), may hold values from 192 to 384, as said below
Outputs:
- out: bfloat16 [98304, 512], P('dom', 'rep')
- grad_input: bfloat16 [98304, 512], P('dom', 'rep')
- grad_stale: float32 [98304, 512], P('dom', 'rep')
- grad_neigh: float32 [512, 512], P('rep')
- grad_self: float32 [512, 512], P('rep')
The draws below stay inside these ranges and needn't reach their ends.
Inputs may be any that keep to these rules, and one draw needn't show every extreme that they name: `counts`: every partition sends exactly 384 live rows to at least one peer; slots at or past the count hold arbitrary rows and are ignored.
All inputs are finite; a program needn't handle non-finite values.
Results may differ from the reference program's by a relative error of at most 0.02.
Values may be sent and summed in bfloat16 or wider, within the bound.
No kernel may reach another device: no remote copies, remote signals or barrier semaphores. Data moves between devices by JAX's collectives and lax.ppermute only.
A program may use at most 192 MiB of HBM per device.

```python
import jax
import jax.numpy as jnp
from jax import lax

D = 512
TILE = 128
ROWS = 3072
B = 384
TPR = 20
NODES = 98304
RT = 24
CT = 120
N_DOM = 32


def draw_counts(key, part):
    key = jax.random.fold_in(key, 7)
    first_key, second_key, busy_key, full_key = jax.random.split(key, 4)
    first = jax.random.randint(first_key, (N_DOM, N_DOM), B // 2, B + 1)
    second = jax.random.randint(second_key, (N_DOM, N_DOM), B // 2, B + 1)
    busy = jax.random.randint(busy_key, (1, N_DOM), 0, 4) == 0
    drawn = jnp.where(busy, jnp.maximum(first, second), jnp.minimum(first, second))
    full_peer = jax.random.randint(full_key, (N_DOM,), 0, N_DOM)
    peers = jnp.arange(N_DOM, dtype=jnp.int32)
    drawn = jnp.where(peers[None, :] == full_peer[:, None], B, drawn)
    return drawn.astype(jnp.int32)


def set_ends(values, key, low, top_value):
    longest = values.shape.index(max(values.shape))
    spots = []
    for shift in (0, 1):
        where = [jax.random.randint(jax.random.fold_in(key, axis), (), 0, length) for axis, length in enumerate(values.shape)]
        where[longest] = (where[longest] + shift) % values.shape[longest]
        spots.append(tuple(where))
    return values.at[spots[0]].set(low).at[spots[1]].set(top_value)


def levels(stream_key, extent, shards, least, top_value):
    loudness, own = 1.0, jax.random.fold_in(stream_key, 6)
    for axis_at, blocks in shards:
        heights = jnp.exp(jax.random.uniform(jax.random.fold_in(own, axis_at), (blocks,), jnp.float32, least / len(shards), top_value / len(shards)))
        loudness = loudness * jnp.repeat(heights, extent[axis_at] // blocks).reshape([-1 if axis == axis_at else 1 for axis in range(len(extent))])
    return loudness


def bell_draw(stream_key, dims, scale, most, shards=(), held_as=jnp.bfloat16):
    result = scale * jax.random.normal(stream_key, dims, jnp.float32)
    if shards:
        result = result * levels(stream_key, dims, shards, -0.22, 0.18)
    return jnp.clip(result, -most, most).astype(held_as)


def setup_inputs(seed: int = 0) -> dict:
    splits = jax.random.split(jax.random.key(seed), 10)
    features = bell_draw(splits[0], (NODES, D), 1.0, 6.0, ((0, 32), (1, 4)))
    stale_features = bell_draw(splits[1], (NODES, D), 1.0, 6.0, ((0, 32), (1, 4)))
    grad_output = bell_draw(splits[2], (NODES, D), 1.0, 6.0, ((0, 32), (1, 4)))
    w_neigh = bell_draw(splits[3], (D, D), D ** -0.5, 0.25)
    w_self = bell_draw(splits[4], (D, D), D ** -0.5, 0.25)
    adj_tiles = bell_draw(splits[5], (N_DOM, RT, TPR, TILE, TILE), (TPR * TILE) ** -0.5, 0.125, ((0, 32),))
    tile_cols = set_ends(jax.random.randint(splits[6], (N_DOM, RT, TPR), 0, CT), jax.random.fold_in(splits[6], 1), 0, CT - 1).astype(jnp.int32)
    send_idx = set_ends(jax.random.randint(splits[7], (N_DOM, N_DOM, B), 0, ROWS), jax.random.fold_in(splits[7], 1), 0, ROWS - 1).astype(jnp.int32)
    counts = draw_counts(jax.random.fold_in(splits[9], 71), 0)
    return {"features": features, "stale_features": stale_features, "grad_output": grad_output, "w_neigh": w_neigh, "w_self": w_self, "adj_tiles": adj_tiles, "tile_cols": tile_cols, "send_idx": send_idx, "counts": counts}


def gelu_tanh(value):
    return jax.nn.gelu(value, approximate=True)

def reference(features, stale_features, grad_output, w_neigh, w_self, adj_tiles, tile_cols, send_idx, counts):
    dom_count = N_DOM
    col_tiles = (ROWS + dom_count * B) // TILE
    stale_parts = stale_features.reshape(dom_count, ROWS, D)
    slot_range = jnp.arange(B, dtype=jnp.int32)
    live_all = slot_range[None, None, :] < counts[:, :, None]
    source_ids = jnp.arange(dom_count, dtype=jnp.int32)

    def one_part(carry, part_id):
        sum_neigh, sum_self, stale_grad = carry
        index_rows = send_idx[:, part_id, :]
        chosen = stale_parts[source_ids[:, None], index_rows]
        live_now = live_all[:, part_id, :]
        halo_rows = jnp.where(live_now[:, :, None], chosen, jnp.zeros_like(chosen)).astype(jnp.bfloat16)
        start_row = (part_id * ROWS).astype(jnp.int32)
        local = lax.dynamic_slice_in_dim(features, start_row, ROWS, 0)
        upstream = lax.dynamic_slice_in_dim(grad_output, start_row, ROWS, 0)
        extended = jnp.concatenate([local, halo_rows.reshape(dom_count * B, D)], axis=0)
        block_ids = tile_cols[part_id]
        blocks = adj_tiles[part_id].astype(jnp.float32)
        picked = extended.reshape(col_tiles, TILE, D)[block_ids].astype(jnp.float32)
        aggregate = jnp.einsum('rtij,rtjf->rif', blocks, picked).reshape(ROWS, D).astype(jnp.bfloat16)
        pre_act = jnp.dot(aggregate, w_neigh, preferred_element_type=jnp.float32) + jnp.dot(local, w_self, preferred_element_type=jnp.float32)
        activated, pullback = jax.vjp(gelu_tanh, pre_act)
        grad_pre = pullback(upstream.astype(jnp.float32))[0].astype(jnp.bfloat16)
        contract_rows = (((0,), (0,)), ((), ()))
        contract_cols = (((1,), (1,)), ((), ()))
        sum_neigh = sum_neigh + lax.dot_general(aggregate, grad_pre, contract_rows, preferred_element_type=jnp.float32)
        sum_self = sum_self + lax.dot_general(local, grad_pre, contract_rows, preferred_element_type=jnp.float32)
        grad_agg = lax.dot_general(grad_pre, w_neigh, contract_cols, preferred_element_type=jnp.float32).astype(jnp.bfloat16)
        grad_direct = lax.dot_general(grad_pre, w_self, contract_cols, preferred_element_type=jnp.float32)
        contrib = jnp.einsum('rtij,rif->rtjf', blocks, grad_agg.reshape(ROWS // TILE, TILE, D).astype(jnp.float32))
        grad_ext = jax.ops.segment_sum(contrib.reshape(-1, TILE, D), block_ids.reshape(-1), num_segments=col_tiles).reshape(-1, D)
        grad_local = (grad_direct + grad_ext[:ROWS]).astype(jnp.bfloat16)
        grad_halo = grad_ext[ROWS:].reshape(dom_count, B, D).astype(jnp.bfloat16).astype(jnp.float32)
        grad_halo = jnp.where(live_now[:, :, None], grad_halo, jnp.zeros_like(grad_halo))
        targets = (source_ids[:, None] * ROWS + index_rows).reshape(-1).astype(jnp.int32)
        stale_grad = stale_grad + jax.ops.segment_sum(grad_halo.reshape(-1, D), targets, num_segments=dom_count * ROWS)
        return ((sum_neigh, sum_self, stale_grad), (activated.astype(jnp.bfloat16), grad_local))
    start = (jnp.zeros((D, D), jnp.float32), jnp.zeros((D, D), jnp.float32), jnp.zeros((dom_count * ROWS, D), jnp.float32))
    (sum_neigh, sum_self, stale_grad), (outputs, grad_locals) = lax.scan(one_part, start, source_ids)
    return (outputs.reshape(-1, D), grad_locals.reshape(-1, D), stale_grad, sum_neigh, sum_self)
```

```python
import functools

import jax
import jax.numpy as jnp
from jax import lax
from jax.experimental import pallas as pl
from jax.experimental.pallas import tpu as pltpu
from jax.sharding import PartitionSpec as P

TILE = 128
B = 384
CHUNKS = B // TILE
LOW = 512
F32 = jnp.float32
BF16 = jnp.bfloat16
NT = (((1,), (1,)), ((), ()))
TN = (((0,), (0,)), ((), ()))


def params(mib):
    return pltpu.CompilerParams(vmem_limit_bytes=mib * 1024 * 1024)


def cost(flops, nbytes, trans=0):
    return pl.CostEstimate(flops=int(flops), bytes_accessed=int(nbytes), transcendentals=int(trans))


def shape(dims, dtype):
    return jax.ShapeDtypeStruct(dims, dtype)


def turned(block):
    return jnp.transpose(block.astype(F32))


def gather_kernel(ids_ref, table_ref, out_ref, flipped):
    rows = table_ref.shape[0]
    groups = rows // LOW

    @pl.when(pl.program_id(0) == 0)
    def _():
        for g in range(groups):
            for k in range(LOW // TILE):
                block = table_ref[g * LOW + k * TILE : g * LOW + (k + 1) * TILE, :]
                flipped[g * TILE : (g + 1) * TILE, k * TILE : (k + 1) * TILE] = turned(block).astype(
                    BF16
                )

    spot = lax.broadcasted_iota(jnp.int32, (LOW, LOW), 0)
    for n in range(ids_ref.shape[1]):
        ids = ids_ref[0, n : n + 1, :]
        onehot = jnp.where(spot == (ids & (LOW - 1)), 1.0, 0.0).astype(BF16)
        found = jnp.dot(flipped[...], onehot, preferred_element_type=F32)
        total = jnp.zeros((TILE, LOW), F32)
        for g in range(groups):
            here = (ids >= g * LOW) & (ids < (g + 1) * LOW)
            total = jnp.where(here, found[g * TILE : (g + 1) * TILE, :], total)
        total = total.astype(BF16)
        for p in range(LOW // TILE):
            out_ref[n * (LOW // TILE) + p] = total[:, p * TILE : (p + 1) * TILE]


def gather_rows(ids, table):
    steps, parts, width = ids.shape
    blocks = parts * width // TILE
    rows, cols = table.shape
    return pl.pallas_call(
        gather_kernel,
        grid=(steps,),
        in_specs=[
            pl.BlockSpec((1, parts, width), lambda i: (i, 0, 0)),
            pl.BlockSpec((rows, cols), lambda i: (0, 0)),
        ],
        out_specs=pl.BlockSpec((blocks, TILE, TILE), lambda i: (i, 0, 0)),
        out_shape=shape((steps * blocks, TILE, TILE), BF16),
        scratch_shapes=[pltpu.VMEM((rows // LOW * TILE, LOW), BF16)],
        compiler_params=params(32),
        cost_estimate=cost(2 * ids.size * rows * cols, 4e6),
        name="gather_rows",
    )(ids, table)


def exchange(pieces):
    n = len(pieces)
    return [pieces[0]] + [
        lax.ppermute(pieces[s], "rep", [(i, (i + s) % n) for i in range(n)]) for s in range(1, n)
    ]


def relative(received):
    n = len(received)
    return [received[(n - j) % n] for j in range(n)]


def prep_kernel(me_ref, feat_ref, up_ref, wn_ref, ws_ref, after_ref, own_ref, wn_out, ws_out, *pieces):
    del after_ref
    step = pl.program_id(0)
    n = len(pieces)
    for k in range(own_ref.shape[0]):
        own_ref[k] = turned(feat_ref[k * TILE : (k + 1) * TILE, :]).astype(BF16)
    for j, piece in enumerate(pieces):
        column = pl.multiple_of(lax.rem(me_ref[0] + j, n) * TILE, TILE)
        wn_out[:, j * TILE : (j + 1) * TILE] = wn_ref[:, pl.ds(column, TILE)]
        ws_out[:, j * TILE : (j + 1) * TILE] = ws_ref[:, pl.ds(column, TILE)]

        @pl.when(step == j)
        def _():
            piece[0] = feat_ref[...]
            piece[1] = up_ref[...]


def prep(me, features, upstream, wn, ws, after, n):
    rows, width = features.shape
    share = rows // n
    full = wn.shape[0]
    chunk = pl.BlockSpec((share, width), lambda i, me: (lax.rem(me[0] + i, n), 0))
    weight = pl.BlockSpec((width, full), lambda i, me: (lax.rem(me[0] + i, n), 0))
    placed = pl.BlockSpec((width, full), lambda i, me: (i, 0))
    own, wn, ws, *pieces = pl.pallas_call(
        prep_kernel,
        grid_spec=pltpu.PrefetchScalarGridSpec(
            num_scalar_prefetch=1,
            grid=(n,),
            in_specs=[chunk, chunk, weight, weight, pl.BlockSpec(memory_space=pl.ANY)],
            out_specs=[
                pl.BlockSpec(
                    (share // TILE, TILE, TILE), lambda i, me: (lax.rem(me[0] + i, n), 0, 0)
                ),
                placed,
                placed,
            ]
            + [pl.BlockSpec((2, share, width), lambda i, me: (0, 0, 0))] * n,
        ),
        out_shape=[
            shape((rows // TILE, TILE, TILE), BF16),
            shape((full, full), BF16),
            shape((full, full), BF16),
        ]
        + [shape((2, share, width), BF16)] * n,
        compiler_params=params(32),
        cost_estimate=cost(1e10, 6e6),
        name="prep",
    )(me, features, upstream, wn, ws, after)
    return own, wn, ws, pieces


def spmm_kernel(me_ref, pos_ref, adj_ref, *refs, n):
    parts, outs, (ext, sems) = refs[: -n - 2], refs[-n - 2 : -2], refs[-2:]
    chunk, part = pl.program_id(0), pl.program_id(1)
    blocks, per_row = adj_ref.shape[:2]

    @pl.when((chunk == 0) & (part == 0))
    def _():
        copies, start = [], 0
        for k, source in enumerate(parts):
            size = source.shape[0]
            copies.append(pltpu.make_async_copy(source, ext.at[pl.ds(start, size)], sems.at[k]))
            start += size
        for copy in copies:
            copy.start()
        for copy in copies:
            copy.wait()

    first = (lax.rem(me_ref[0] + chunk, n) * pl.num_programs(1) + part) * blocks
    done = []
    for r in range(blocks):
        base = (first + r) * per_row
        total = None
        for t in range(0, per_row, 2):
            left = jnp.concatenate([adj_ref[r, t], adj_ref[r, t + 1]], axis=1)
            right = jnp.concatenate([ext[pos_ref[base + t]], ext[pos_ref[base + t + 1]]], axis=1)
            term = lax.dot_general(left, right, NT, preferred_element_type=F32)
            total = term if total is None else total + term
        done.append(total.astype(BF16))
    done = jnp.concatenate(done, axis=0)
    place = pl.ds(pl.multiple_of(part * blocks * TILE, blocks * TILE), blocks * TILE)
    for j, out in enumerate(outs):

        @pl.when(chunk == j)
        def _():
            out[place, :] = done


def spmm(me, pos, adj, parts, n):
    row_tiles, per_row = adj.shape[:2]
    blocks = 3
    inner = row_tiles // n // blocks
    share = row_tiles // n * TILE
    col_tiles = sum(p.shape[0] for p in parts)
    return pl.pallas_call(
        functools.partial(spmm_kernel, n=n),
        grid_spec=pltpu.PrefetchScalarGridSpec(
            num_scalar_prefetch=2,
            grid=(n, inner),
            in_specs=[
                pl.BlockSpec(
                    (blocks, per_row, TILE, TILE),
                    lambda i, k, me, pos: (lax.rem(me[0] + i, n) * inner + k, 0, 0, 0),
                )
            ]
            + [pl.BlockSpec(memory_space=pl.ANY)] * len(parts),
            out_specs=[pl.BlockSpec((share, TILE), lambda i, k, me, pos: (0, 0))] * n,
            scratch_shapes=[
                pltpu.VMEM((col_tiles, TILE, TILE), BF16),
                pltpu.SemaphoreType.DMA((len(parts),)),
            ],
        ),
        out_shape=[shape((share, TILE), BF16)] * n,
        compiler_params=params(52),
        cost_estimate=cost(2 * row_tiles * per_row * TILE**3 * 2, 2e7),
        name="spmm",
    )(me, pos, adj, *parts)


def joined(refs):
    return jnp.concatenate([ref[...] for ref in refs], axis=1)


def dense_kernel(*refs, n):
    agg, both, (wn_ref, ws_ref), rest = refs[:n], refs[n : 2 * n], refs[2 * n : 2 * n + 2], refs[2 * n + 2 :]
    ga, (act_ref, gp_ref) = rest[:n], rest[n:]
    wn = wn_ref[...]
    v = jnp.dot(joined(agg), wn, preferred_element_type=F32) + jnp.dot(
        joined([ref.at[0] for ref in both]), ws_ref[...], preferred_element_type=F32
    )
    root = 0.7978845608028654
    square = v * v
    t = jnp.tanh(root * v * (1.0 + 0.044715 * square))
    half = 0.5 * (1.0 + t)
    slope = half + 0.5 * v * (1.0 - t * t) * (root * (1.0 + 0.134145 * square))
    gp = (joined([ref.at[1] for ref in both]).astype(F32) * slope).astype(BF16)
    act_ref[...] = (v * half).astype(BF16)
    gp_ref[...] = gp
    back = lax.dot_general(wn, gp, NT, preferred_element_type=F32).astype(BF16)
    width = back.shape[0] // n
    for q in range(n):
        ga[q][...] = back[q * width : (q + 1) * width, :]


def dense(agg, both, wn, ws):
    n = len(agg)
    rows, width = agg[0].shape
    full = n * width
    size = 256
    weight = pl.BlockSpec((full, full), lambda i: (0, 0))
    whole = pl.BlockSpec((size, full), lambda i: (i, 0))
    results = pl.pallas_call(
        functools.partial(dense_kernel, n=n),
        grid=(rows // size,),
        in_specs=[pl.BlockSpec((size, width), lambda i: (i, 0))] * n
        + [pl.BlockSpec((2, size, width), lambda i: (0, i, 0))] * n
        + [weight, weight],
        out_specs=[pl.BlockSpec((width, size), lambda i: (0, i))] * n + [whole, whole],
        out_shape=[shape((width, rows), BF16)] * n + [shape((rows, full), BF16)] * 2,
        compiler_params=params(24),
        cost_estimate=cost(6 * rows * full * full, 7e6, rows * full),
        name="dense",
    )(*agg, *both, wn, ws)
    return results[:n], results[n], results[n + 1]


def wgrad_kernel(me_ref, *refs, n):
    agg, both, gp_ref, out_ref = refs[:n], refs[n : 2 * n], refs[2 * n], refs[2 * n + 1]
    gp = gp_ref[...]
    rows = out_ref.shape[2]
    width = agg[0].shape[1]
    for j in range(n):
        for kind, left in enumerate((agg[j][...], both[j][0])):
            term = lax.dot_general(left, gp, TN, preferred_element_type=F32).astype(BF16)
            for i in range(n):
                q = lax.rem(me_ref[0] + i, n)
                for k in range(width // rows):
                    at = (kind * (width // rows) + k) * n + q
                    out_ref[at, j] = term[k * rows : (k + 1) * rows, i * TILE : (i + 1) * TILE]


def wgrad(me, agg, both, gp, dom_count):
    n = len(agg)
    rows, width = agg[0].shape
    size = 2 * width * n // dom_count
    vmem = pl.BlockSpec(memory_space=pltpu.VMEM)
    return pl.pallas_call(
        functools.partial(wgrad_kernel, n=n),
        in_specs=[pl.BlockSpec(memory_space=pltpu.SMEM)] + [vmem] * (2 * n + 1),
        out_specs=vmem,
        out_shape=shape((dom_count, n, size, TILE), BF16),
        compiler_params=params(24),
        cost_estimate=cost(4 * rows * (n * width) ** 2, 4e6),
        name="wgrad",
    )(me, *agg, *both, gp)


def spmm_back_kernel(me_ref, pos_ref, adj_ref, *refs, n):
    ga, outs, (total, left_ref) = refs[:n], refs[n:-2], refs[-2:]
    chunk, part = pl.program_id(0), pl.program_id(1)
    blocks, per_row = adj_ref.shape[:2]

    @pl.when((chunk == 0) & (part == 0))
    def _():
        total[...] = jnp.zeros_like(total)

    for s in range(n):

        @pl.when((chunk == s) & (part == 0))
        def _():
            for k in range(left_ref.shape[0]):
                left_ref[k] = ga[s][:, k * blocks * TILE : (k + 1) * blocks * TILE]

    first = (lax.rem(me_ref[0] + n - chunk, n) * pl.num_programs(1) + part) * blocks
    for r in range(blocks):
        base = (first + r) * per_row
        left = left_ref[part, :, r * TILE : (r + 1) * TILE]
        for t in range(0, per_row, 2):
            right = jnp.concatenate([adj_ref[r, t], adj_ref[r, t + 1]], axis=1)
            both = jnp.dot(left, right, preferred_element_type=F32)
            total[pos_ref[base + t]] += both[:, :TILE]
            total[pos_ref[base + t + 1]] += both[:, TILE:]

    @pl.when((chunk == n - 1) & (part == pl.num_programs(1) - 1))
    def _():
        start = 0
        for out in outs:
            size = out.shape[0]
            out[...] = total[start : start + size].astype(out.dtype)
            start += size


def spmm_back(me, pos, adj, ga, sizes):
    n = len(ga)
    row_tiles, per_row = adj.shape[:2]
    rows = ga[0].shape[1]
    blocks = 3
    inner = row_tiles // n // blocks
    outs = [shape((size, TILE, TILE), F32 if i == 0 else BF16) for i, size in enumerate(sizes)]
    return pl.pallas_call(
        functools.partial(spmm_back_kernel, n=n),
        grid_spec=pltpu.PrefetchScalarGridSpec(
            num_scalar_prefetch=2,
            grid=(n, inner),
            in_specs=[
                pl.BlockSpec(
                    (blocks, per_row, TILE, TILE),
                    lambda i, k, me, pos: (lax.rem(me[0] + n - i, n) * inner + k, 0, 0, 0),
                )
            ]
            + [pl.BlockSpec((TILE, rows), lambda i, k, me, pos: (0, 0))] * n,
            out_specs=[
                pl.BlockSpec((size, TILE, TILE), lambda i, k, me, pos: (0, 0, 0)) for size in sizes
            ],
            scratch_shapes=[
                pltpu.VMEM((sum(sizes), TILE, TILE), F32),
                pltpu.VMEM((inner, TILE, blocks * TILE), BF16),
            ],
        ),
        out_shape=outs,
        compiler_params=params(48),
        cost_estimate=cost(2 * row_tiles * per_row * TILE**3 * 2, 2.2e7),
        name="spmm_back",
    )(me, pos, adj, *ga)


def late_kernel(act_ref, gp_ref, ws_ref, after_ref, *pieces):
    del after_ref
    direct = lax.dot_general(gp_ref[...], ws_ref[...], NT, preferred_element_type=F32).astype(BF16)
    for j, piece in enumerate(pieces):
        piece[0] = act_ref[:, j * TILE : (j + 1) * TILE]
        piece[1] = direct[:, j * TILE : (j + 1) * TILE]


def late(act, gp, ws, after, n):
    rows, full = act.shape
    size = 256
    share = pl.BlockSpec((size, full), lambda i: (i, 0))
    return pl.pallas_call(
        late_kernel,
        grid=(rows // size,),
        in_specs=[
            share,
            share,
            pl.BlockSpec((full, full), lambda i: (0, 0)),
            pl.BlockSpec(memory_space=pl.ANY),
        ],
        out_specs=[pl.BlockSpec((2, size, TILE), lambda i: (0, i, 0))] * n,
        out_shape=[shape((2, rows, TILE), BF16)] * n,
        compiler_params=params(24),
        cost_estimate=cost(1e10, 6e6),
        name="late",
    )(act, gp, ws, after)


def finish_kernel(me_ref, ext_ref, *refs):
    pieces, (out_ref, grad_ref) = refs[:-2], refs[-2:]
    for s, piece in enumerate(pieces):

        @pl.when(pl.program_id(0) == s)
        def _():
            out_ref[...] = piece[0]
            for k in range(ext_ref.shape[0]):
                rows = slice(k * TILE, (k + 1) * TILE)
                total = piece[1, rows, :].astype(F32) + jnp.transpose(ext_ref[k])
                grad_ref[rows, :] = total.astype(BF16)


def finish(me, ext, pieces):
    n = len(pieces)
    share = pieces[0].shape[1]
    placed = pl.BlockSpec((share, TILE), lambda i, me: (lax.rem(me[0] + n - i, n), 0))
    return pl.pallas_call(
        finish_kernel,
        grid_spec=pltpu.PrefetchScalarGridSpec(
            num_scalar_prefetch=1,
            grid=(n,),
            in_specs=[
                pl.BlockSpec(
                    (share // TILE, TILE, TILE), lambda i, me: (lax.rem(me[0] + n - i, n), 0, 0)
                )
            ]
            + [pl.BlockSpec((2, share, TILE), lambda i, me: (0, 0, 0))] * n,
            out_specs=[placed, placed],
        ),
        out_shape=[shape((n * share, TILE), BF16)] * 2,
        compiler_params=params(24),
        cost_estimate=cost(1e6, 7e6),
        name="finish",
    )(me, ext, *pieces)


def scatter_kernel(ids_ref, val_ref, out_ref):
    groups = out_ref.shape[0] // LOW

    @pl.when(pl.program_id(0) == 0)
    def _():
        out_ref[...] = jnp.zeros_like(out_ref)

    ids = ids_ref[0]
    width = ids.shape[1]
    spot = lax.broadcasted_iota(jnp.int32, (LOW, width), 0)
    onehot = jnp.where(spot == (ids & (LOW - 1)), 1.0, 0.0).astype(BF16)
    values = jnp.concatenate([val_ref[p] for p in range(val_ref.shape[0])], axis=1)
    zero = jnp.zeros_like(values)
    for g in range(0, groups, 2):
        pair = [
            jnp.where((ids >= k * LOW) & (ids < (k + 1) * LOW), values, zero) for k in (g, g + 1)
        ]
        both = lax.dot_general(
            onehot, jnp.concatenate(pair, axis=0), NT, preferred_element_type=F32
        )
        out_ref[g * LOW : (g + 1) * LOW, :] += both[:, :TILE]
        out_ref[(g + 1) * LOW : (g + 2) * LOW, :] += both[:, TILE:]


def scatter_rows(ids, values, rows):
    steps, _, width = ids.shape
    blocks = width // TILE
    return pl.pallas_call(
        scatter_kernel,
        grid=(steps,),
        in_specs=[
            pl.BlockSpec((1, 1, width), lambda i: (i, 0, 0)),
            pl.BlockSpec((blocks, TILE, TILE), lambda i: (i, 0, 0)),
        ],
        out_specs=pl.BlockSpec((rows, TILE), lambda i: (0, 0)),
        out_shape=shape((rows, TILE), F32),
        compiler_params=params(32),
        cost_estimate=cost(2 * ids.size * rows * TILE, 4e6),
        name="scatter_rows",
    )(ids, values)


def per_device(
    features, stale_features, grad_output, w_neigh, w_self, adj_tiles, tile_cols, send_idx, counts
):
    dom_count = lax.axis_size("dom")
    n = lax.axis_size("rep")
    row_count, width = features.shape
    row_tiles = row_count // TILE
    swap = functools.partial(
        lax.all_to_all, axis_name="dom", split_axis=0, concat_axis=0, tiled=True
    )
    me = lax.axis_index("rep").astype(jnp.int32).reshape(1)

    live = jnp.arange(B, dtype=jnp.int32)[None, :] < counts[0][:, None]
    ids = jnp.where(live, send_idx[0], -1)
    pos = tile_cols[0].reshape(-1)
    adj = adj_tiles[0]

    packed = gather_rows(ids.reshape(-1, 2, LOW), stale_features)
    halo = swap(packed)
    own, wn, ws, pieces = prep(me, features, grad_output, w_neigh, w_self, packed, n)
    both = relative(exchange(pieces))

    agg = relative(exchange(spmm(me, pos, adj, [own, halo], n)))
    grad_agg, act, grad_pre = dense(agg, both, wn, ws)
    grad_agg = exchange(grad_agg)
    terms = swap(wgrad(me, agg, both, grad_pre, dom_count))

    local, away = spmm_back(me, pos, adj, grad_agg, [row_tiles, dom_count * CHUNKS])
    returned = swap(away)
    pieces = exchange(late(act, grad_pre, ws, away, n))
    out, grad_input = finish(me, local, pieces)

    terms = jnp.sum(terms.astype(F32), axis=0).astype(BF16)
    terms = exchange([terms[j] for j in range(n)])
    terms = sum(t.astype(F32) for t in terms).astype(BF16)
    terms = swap(jnp.broadcast_to(terms[None], (dom_count, *terms.shape)))
    terms = terms.reshape(dom_count // n, n, -1, TILE).astype(F32)
    terms = jnp.transpose(terms, (0, 2, 1, 3)).reshape(2 * width, n * TILE)

    grad_stale = scatter_rows(ids.reshape(-1, 1, 2 * LOW), returned, row_count)
    return (out, grad_input, grad_stale, terms[:width], terms[width:])


def solution(mesh):
    in_specs = (
        P("dom", "rep"),
        P("dom", "rep"),
        P("dom", "rep"),
        P(),
        P(),
        P("dom", None, None, None, None),
        P("dom", None, None),
        P("dom", None, None),
        P("dom", None),
    )
    out_specs = (P("dom", "rep"), P("dom", "rep"), P("dom", "rep"), P("rep", None), P("rep", None))
    return jax.shard_map(
        per_device, mesh=mesh, in_specs=in_specs, out_specs=out_specs, check_vma=False
    )
```

```python
import functools

import jax
import jax.numpy as jnp
from jax import lax
from jax.experimental import pallas as pl
from jax.experimental.pallas import tpu as pltpu
from jax.sharding import PartitionSpec as P

TILE = 128
B = 384
CHUNKS = B // TILE
LOW = 512
F32 = jnp.float32
BF16 = jnp.bfloat16
NT = (((1,), (1,)), ((), ()))
TN = (((0,), (0,)), ((), ()))


def params(mib):
    return pltpu.CompilerParams(vmem_limit_bytes=mib * 1024 * 1024)


def cost(flops, nbytes, trans=0):
    return pl.CostEstimate(flops=int(flops), bytes_accessed=int(nbytes), transcendentals=int(trans))


def shape(dims, dtype):
    return jax.ShapeDtypeStruct(dims, dtype)


def turned(block):
    return jnp.transpose(block.astype(F32))


def masked_ids(ids_ref, counts_ref, first, peers):
    base = pl.program_id(0) * ids_ref.shape[0]
    slot = lax.broadcasted_iota(jnp.int32, (1, ids_ref.shape[1]), 1)
    rows = [
        jnp.where(slot < counts_ref[0, base + p], ids_ref[p : p + 1, :], -1)
        for p in range(first, first + peers)
    ]
    return jnp.concatenate(rows, axis=1)


def low_onehot(ids):
    spot = lax.broadcasted_iota(jnp.int32, (LOW, ids.shape[1]), 0)
    return jnp.where(spot == (ids & (LOW - 1)), 1.0, 0.0).astype(BF16)


def in_group(ids, g):
    return (ids >= g * LOW) & (ids < (g + 1) * LOW)


def gather_kernel(ids_ref, counts_ref, table_ref, out_ref, flipped):
    groups = table_ref.shape[0] // LOW

    @pl.when(pl.program_id(0) == 0)
    def _():
        for g in range(groups):
            for k in range(LOW // TILE):
                block = table_ref[g * LOW + k * TILE : g * LOW + (k + 1) * TILE, :]
                flipped[g * TILE : (g + 1) * TILE, k * TILE : (k + 1) * TILE] = turned(block).astype(
                    BF16
                )

    for p in range(0, ids_ref.shape[0], 2):
        ids = masked_ids(ids_ref, counts_ref, p, 2)
        found = jnp.dot(flipped[...], low_onehot(ids), preferred_element_type=F32)
        total = jnp.zeros((TILE, ids.shape[1]), F32)
        for g in range(groups):
            total = jnp.where(in_group(ids, g), found[g * TILE : (g + 1) * TILE, :], total)
        total = total.astype(BF16)
        for k in range(2 * CHUNKS):
            out_ref[p * CHUNKS + k] = total[:, k * TILE : (k + 1) * TILE]


def gather_rows(ids, counts, table):
    peers = ids.shape[0]
    size = 8
    rows, cols = table.shape
    return pl.pallas_call(
        gather_kernel,
        grid=(peers // size,),
        in_specs=[
            pl.BlockSpec((size, B), lambda i: (i, 0)),
            pl.BlockSpec(memory_space=pltpu.SMEM),
            pl.BlockSpec((rows, cols), lambda i: (0, 0)),
        ],
        out_specs=pl.BlockSpec((size * CHUNKS, TILE, TILE), lambda i: (i, 0, 0)),
        out_shape=shape((peers * CHUNKS, TILE, TILE), BF16),
        scratch_shapes=[pltpu.VMEM((rows // LOW * TILE, LOW), BF16)],
        compiler_params=params(48),
        cost_estimate=cost(2 * ids.size * rows * cols, 4e6),
        name="gather_rows",
    )(ids, counts, table)


def exchange(pieces):
    n = len(pieces)
    return [pieces[0]] + [
        lax.ppermute(pieces[s], "rep", [(i, (i + s) % n) for i in range(n)]) for s in range(1, n)
    ]


def relative(received):
    n = len(received)
    return [received[(n - j) % n] for j in range(n)]


def prep_kernel(
    me_ref, feat_ref, up_ref, wn_ref, ws_ref, adj_ref, after_ref, own_ref, wn_out, ws_out, adj_out, *refs
):
    del after_ref
    pieces, sems = refs[:-1], refs[-1]
    step = pl.program_id(0)
    n = len(pieces)
    part = adj_ref.shape[0] // sems.shape[0]
    copies = [
        pltpu.make_async_copy(
            adj_ref.at[pl.ds(k * part, part)], adj_out.at[pl.ds(k * part, part)], sems.at[k]
        )
        for k in range(sems.shape[0])
    ]

    @pl.when(step == 0)
    def _():
        for copy in copies:
            copy.start()

    for k in range(own_ref.shape[0]):
        own_ref[k] = turned(feat_ref[k * TILE : (k + 1) * TILE, :]).astype(BF16)
    for j, piece in enumerate(pieces):
        column = pl.multiple_of(lax.rem(me_ref[0] + j, n) * TILE, TILE)
        wn_out[:, j * TILE : (j + 1) * TILE] = wn_ref[:, pl.ds(column, TILE)]
        ws_out[:, j * TILE : (j + 1) * TILE] = ws_ref[:, pl.ds(column, TILE)]

        @pl.when(step == j)
        def _():
            piece[0] = feat_ref[...]
            piece[1] = up_ref[...]

    @pl.when(step == n - 1)
    def _():
        for copy in copies:
            copy.wait()


def prep(me, features, upstream, wn, ws, adj, after, n):
    rows, width = features.shape
    share = rows // n
    full = wn.shape[0]
    chunk = pl.BlockSpec((share, width), lambda i, me: (lax.rem(me[0] + i, n), 0))
    weight = pl.BlockSpec((width, full), lambda i, me: (lax.rem(me[0] + i, n), 0))
    placed = pl.BlockSpec((width, full), lambda i, me: (i, 0))
    own, wn, ws, adj, *pieces = pl.pallas_call(
        prep_kernel,
        grid_spec=pltpu.PrefetchScalarGridSpec(
            num_scalar_prefetch=1,
            grid=(n,),
            in_specs=[chunk, chunk, weight, weight] + [pl.BlockSpec(memory_space=pl.ANY)] * 2,
            out_specs=[
                pl.BlockSpec(
                    (share // TILE, TILE, TILE), lambda i, me: (lax.rem(me[0] + i, n), 0, 0)
                ),
                placed,
                placed,
                pl.BlockSpec(memory_space=pl.ANY),
            ]
            + [pl.BlockSpec((2, share, width), lambda i, me: (0, 0, 0))] * n,
            scratch_shapes=[pltpu.SemaphoreType.DMA((4,))],
        ),
        out_shape=[
            shape((rows // TILE, TILE, TILE), BF16),
            shape((full, full), BF16),
            shape((full, full), BF16),
            pltpu.VMEM(adj.shape, BF16),
        ]
        + [shape((2, share, width), BF16)] * n,
        compiler_params=params(16),
        cost_estimate=cost(1e10, 6e6),
        name="prep",
    )(me, features, upstream, wn, ws, adj, after)
    return own, wn, ws, adj, pieces


BLOCKS = 3


def adj_spec(per_row, inner, chunk_of):
    return pl.BlockSpec(
        (BLOCKS, per_row, TILE, TILE),
        lambda i, k, me, pos: (chunk_of(i, me) * inner + k, 0, 0, 0),
    )


def spmm_kernel(me_ref, pos_ref, *refs, n):
    adj, parts, outs, (ext, sems) = refs[0], refs[1 : -n - 2], refs[-n - 2 : -2], refs[-2:]
    chunk, part = pl.program_id(0), pl.program_id(1)
    per_row = adj.shape[1]

    @pl.when((chunk == 0) & (part == 0))
    def _():
        copies, start, at = [], 0, 0
        for source in parts:
            size = source.shape[0] // 4
            for k in range(4):
                copies.append(
                    pltpu.make_async_copy(
                        source.at[pl.ds(k * size, size)], ext.at[pl.ds(start, size)], sems.at[at]
                    )
                )
                start, at = start + size, at + 1
        for copy in copies:
            copy.start()
        for copy in copies:
            copy.wait()

    first = (lax.rem(me_ref[0] + chunk, n) * pl.num_programs(1) + part) * BLOCKS
    done = []
    for r in range(BLOCKS):
        base = (first + r) * per_row
        total = None
        for t in range(0, per_row, 2):
            left = jnp.concatenate([adj[r, t], adj[r, t + 1]], axis=1)
            right = jnp.concatenate([ext[pos_ref[base + t]], ext[pos_ref[base + t + 1]]], axis=1)
            term = lax.dot_general(left, right, NT, preferred_element_type=F32)
            total = term if total is None else total + term
        done.append(total.astype(BF16))
    done = jnp.concatenate(done, axis=0)
    size = BLOCKS * TILE
    place = pl.ds(pl.multiple_of(part * size, size), size)
    for j, out in enumerate(outs):

        @pl.when(chunk == j)
        def _():
            out[place, :] = done


def spmm(me, pos, adj, parts, n):
    row_tiles, per_row = adj.shape[:2]
    inner = row_tiles // n // BLOCKS
    share = row_tiles // n * TILE
    col_tiles = sum(p.shape[0] for p in parts)
    return pl.pallas_call(
        functools.partial(spmm_kernel, n=n),
        grid_spec=pltpu.PrefetchScalarGridSpec(
            num_scalar_prefetch=2,
            grid=(n, inner),
            in_specs=[adj_spec(per_row, inner, lambda i, me: lax.rem(me[0] + i, n))]
            + [pl.BlockSpec(memory_space=pl.ANY)] * len(parts),
            out_specs=[pl.BlockSpec((share, TILE), lambda i, k, me, pos: (0, 0))] * n,
            scratch_shapes=[
                pltpu.VMEM((col_tiles, TILE, TILE), BF16),
                pltpu.SemaphoreType.DMA((4 * len(parts),)),
            ],
        ),
        out_shape=[shape((share, TILE), BF16)] * n,
        compiler_params=params(20),
        cost_estimate=cost(2 * row_tiles * per_row * TILE**3 * 2, 2e7),
        name="spmm",
    )(me, pos, adj, *parts)


def joined(refs):
    return jnp.concatenate([ref[...] for ref in refs], axis=1)


def dense_kernel(*refs, n):
    agg, both, (wn_ref, ws_ref), rest = refs[:n], refs[n : 2 * n], refs[2 * n : 2 * n + 2], refs[2 * n + 2 :]
    ga, (act_ref, gp_ref) = rest[:n], rest[n:]
    wn = wn_ref[...]
    v = jnp.dot(joined(agg), wn, preferred_element_type=F32) + jnp.dot(
        joined([ref.at[0] for ref in both]), ws_ref[...], preferred_element_type=F32
    )
    root = 0.7978845608028654
    square = v * v
    t = jnp.tanh(root * v * (1.0 + 0.044715 * square))
    half = 0.5 * (1.0 + t)
    slope = half + 0.5 * v * (1.0 - t * t) * (root * (1.0 + 0.134145 * square))
    gp = (joined([ref.at[1] for ref in both]).astype(F32) * slope).astype(BF16)
    act_ref[...] = (v * half).astype(BF16)
    gp_ref[...] = gp
    back = lax.dot_general(wn, gp, NT, preferred_element_type=F32).astype(BF16)
    width = back.shape[0] // n
    for q in range(n):
        ga[q][...] = back[q * width : (q + 1) * width, :]


def dense(agg, both, wn, ws):
    n = len(agg)
    rows, width = agg[0].shape
    full = n * width
    size = 256
    weight = pl.BlockSpec((full, full), lambda i: (0, 0))
    whole = pl.BlockSpec((size, full), lambda i: (i, 0))
    results = pl.pallas_call(
        functools.partial(dense_kernel, n=n),
        grid=(rows // size,),
        in_specs=[pl.BlockSpec((size, width), lambda i: (i, 0))] * n
        + [pl.BlockSpec((2, size, width), lambda i: (0, i, 0))] * n
        + [weight, weight],
        out_specs=[pl.BlockSpec((width, size), lambda i: (0, i))] * n + [whole, whole],
        out_shape=[shape((width, rows), BF16)] * n + [pltpu.HBM((rows, full), BF16)] * 2,
        compiler_params=params(24),
        cost_estimate=cost(6 * rows * full * full, 7e6, rows * full),
        name="dense",
    )(*agg, *both, wn, ws)
    return results[:n], results[n], results[n + 1]


def wgrad_kernel(me_ref, *refs, n):
    agg, both, gp_ref, out_ref = refs[:n], refs[n : 2 * n], refs[2 * n], refs[-1]
    gp = gp_ref[...]
    rows = out_ref.shape[2]
    width = agg[0].shape[1]
    for j in range(n):
        for kind, left in enumerate((agg[j][...], both[j][0])):
            term = lax.dot_general(left, gp, TN, preferred_element_type=F32).astype(BF16)
            for i in range(n):
                q = lax.rem(me_ref[0] + i, n)
                for k in range(width // rows):
                    at = (kind * (width // rows) + k) * n + q
                    out_ref[at, j] = term[k * rows : (k + 1) * rows, i * TILE : (i + 1) * TILE]


def wgrad(me, agg, both, gp, after, dom_count):
    n = len(agg)
    rows, width = agg[0].shape
    size = 2 * width * n // dom_count
    vmem = pl.BlockSpec(memory_space=pltpu.VMEM)
    return pl.pallas_call(
        functools.partial(wgrad_kernel, n=n),
        in_specs=[pl.BlockSpec(memory_space=pltpu.SMEM)]
        + [vmem] * (2 * n + 1)
        + [pl.BlockSpec(memory_space=pl.ANY)],
        out_specs=vmem,
        out_shape=shape((dom_count, n, size, TILE), BF16),
        compiler_params=params(24),
        cost_estimate=cost(1e10, 4e6),
        name="wgrad",
    )(me, *agg, *both, gp, after)


PIECES = 6


def spmm_back_kernel(me_ref, pos_ref, *refs, n):
    adj, ga = refs[0], refs[1 : 1 + n]
    local_ref, away_ref, total, left_ref, stage, sems = refs[1 + n :]
    chunk, part = pl.program_id(0), pl.program_id(1)
    per_row = adj.shape[1]
    size = BLOCKS * TILE

    @pl.when((chunk == 0) & (part == 0))
    def _():
        total[...] = jnp.zeros_like(total)

    for s in range(n):

        @pl.when((chunk == s) & (part == 0))
        def _():
            for k in range(left_ref.shape[0]):
                left_ref[k] = ga[s][:, k * size : (k + 1) * size]

    first = (lax.rem(me_ref[0] + n - chunk, n) * pl.num_programs(1) + part) * BLOCKS
    for r in range(BLOCKS):
        base = (first + r) * per_row
        left = left_ref[part, :, r * TILE : (r + 1) * TILE]
        for t in range(0, per_row, 2):
            right = jnp.concatenate([adj[r, t], adj[r, t + 1]], axis=1)
            both = jnp.dot(left, right, preferred_element_type=F32)
            total[pos_ref[base + t]] += both[:, :TILE]
            total[pos_ref[base + t + 1]] += both[:, TILE:]

    @pl.when((chunk == n - 1) & (part == pl.num_programs(1) - 1))
    def _():
        own = local_ref.shape[0]
        step = away_ref.shape[0] // PIECES
        copies = [pltpu.make_async_copy(total.at[pl.ds(0, own)], local_ref, sems.at[PIECES])]
        copies[0].start()
        for k in range(PIECES):
            stage[k * step : (k + 1) * step] = total[own + k * step : own + (k + 1) * step].astype(BF16)
            copies.append(
                pltpu.make_async_copy(
                    stage.at[pl.ds(k * step, step)], away_ref.at[pl.ds(k * step, step)], sems.at[k]
                )
            )
            copies[-1].start()
        for copy in copies:
            copy.wait()


def spmm_back(me, pos, adj, ga, own, away):
    n = len(ga)
    row_tiles, per_row = adj.shape[:2]
    rows = ga[0].shape[1]
    inner = row_tiles // n // BLOCKS
    return pl.pallas_call(
        functools.partial(spmm_back_kernel, n=n),
        grid_spec=pltpu.PrefetchScalarGridSpec(
            num_scalar_prefetch=2,
            grid=(n, inner),
            in_specs=[adj_spec(per_row, inner, lambda i, me: lax.rem(me[0] + n - i, n))]
            + [pl.BlockSpec((TILE, rows), lambda i, k, me, pos: (0, 0))] * n,
            out_specs=[pl.BlockSpec(memory_space=pl.ANY)] * 2,
            scratch_shapes=[
                pltpu.VMEM((own + away, TILE, TILE), F32),
                pltpu.VMEM((inner, TILE, BLOCKS * TILE), BF16),
                pltpu.VMEM((away, TILE, TILE), BF16),
                pltpu.SemaphoreType.DMA((PIECES + 1,)),
            ],
        ),
        out_shape=[pltpu.HBM((own, TILE, TILE), F32), pltpu.HBM((away, TILE, TILE), BF16)],
        compiler_params=params(24),
        cost_estimate=cost(2 * row_tiles * per_row * TILE**3 * 2, 2.2e7),
        name="spmm_back",
    )(me, pos, adj, *ga)


def late_kernel(act_ref, gp_ref, ws_ref, after_ref, *pieces):
    del after_ref
    direct = lax.dot_general(gp_ref[...], ws_ref[...], NT, preferred_element_type=F32).astype(BF16)
    for j, piece in enumerate(pieces):
        piece[0] = act_ref[:, j * TILE : (j + 1) * TILE]
        piece[1] = direct[:, j * TILE : (j + 1) * TILE]


def late(act, gp, ws, after, n):
    rows, full = act.shape
    size = 256
    share = pl.BlockSpec((size, full), lambda i: (i, 0))
    return pl.pallas_call(
        late_kernel,
        grid=(rows // size,),
        in_specs=[
            share,
            share,
            pl.BlockSpec((full, full), lambda i: (0, 0)),
            pl.BlockSpec(memory_space=pl.ANY),
        ],
        out_specs=[pl.BlockSpec((2, size, TILE), lambda i: (0, i, 0))] * n,
        out_shape=[shape((2, rows, TILE), BF16)] * n,
        compiler_params=params(24),
        cost_estimate=cost(1e10, 6e6),
        name="late",
    )(act, gp, ws, after)


def finish_kernel(me_ref, ext_ref, *refs):
    pieces, (out_ref, grad_ref) = refs[:-2], refs[-2:]
    for s, piece in enumerate(pieces):

        @pl.when(pl.program_id(0) == s)
        def _():
            out_ref[...] = piece[0]
            for k in range(ext_ref.shape[0]):
                rows = slice(k * TILE, (k + 1) * TILE)
                total = piece[1, rows, :].astype(F32) + jnp.transpose(ext_ref[k])
                grad_ref[rows, :] = total.astype(BF16)


def finish(me, ext, pieces):
    n = len(pieces)
    share = pieces[0].shape[1]
    placed = pl.BlockSpec((share, TILE), lambda i, me: (lax.rem(me[0] + n - i, n), 0))
    return pl.pallas_call(
        finish_kernel,
        grid_spec=pltpu.PrefetchScalarGridSpec(
            num_scalar_prefetch=1,
            grid=(n,),
            in_specs=[
                pl.BlockSpec(
                    (share // TILE, TILE, TILE), lambda i, me: (lax.rem(me[0] + n - i, n), 0, 0)
                )
            ]
            + [pl.BlockSpec((2, share, TILE), lambda i, me: (0, 0, 0))] * n,
            out_specs=[placed, placed],
        ),
        out_shape=[shape((n * share, TILE), BF16)] * 2,
        compiler_params=params(24),
        cost_estimate=cost(1e6, 7e6),
        name="finish",
    )(me, ext, *pieces)


def scatter_kernel(ids_ref, counts_ref, val_ref, out_ref):
    groups = out_ref.shape[0] // LOW

    @pl.when(pl.program_id(0) == 0)
    def _():
        out_ref[...] = jnp.zeros_like(out_ref)

    for p in range(0, ids_ref.shape[0], 2):
        ids = masked_ids(ids_ref, counts_ref, p, 2)
        onehot = low_onehot(ids)
        values = jnp.concatenate([val_ref[p * CHUNKS + k] for k in range(2 * CHUNKS)], axis=1)
        zero = jnp.zeros_like(values)
        for g in range(0, groups, 2):
            pair = [jnp.where(in_group(ids, k), values, zero) for k in (g, g + 1)]
            both = lax.dot_general(
                onehot, jnp.concatenate(pair, axis=0), NT, preferred_element_type=F32
            )
            out_ref[g * LOW : (g + 1) * LOW, :] += both[:, :TILE]
            out_ref[(g + 1) * LOW : (g + 2) * LOW, :] += both[:, TILE:]


def scatter_rows(ids, counts, values, rows):
    peers = ids.shape[0]
    size = 8
    return pl.pallas_call(
        scatter_kernel,
        grid=(peers // size,),
        in_specs=[
            pl.BlockSpec((size, B), lambda i: (i, 0)),
            pl.BlockSpec(memory_space=pltpu.SMEM),
            pl.BlockSpec((size * CHUNKS, TILE, TILE), lambda i: (i, 0, 0)),
        ],
        out_specs=pl.BlockSpec((rows, TILE), lambda i: (0, 0)),
        out_shape=shape((rows, TILE), F32),
        compiler_params=params(40),
        cost_estimate=cost(2 * ids.size * rows * TILE, 4e6),
        name="scatter_rows",
    )(ids, counts, values)


def sum_kernel(terms_ref, after_ref, *outs):
    del after_ref
    total = jnp.sum(terms_ref[...].astype(F32), axis=0).astype(BF16)
    for j, out in enumerate(outs):
        out[...] = total[j]


def sum_terms(terms, after):
    n = terms.shape[1]
    return pl.pallas_call(
        sum_kernel,
        in_specs=[pl.BlockSpec(memory_space=pltpu.VMEM), pl.BlockSpec(memory_space=pl.ANY)],
        out_specs=[pl.BlockSpec(memory_space=pltpu.VMEM)] * n,
        out_shape=[shape(terms.shape[2:], BF16)] * n,
        compiler_params=params(16),
        cost_estimate=cost(1e9, 1e6),
        name="sum_terms",
    )(terms, after)


def spread_kernel(*refs):
    terms, out_ref = refs[:-2], refs[-1]
    total = terms[0][...].astype(F32)
    for term in terms[1:]:
        total = total + term[...].astype(F32)
    out_ref[...] = jnp.broadcast_to(total.astype(BF16)[None], out_ref.shape)


def spread_terms(terms, after, dom_count):
    return pl.pallas_call(
        spread_kernel,
        in_specs=[pl.BlockSpec(memory_space=pltpu.VMEM)] * len(terms)
        + [pl.BlockSpec(memory_space=pl.ANY)],
        out_specs=pl.BlockSpec(memory_space=pltpu.VMEM),
        out_shape=shape((dom_count, *terms[0].shape), BF16),
        compiler_params=params(8),
        cost_estimate=cost(1e5, 3e5),
        name="spread_terms",
    )(*terms, after)


def place_kernel(terms_ref, *outs):
    rows, width = terms_ref.shape[1:]
    n = outs[0].shape[1] // width
    for at in range(terms_ref.shape[0]):
        group, q = at // n, at % n
        per = outs[0].shape[0] // rows
        out = outs[group // per]
        first = group % per * rows
        out[first : first + rows, q * width : (q + 1) * width] = terms_ref[at].astype(F32)


def place_terms(terms, width, n):
    return pl.pallas_call(
        place_kernel,
        out_shape=[shape((width, n * width), F32)] * 2,
        compiler_params=params(8),
        cost_estimate=cost(1e5, 8e5),
        name="place_terms",
    )(terms)


def per_device(
    features, stale_features, grad_output, w_neigh, w_self, adj_tiles, tile_cols, send_idx, counts
):
    dom_count = lax.axis_size("dom")
    n = lax.axis_size("rep")
    row_count, width = features.shape
    row_tiles = row_count // TILE
    swap = functools.partial(
        lax.all_to_all, axis_name="dom", split_axis=0, concat_axis=0, tiled=True
    )
    me = lax.axis_index("rep").astype(jnp.int32).reshape(1)

    ids = send_idx[0]
    pos = tile_cols[0].reshape(-1)

    packed = gather_rows(ids, counts, stale_features)
    halo = swap(packed)
    own, wn, ws, adj, pieces = prep(
        me, features, grad_output, w_neigh, w_self, adj_tiles[0], packed, n
    )
    both = relative(exchange(pieces))

    agg = relative(exchange(spmm(me, pos, adj, [own, halo], n)))
    grad_agg, act, grad_pre = dense(agg, both, wn, ws)
    grad_agg = exchange(grad_agg)
    terms = swap(wgrad(me, agg, both, grad_pre, grad_agg[1], dom_count))

    local, away = spmm_back(me, pos, adj, grad_agg, row_tiles, dom_count * CHUNKS)
    returned = swap(away)
    pieces = exchange(late(act, grad_pre, ws, away, n))
    out, grad_input = finish(me, local, pieces)

    terms = exchange(sum_terms(terms, away))
    terms = swap(spread_terms(terms, returned, dom_count))
    grad_neigh, grad_self = place_terms(terms, width, n)

    grad_stale = scatter_rows(ids, counts, returned, row_count)
    return (out, grad_input, grad_stale, grad_neigh, grad_self)


def solution(mesh):
    in_specs = (
        P("dom", "rep"),
        P("dom", "rep"),
        P("dom", "rep"),
        P(),
        P(),
        P("dom", None, None, None, None),
        P("dom", None, None),
        P("dom", None, None),
        P("dom", None),
    )
    out_specs = (P("dom", "rep"), P("dom", "rep"), P("dom", "rep"), P("rep", None), P("rep", None))
    return jax.shard_map(
        per_device, mesh=mesh, in_specs=in_specs, out_specs=out_specs, check_vma=False
    )
```

```python
import functools

import jax
import jax.numpy as jnp
from jax import lax
from jax.experimental import pallas as pl
from jax.experimental.pallas import tpu as pltpu
from jax.sharding import PartitionSpec as P

TILE = 128
B = 384
CHUNKS = B // TILE
LOW = 512
F32 = jnp.float32
BF16 = jnp.bfloat16
NT = (((1,), (1,)), ((), ()))
TN = (((0,), (0,)), ((), ()))


def params(mib):
    return pltpu.CompilerParams(vmem_limit_bytes=mib * 1024 * 1024)


def cost(flops, nbytes, trans=0):
    return pl.CostEstimate(flops=int(flops), bytes_accessed=int(nbytes), transcendentals=int(trans))


def shape(dims, dtype):
    return jax.ShapeDtypeStruct(dims, dtype)


def turned(block):
    return jnp.transpose(block.astype(F32))


def masked_ids(ids_ref, counts_ref, first, peers, skipped=0):
    base = (pl.program_id(0) + skipped) * ids_ref.shape[0]
    slot = lax.broadcasted_iota(jnp.int32, (1, ids_ref.shape[1]), 1)
    rows = [
        jnp.where(slot < counts_ref[0, base + p], ids_ref[p : p + 1, :], -1)
        for p in range(first, first + peers)
    ]
    return jnp.concatenate(rows, axis=1)


def low_onehot(ids):
    spot = lax.broadcasted_iota(jnp.int32, (LOW, ids.shape[1]), 0)
    return jnp.where(spot == (ids & (LOW - 1)), 1.0, 0.0).astype(BF16)


def in_group(ids, g):
    return (ids >= g * LOW) & (ids < (g + 1) * LOW)


def gather_kernel(ids_ref, counts_ref, table_ref, out_ref, flipped):
    groups = table_ref.shape[0] // LOW

    @pl.when(pl.program_id(0) == 0)
    def _():
        for g in range(groups):
            for k in range(LOW // TILE):
                block = table_ref[g * LOW + k * TILE : g * LOW + (k + 1) * TILE, :]
                flipped[g * TILE : (g + 1) * TILE, k * TILE : (k + 1) * TILE] = turned(block).astype(
                    BF16
                )

    for p in range(0, ids_ref.shape[0], 2):
        ids = masked_ids(ids_ref, counts_ref, p, 2)
        found = jnp.dot(flipped[...], low_onehot(ids), preferred_element_type=F32)
        total = jnp.zeros((TILE, ids.shape[1]), F32)
        for g in range(groups):
            total = jnp.where(in_group(ids, g), found[g * TILE : (g + 1) * TILE, :], total)
        total = total.astype(BF16)
        for k in range(2 * CHUNKS):
            out_ref[p * CHUNKS + k] = total[:, k * TILE : (k + 1) * TILE]


def gather_rows(ids, counts, table):
    peers = ids.shape[0]
    size = 8
    rows, cols = table.shape
    return pl.pallas_call(
        gather_kernel,
        grid=(peers // size,),
        in_specs=[
            pl.BlockSpec((size, B), lambda i: (i, 0)),
            pl.BlockSpec(memory_space=pltpu.SMEM),
            pl.BlockSpec((rows, cols), lambda i: (0, 0)),
        ],
        out_specs=pl.BlockSpec((size * CHUNKS, TILE, TILE), lambda i: (i, 0, 0)),
        out_shape=shape((peers * CHUNKS, TILE, TILE), BF16),
        scratch_shapes=[pltpu.VMEM((rows // LOW * TILE, LOW), BF16)],
        compiler_params=params(56),
        cost_estimate=cost(2 * ids.size * rows * cols, 4e6),
        name="gather_rows",
    )(ids, counts, table)


def exchange(pieces):
    n = len(pieces)
    return [pieces[0]] + [
        lax.ppermute(pieces[s], "rep", [(i, (i + s) % n) for i in range(n)]) for s in range(1, n)
    ]


def relative(received):
    n = len(received)
    return [received[(n - j) % n] for j in range(n)]


def prep_kernel(me_ref, feat_ref, up_ref, wn_ref, ws_ref, after_ref, own_ref, wn_out, ws_out, *pieces):
    del after_ref
    step = pl.program_id(0)
    n = len(pieces)
    for k in range(own_ref.shape[0]):
        own_ref[k] = turned(feat_ref[k * TILE : (k + 1) * TILE, :]).astype(BF16)
    for j, piece in enumerate(pieces):
        column = pl.multiple_of(lax.rem(me_ref[0] + j, n) * TILE, TILE)
        wn_out[:, j * TILE : (j + 1) * TILE] = wn_ref[:, pl.ds(column, TILE)]
        ws_out[:, j * TILE : (j + 1) * TILE] = ws_ref[:, pl.ds(column, TILE)]

        @pl.when(step == j)
        def _():
            piece[0] = feat_ref[...]
            piece[1] = up_ref[...]


def prep(me, features, upstream, wn, ws, after, n):
    rows, width = features.shape
    share = rows // n
    full = wn.shape[0]
    chunk = pl.BlockSpec((share, width), lambda i, me: (lax.rem(me[0] + i, n), 0))
    weight = pl.BlockSpec((width, full), lambda i, me: (lax.rem(me[0] + i, n), 0))
    placed = pl.BlockSpec((width, full), lambda i, me: (i, 0))
    own, wn, ws, *pieces = pl.pallas_call(
        prep_kernel,
        grid_spec=pltpu.PrefetchScalarGridSpec(
            num_scalar_prefetch=1,
            grid=(n,),
            in_specs=[chunk, chunk, weight, weight, pl.BlockSpec(memory_space=pl.ANY)],
            out_specs=[
                pl.BlockSpec(
                    (share // TILE, TILE, TILE), lambda i, me: (lax.rem(me[0] + i, n), 0, 0)
                ),
                placed,
                placed,
            ]
            + [pl.BlockSpec((2, share, width), lambda i, me: (0, 0, 0))] * n,
        ),
        out_shape=[
            pltpu.HBM((rows // TILE, TILE, TILE), BF16),
            pltpu.HBM((full, full), BF16),
            pltpu.HBM((full, full), BF16),
        ]
        + [shape((2, share, width), BF16)] * n,
        compiler_params=params(56),
        cost_estimate=cost(1e10, 6e6),
        name="prep",
    )(me, features, upstream, wn, ws, after)
    return own, wn, ws, pieces


BLOCKS = 3


def adj_copies(adj_ref, held, sems, inner, n, chunk_of):
    def copy(step):
        first = (chunk_of(step // inner) * inner + lax.rem(step, inner)) * BLOCKS
        return pltpu.make_async_copy(
            adj_ref.at[pl.ds(first, BLOCKS)], held.at[pl.ds(step * BLOCKS, BLOCKS)], sems.at[step]
        )

    return copy


def spmm_kernel(me_ref, pos_ref, *refs, n):
    adj_ref, parts, outs, (ext, sems, adj, adj_sems) = (
        refs[0],
        refs[1 : -n - 4],
        refs[-n - 4 : -4],
        refs[-4:],
    )
    chunk, part = pl.program_id(0), pl.program_id(1)
    inner = adj_sems.shape[0] // n
    step = chunk * inner + part
    per_row = adj.shape[1]
    copy_of = adj_copies(adj_ref, adj, adj_sems, inner, n, lambda c: lax.rem(me_ref[0] + c, n))

    @pl.when((chunk == 0) & (part == 0))
    def _():
        copies, start, at = [], 0, 0
        for source in parts:
            size = source.shape[0] // 4
            for k in range(4):
                copies.append(
                    pltpu.make_async_copy(
                        source.at[pl.ds(k * size, size)], ext.at[pl.ds(start, size)], sems.at[at]
                    )
                )
                start, at = start + size, at + 1
        for copy in copies:
            copy.start()
        for k in range(adj_sems.shape[0]):
            copy_of(k).start()
        for copy in copies:
            copy.wait()

    copy_of(step).wait()
    first = (lax.rem(me_ref[0] + chunk, n) * pl.num_programs(1) + part) * BLOCKS
    done = []
    for r in range(BLOCKS):
        base = (first + r) * per_row
        total = None
        for t in range(0, per_row, 2):
            left = jnp.concatenate([adj[step * BLOCKS + r, t], adj[step * BLOCKS + r, t + 1]], axis=1)
            right = jnp.concatenate([ext[pos_ref[base + t]], ext[pos_ref[base + t + 1]]], axis=1)
            term = lax.dot_general(left, right, NT, preferred_element_type=F32)
            total = term if total is None else total + term
        done.append(total.astype(BF16))
    done = jnp.concatenate(done, axis=0)
    size = BLOCKS * TILE
    place = pl.ds(pl.multiple_of(part * size, size), size)
    for j, out in enumerate(outs):

        @pl.when(chunk == j)
        def _():
            out[place, :] = done


def spmm(me, pos, adj, parts, n):
    row_tiles, per_row = adj.shape[:2]
    inner = row_tiles // n // BLOCKS
    share = row_tiles // n * TILE
    col_tiles = sum(p.shape[0] for p in parts)
    return pl.pallas_call(
        functools.partial(spmm_kernel, n=n),
        grid_spec=pltpu.PrefetchScalarGridSpec(
            num_scalar_prefetch=2,
            grid=(n, inner),
            in_specs=[pl.BlockSpec(memory_space=pl.ANY)] * (1 + len(parts)),
            out_specs=[pl.BlockSpec((share, TILE), lambda i, k, me, pos: (0, 0))] * n,
            scratch_shapes=[
                pltpu.VMEM((col_tiles, TILE, TILE), BF16),
                pltpu.SemaphoreType.DMA((4 * len(parts),)),
                pltpu.VMEM(adj.shape, BF16),
                pltpu.SemaphoreType.DMA((n * inner,)),
            ],
        ),
        out_shape=[shape((share, TILE), BF16)] * n,
        compiler_params=params(52),
        cost_estimate=cost(2 * row_tiles * per_row * TILE**3 * 2, 2e7),
        name="spmm",
    )(me, pos, adj, *parts)


def joined(refs):
    return jnp.concatenate([ref[...] for ref in refs], axis=1)


def dense_kernel(*refs, n):
    agg, both, (wn_ref, ws_ref), rest = refs[:n], refs[n : 2 * n], refs[2 * n : 2 * n + 2], refs[2 * n + 2 :]
    ga, (act_ref, gp_ref) = rest[:n], rest[n:]
    wn = wn_ref[...]
    v = jnp.dot(joined(agg), wn, preferred_element_type=F32) + jnp.dot(
        joined([ref.at[0] for ref in both]), ws_ref[...], preferred_element_type=F32
    )
    root = 0.7978845608028654
    square = v * v
    t = jnp.tanh(root * v * (1.0 + 0.044715 * square))
    half = 0.5 * (1.0 + t)
    slope = half + 0.5 * v * (1.0 - t * t) * (root * (1.0 + 0.134145 * square))
    gp = (joined([ref.at[1] for ref in both]).astype(F32) * slope).astype(BF16)
    act_ref[...] = (v * half).astype(BF16)
    gp_ref[...] = gp
    back = lax.dot_general(wn, gp, NT, preferred_element_type=F32).astype(BF16)
    width = back.shape[0] // n
    for q in range(n):
        ga[q][...] = back[q * width : (q + 1) * width, :]


def dense(agg, both, wn, ws):
    n = len(agg)
    rows, width = agg[0].shape
    full = n * width
    size = 256
    weight = pl.BlockSpec((full, full), lambda i: (0, 0))
    whole = pl.BlockSpec((size, full), lambda i: (i, 0))
    results = pl.pallas_call(
        functools.partial(dense_kernel, n=n),
        grid=(rows // size,),
        in_specs=[pl.BlockSpec((size, width), lambda i: (i, 0))] * n
        + [pl.BlockSpec((2, size, width), lambda i: (0, i, 0))] * n
        + [weight, weight],
        out_specs=[pl.BlockSpec((width, size), lambda i: (0, i))] * n + [whole, whole],
        out_shape=[shape((width, rows), BF16)] * n + [pltpu.HBM((rows, full), BF16)] * 2,
        compiler_params=params(24),
        cost_estimate=cost(6 * rows * full * full, 7e6, rows * full),
        name="dense",
    )(*agg, *both, wn, ws)
    return results[:n], results[n], results[n + 1]


def wgrad_kernel(me_ref, *refs, n):
    agg, both, gp_ref, outs = refs[:n], refs[n : 2 * n], refs[2 * n], refs[-n:]
    gp = gp_ref[...]
    rows = outs[0].shape[1]
    width = agg[0].shape[1]
    for j in range(n):
        for kind, left in enumerate((agg[j][...], both[j][0])):
            term = lax.dot_general(left, gp, TN, preferred_element_type=F32).astype(BF16)
            for i in range(n):
                q = lax.rem(me_ref[0] + i, n)
                for k in range(width // rows):
                    at = (kind * (width // rows) + k) * n + q
                    outs[j][at] = term[k * rows : (k + 1) * rows, i * TILE : (i + 1) * TILE]


def wgrad(me, agg, both, gp, after, dom_count):
    n = len(agg)
    rows, width = agg[0].shape
    size = 2 * width * n // dom_count
    vmem = pl.BlockSpec(memory_space=pltpu.VMEM)
    return pl.pallas_call(
        functools.partial(wgrad_kernel, n=n),
        in_specs=[pl.BlockSpec(memory_space=pltpu.SMEM)]
        + [vmem] * (2 * n + 1)
        + [pl.BlockSpec(memory_space=pl.ANY)],
        out_specs=[vmem] * n,
        out_shape=[shape((dom_count, size, TILE), BF16)] * n,
        compiler_params=params(24),
        cost_estimate=cost(1e10, 4e6),
        name="wgrad",
    )(me, *agg, *both, gp, after)


PIECES = 6


def spmm_back_kernel(me_ref, pos_ref, *refs, n):
    adj_ref, ga = refs[0], refs[1 : 1 + n]
    local_ref, away_ref, total, left_ref, stage, sems, adj, adj_sems = refs[1 + n :]
    chunk, part = pl.program_id(0), pl.program_id(1)
    inner = adj_sems.shape[0] // n
    step = chunk * inner + part
    per_row = adj.shape[1]
    copy_of = adj_copies(adj_ref, adj, adj_sems, inner, n, lambda c: lax.rem(me_ref[0] + n - c, n))
    size = BLOCKS * TILE

    @pl.when((chunk == 0) & (part == 0))
    def _():
        for k in range(adj_sems.shape[0]):
            copy_of(k).start()
        total[...] = jnp.zeros_like(total)

    for s in range(n):

        @pl.when((chunk == s) & (part == 0))
        def _():
            for k in range(left_ref.shape[0]):
                left_ref[k] = ga[s][:, k * size : (k + 1) * size]

    copy_of(step).wait()
    first = (lax.rem(me_ref[0] + n - chunk, n) * pl.num_programs(1) + part) * BLOCKS
    for r in range(BLOCKS):
        base = (first + r) * per_row
        left = left_ref[part, :, r * TILE : (r + 1) * TILE]
        for t in range(0, per_row, 2):
            right = jnp.concatenate([adj[step * BLOCKS + r, t], adj[step * BLOCKS + r, t + 1]], axis=1)
            both = jnp.dot(left, right, preferred_element_type=F32)
            total[pos_ref[base + t]] += both[:, :TILE]
            total[pos_ref[base + t + 1]] += both[:, TILE:]

    @pl.when((chunk == n - 1) & (part == pl.num_programs(1) - 1))
    def _():
        own = local_ref.shape[0]
        step = away_ref.shape[0] // PIECES
        copies = [pltpu.make_async_copy(total.at[pl.ds(0, own)], local_ref, sems.at[PIECES])]
        copies[0].start()
        for k in range(PIECES):
            stage[k * step : (k + 1) * step] = total[own + k * step : own + (k + 1) * step].astype(BF16)
            copies.append(
                pltpu.make_async_copy(
                    stage.at[pl.ds(k * step, step)], away_ref.at[pl.ds(k * step, step)], sems.at[k]
                )
            )
            copies[-1].start()
        for copy in copies:
            copy.wait()


def spmm_back(me, pos, adj, ga, own, away):
    n = len(ga)
    row_tiles, per_row = adj.shape[:2]
    rows = ga[0].shape[1]
    inner = row_tiles // n // BLOCKS
    return pl.pallas_call(
        functools.partial(spmm_back_kernel, n=n),
        grid_spec=pltpu.PrefetchScalarGridSpec(
            num_scalar_prefetch=2,
            grid=(n, inner),
            in_specs=[pl.BlockSpec(memory_space=pl.ANY)]
            + [pl.BlockSpec((TILE, rows), lambda i, k, me, pos: (0, 0))] * n,
            out_specs=[pl.BlockSpec(memory_space=pl.ANY)] * 2,
            scratch_shapes=[
                pltpu.VMEM((own + away, TILE, TILE), F32),
                pltpu.VMEM((inner, TILE, BLOCKS * TILE), BF16),
                pltpu.VMEM((away, TILE, TILE), BF16),
                pltpu.SemaphoreType.DMA((PIECES + 1,)),
                pltpu.VMEM(adj.shape, BF16),
                pltpu.SemaphoreType.DMA((n * inner,)),
            ],
        ),
        out_shape=[pltpu.HBM((own, TILE, TILE), F32), pltpu.HBM((away, TILE, TILE), BF16)],
        compiler_params=params(52),
        cost_estimate=cost(2 * row_tiles * per_row * TILE**3 * 2, 2.2e7),
        name="spmm_back",
    )(me, pos, adj, *ga)


def late_kernel(act_ref, gp_ref, ws_ref, after_ref, *pieces):
    del after_ref
    direct = lax.dot_general(gp_ref[...], ws_ref[...], NT, preferred_element_type=F32).astype(BF16)
    for j, piece in enumerate(pieces):
        piece[0] = act_ref[:, j * TILE : (j + 1) * TILE]
        piece[1] = direct[:, j * TILE : (j + 1) * TILE]


def late(act, gp, ws, after, n):
    rows, full = act.shape
    size = 256
    share = pl.BlockSpec((size, full), lambda i: (i, 0))
    return pl.pallas_call(
        late_kernel,
        grid=(rows // size,),
        in_specs=[
            share,
            share,
            pl.BlockSpec((full, full), lambda i: (0, 0)),
            pl.BlockSpec(memory_space=pl.ANY),
        ],
        out_specs=[pl.BlockSpec((2, size, TILE), lambda i: (0, i, 0))] * n,
        out_shape=[shape((2, rows, TILE), BF16)] * n,
        compiler_params=params(24),
        cost_estimate=cost(1e10, 6e6),
        name="late",
    )(act, gp, ws, after)


def finish_kernel(me_ref, ext_ref, *refs):
    pieces, (out_ref, grad_ref) = refs[:-2], refs[-2:]
    for s, piece in enumerate(pieces):

        @pl.when(pl.program_id(0) == s)
        def _():
            out_ref[...] = piece[0]
            for k in range(ext_ref.shape[0]):
                rows = slice(k * TILE, (k + 1) * TILE)
                total = piece[1, rows, :].astype(F32) + jnp.transpose(ext_ref[k])
                grad_ref[rows, :] = total.astype(BF16)


def finish(me, ext, pieces):
    n = len(pieces)
    share = pieces[0].shape[1]
    placed = pl.BlockSpec((share, TILE), lambda i, me: (lax.rem(me[0] + n - i, n), 0))
    return pl.pallas_call(
        finish_kernel,
        grid_spec=pltpu.PrefetchScalarGridSpec(
            num_scalar_prefetch=1,
            grid=(n,),
            in_specs=[
                pl.BlockSpec(
                    (share // TILE, TILE, TILE), lambda i, me: (lax.rem(me[0] + n - i, n), 0, 0)
                )
            ]
            + [pl.BlockSpec((2, share, TILE), lambda i, me: (0, 0, 0))] * n,
            out_specs=[placed, placed],
        ),
        out_shape=[shape((n * share, TILE), BF16)] * 2,
        compiler_params=params(24),
        cost_estimate=cost(1e6, 7e6),
        name="finish",
    )(me, ext, *pieces)


def scatter_kernel(ids_ref, counts_ref, val_ref, *refs, first):
    before, out_ref = refs[:-1], refs[-1]
    groups = out_ref.shape[0] // LOW

    @pl.when(pl.program_id(0) == 0)
    def _():
        out_ref[...] = before[0][...] if before else jnp.zeros_like(out_ref)

    for p in range(0, ids_ref.shape[0], 2):
        ids = masked_ids(ids_ref, counts_ref, p, 2, first)
        onehot = low_onehot(ids)
        values = jnp.concatenate([val_ref[p * CHUNKS + k] for k in range(2 * CHUNKS)], axis=1)
        zero = jnp.zeros_like(values)
        for g in range(0, groups, 2):
            pair = [jnp.where(in_group(ids, k), values, zero) for k in (g, g + 1)]
            both = lax.dot_general(
                onehot, jnp.concatenate(pair, axis=0), NT, preferred_element_type=F32
            )
            out_ref[g * LOW : (g + 1) * LOW, :] += both[:, :TILE]
            out_ref[(g + 1) * LOW : (g + 2) * LOW, :] += both[:, TILE:]


def scatter_rows(ids, counts, values, rows, first, steps, before):
    size = 8
    whole = pl.BlockSpec((rows, TILE), lambda i: (0, 0))
    extra = [] if before is None else [before]
    return pl.pallas_call(
        functools.partial(scatter_kernel, first=first),
        grid=(steps,),
        in_specs=[
            pl.BlockSpec((size, B), lambda i: (i + first, 0)),
            pl.BlockSpec(memory_space=pltpu.SMEM),
            pl.BlockSpec((size * CHUNKS, TILE, TILE), lambda i: (i + first, 0, 0)),
        ]
        + [whole] * len(extra),
        out_specs=whole,
        out_shape=shape((rows, TILE), F32),
        compiler_params=params(40),
        cost_estimate=cost(2 * steps * size * B * rows * TILE * 4, 4e6),
        name="scatter_rows",
    )(ids, counts, values, *extra)


def add_kernel(*refs):
    terms, out_ref = refs[:-2], refs[-1]
    total = terms[0][...].astype(F32)
    for term in terms[1:]:
        total = total + term[...].astype(F32)
    out_ref[...] = total.astype(BF16)


def add_terms(terms, after):
    vmem = pl.BlockSpec(memory_space=pltpu.VMEM)
    return pl.pallas_call(
        add_kernel,
        in_specs=[vmem] * len(terms) + [pl.BlockSpec(memory_space=pl.ANY)],
        out_specs=vmem,
        out_shape=shape(terms[0].shape, BF16),
        compiler_params=params(8),
        cost_estimate=cost(1e6, 1e6),
        name="add_terms",
    )(*terms, after)


def spread_kernel(terms_ref, after_ref, out_ref):
    del after_ref
    total = jnp.sum(terms_ref[...].astype(F32), axis=0).astype(BF16)
    out_ref[...] = jnp.broadcast_to(total[None], out_ref.shape)


def spread_terms(terms, after):
    vmem = pl.BlockSpec(memory_space=pltpu.VMEM)
    return pl.pallas_call(
        spread_kernel,
        in_specs=[vmem, pl.BlockSpec(memory_space=pl.ANY)],
        out_specs=vmem,
        out_shape=shape(terms.shape, BF16),
        compiler_params=params(8),
        cost_estimate=cost(1e6, 6e5),
        name="spread_terms",
    )(terms, after)


def place_kernel(terms_ref, *outs):
    rows, width = terms_ref.shape[1:]
    n = outs[0].shape[1] // width
    for at in range(terms_ref.shape[0]):
        group, q = at // n, at % n
        per = outs[0].shape[0] // rows
        out = outs[group // per]
        first = group % per * rows
        out[first : first + rows, q * width : (q + 1) * width] = terms_ref[at].astype(F32)


def place_terms(terms, width, n):
    return pl.pallas_call(
        place_kernel,
        out_shape=[shape((width, n * width), F32)] * 2,
        compiler_params=params(8),
        cost_estimate=cost(1e5, 8e5),
        name="place_terms",
    )(terms)


def per_device(
    features, stale_features, grad_output, w_neigh, w_self, adj_tiles, tile_cols, send_idx, counts
):
    dom_count = lax.axis_size("dom")
    n = lax.axis_size("rep")
    row_count, width = features.shape
    row_tiles = row_count // TILE
    swap = functools.partial(
        lax.all_to_all, axis_name="dom", split_axis=0, concat_axis=0, tiled=True
    )
    me = lax.axis_index("rep").astype(jnp.int32).reshape(1)

    ids = send_idx[0]
    pos = tile_cols[0].reshape(-1)
    adj = adj_tiles[0]

    packed = gather_rows(ids, counts, stale_features)
    halo = swap(packed)
    own, wn, ws, pieces = prep(me, features, grad_output, w_neigh, w_self, packed, n)
    both = relative(exchange(pieces))

    agg = relative(exchange(spmm(me, pos, adj, [own, halo], n)))
    grad_agg, act, grad_pre = dense(agg, both, wn, ws)
    grad_agg = exchange(grad_agg)

    local, away = spmm_back(me, pos, adj, grad_agg, row_tiles, dom_count * CHUNKS)
    returned = swap(away)
    pieces = exchange(late(act, grad_pre, ws, away, n))
    out, grad_input = finish(me, local, pieces)
    terms = exchange(wgrad(me, agg, both, grad_pre, away, dom_count))

    blocks = dom_count // 8
    half = (blocks + 1) // 2
    terms = swap(add_terms(terms, returned))
    grad_stale = scatter_rows(ids, counts, returned, row_count, 0, half, None)
    terms = swap(spread_terms(terms, grad_stale))
    if blocks > half:
        grad_stale = scatter_rows(
            ids, counts, returned, row_count, half, blocks - half, grad_stale
        )
    grad_neigh, grad_self = place_terms(terms, width, n)
    return (out, grad_input, grad_stale, grad_neigh, grad_self)


def solution(mesh):
    in_specs = (
        P("dom", "rep"),
        P("dom", "rep"),
        P("dom", "rep"),
        P(),
        P(),
        P("dom", None, None, None, None),
        P("dom", None, None),
        P("dom", None, None),
        P("dom", None),
    )
    out_specs = (P("dom", "rep"), P("dom", "rep"), P("dom", "rep"), P("rep", None), P("rep", None))
    return jax.shard_map(
        per_device, mesh=mesh, in_specs=in_specs, out_specs=out_specs, check_vma=False
    )
```

```python
import functools

import jax
import jax.numpy as jnp
from jax import lax
from jax.experimental import pallas as pl
from jax.experimental.pallas import tpu as pltpu
from jax.sharding import PartitionSpec as P

TILE = 128
B = 384
CHUNKS = B // TILE
LOW = 512
F32 = jnp.float32
BF16 = jnp.bfloat16
NT = (((1,), (1,)), ((), ()))
TN = (((0,), (0,)), ((), ()))


def params(mib):
    return pltpu.CompilerParams(vmem_limit_bytes=mib * 1024 * 1024)


def cost(flops, nbytes, trans=0):
    return pl.CostEstimate(flops=int(flops), bytes_accessed=int(nbytes), transcendentals=int(trans))


def shape(dims, dtype):
    return jax.ShapeDtypeStruct(dims, dtype)


def turned(block):
    return jnp.transpose(block.astype(F32))


def masked_ids(ids_ref, counts_ref, first, peers, skipped=0):
    base = (pl.program_id(0) + skipped) * ids_ref.shape[0]
    slot = lax.broadcasted_iota(jnp.int32, (1, ids_ref.shape[1]), 1)
    rows = [
        jnp.where(slot < counts_ref[0, base + p], ids_ref[p : p + 1, :], -1)
        for p in range(first, first + peers)
    ]
    return jnp.concatenate(rows, axis=1)


def low_onehot(ids):
    spot = lax.broadcasted_iota(jnp.int32, (LOW, ids.shape[1]), 0)
    return jnp.where(spot == (ids & (LOW - 1)), 1.0, 0.0).astype(BF16)


def in_group(ids, g):
    return (ids >= g * LOW) & (ids < (g + 1) * LOW)


def gather_kernel(ids_ref, counts_ref, table_ref, out_ref, flipped):
    groups = table_ref.shape[0] // LOW

    @pl.when(pl.program_id(0) == 0)
    def _():
        for g in range(groups):
            for k in range(LOW // TILE):
                block = table_ref[g * LOW + k * TILE : g * LOW + (k + 1) * TILE, :]
                flipped[g * TILE : (g + 1) * TILE, k * TILE : (k + 1) * TILE] = turned(block).astype(
                    BF16
                )

    for p in range(0, ids_ref.shape[0], 2):
        ids = masked_ids(ids_ref, counts_ref, p, 2)
        found = jnp.dot(flipped[...], low_onehot(ids), preferred_element_type=F32)
        total = jnp.zeros((TILE, ids.shape[1]), F32)
        for g in range(groups):
            total = jnp.where(in_group(ids, g), found[g * TILE : (g + 1) * TILE, :], total)
        total = total.astype(BF16)
        for k in range(2 * CHUNKS):
            out_ref[p * CHUNKS + k] = total[:, k * TILE : (k + 1) * TILE]


def gather_rows(ids, counts, table):
    peers = ids.shape[0]
    size = 8
    rows, cols = table.shape
    return pl.pallas_call(
        gather_kernel,
        grid=(peers // size,),
        in_specs=[
            pl.BlockSpec((size, B), lambda i: (i, 0)),
            pl.BlockSpec(memory_space=pltpu.SMEM),
            pl.BlockSpec((rows, cols), lambda i: (0, 0)),
        ],
        out_specs=pl.BlockSpec((size * CHUNKS, TILE, TILE), lambda i: (i, 0, 0)),
        out_shape=shape((peers * CHUNKS, TILE, TILE), BF16),
        scratch_shapes=[pltpu.VMEM((rows // LOW * TILE, LOW), BF16)],
        compiler_params=params(56),
        cost_estimate=cost(2 * ids.size * rows * cols, 4e6),
        name="gather_rows",
    )(ids, counts, table)


def exchange(pieces):
    n = len(pieces)
    return [pieces[0]] + [
        lax.ppermute(pieces[s], "rep", [(i, (i + s) % n) for i in range(n)]) for s in range(1, n)
    ]


def relative(received):
    n = len(received)
    return [received[(n - j) % n] for j in range(n)]


def prep_kernel(me_ref, feat_ref, up_ref, wn_ref, ws_ref, after_ref, own_ref, wn_out, ws_out, *pieces):
    del after_ref
    step = pl.program_id(0)
    n = len(pieces)
    for k in range(own_ref.shape[0]):
        own_ref[k] = turned(feat_ref[k * TILE : (k + 1) * TILE, :]).astype(BF16)
    for j, piece in enumerate(pieces):
        column = pl.multiple_of(lax.rem(me_ref[0] + j, n) * TILE, TILE)
        wn_out[:, j * TILE : (j + 1) * TILE] = wn_ref[:, pl.ds(column, TILE)]
        ws_out[:, j * TILE : (j + 1) * TILE] = ws_ref[:, pl.ds(column, TILE)]

        @pl.when(step == j)
        def _():
            piece[0] = feat_ref[...]
            piece[1] = up_ref[...]


def prep(me, features, upstream, wn, ws, after, n):
    rows, width = features.shape
    share = rows // n
    full = wn.shape[0]
    chunk = pl.BlockSpec((share, width), lambda i, me: (lax.rem(me[0] + i, n), 0))
    weight = pl.BlockSpec((width, full), lambda i, me: (lax.rem(me[0] + i, n), 0))
    placed = pl.BlockSpec((width, full), lambda i, me: (i, 0))
    own, wn, ws, *pieces = pl.pallas_call(
        prep_kernel,
        grid_spec=pltpu.PrefetchScalarGridSpec(
            num_scalar_prefetch=1,
            grid=(n,),
            in_specs=[chunk, chunk, weight, weight, pl.BlockSpec(memory_space=pl.ANY)],
            out_specs=[
                pl.BlockSpec(
                    (share // TILE, TILE, TILE), lambda i, me: (lax.rem(me[0] + i, n), 0, 0)
                ),
                placed,
                placed,
            ]
            + [pl.BlockSpec((2, share, width), lambda i, me: (0, 0, 0))] * n,
        ),
        out_shape=[
            pltpu.HBM((rows // TILE, TILE, TILE), BF16),
            pltpu.HBM((full, full), BF16),
            pltpu.HBM((full, full), BF16),
        ]
        + [shape((2, share, width), BF16)] * n,
        compiler_params=params(56),
        cost_estimate=cost(1e10, 6e6),
        name="prep",
    )(me, features, upstream, wn, ws, after)
    return own, wn, ws, pieces


BLOCKS = 3


def span(index, size):
    return pl.ds(pl.multiple_of(index * size, size), size)


def adj_copies(adj_ref, held, sems, inner, chunk_of):
    size = held.shape[0] // sems.shape[0]

    def copy(step):
        source = chunk_of(step // inner) * inner + lax.rem(step, inner)
        return pltpu.make_async_copy(
            adj_ref.at[span(source, size), :], held.at[span(step, size), :], sems.at[step]
        )

    return copy


def tile_pair(adj, at):
    return jnp.concatenate([adj[span(at, TILE), :], adj[span(at + 1, TILE), :]], axis=1)


def spmm_kernel(me_ref, pos_ref, *refs, n, per_row):
    adj_ref, parts, outs, (ext, sems, adj, adj_sems) = (
        refs[0],
        refs[1 : -n - 4],
        refs[-n - 4 : -4],
        refs[-4:],
    )
    chunk, part = pl.program_id(0), pl.program_id(1)
    inner = adj_sems.shape[0] // n
    step = chunk * inner + part
    copy_of = adj_copies(adj_ref, adj, adj_sems, inner, lambda c: lax.rem(me_ref[0] + c, n))

    @pl.when((chunk == 0) & (part == 0))
    def _():
        copies, start, at = [], 0, 0
        for source in parts:
            size = source.shape[0] // 4
            for k in range(4):
                copies.append(
                    pltpu.make_async_copy(
                        source.at[pl.ds(k * size, size), :], ext.at[pl.ds(start, size), :], sems.at[at]
                    )
                )
                start, at = start + size, at + 1
        for copy in copies:
            copy.start()
        for k in range(adj_sems.shape[0]):
            copy_of(k).start()
        for copy in copies:
            copy.wait()

    copy_of(step).wait()
    first = (lax.rem(me_ref[0] + chunk, n) * pl.num_programs(1) + part) * BLOCKS
    done = []
    for r in range(BLOCKS):
        base = (first + r) * per_row
        total = None
        for t in range(0, per_row, 2):
            left = tile_pair(adj, (step * BLOCKS + r) * per_row + t)
            right = jnp.concatenate(
                [ext[span(pos_ref[base + t], TILE), :], ext[span(pos_ref[base + t + 1], TILE), :]],
                axis=1,
            )
            term = lax.dot_general(left, right, NT, preferred_element_type=F32)
            total = term if total is None else total + term
        done.append(total.astype(BF16))
    done = jnp.concatenate(done, axis=0)
    size = BLOCKS * TILE
    place = pl.ds(pl.multiple_of(part * size, size), size)
    for j, out in enumerate(outs):

        @pl.when(chunk == j)
        def _():
            out[place, :] = done


def spmm(me, pos, adj, parts, n, row_tiles):
    per_row = pos.shape[0] // row_tiles
    inner = row_tiles // n // BLOCKS
    share = row_tiles // n * TILE
    col_rows = sum(p.shape[0] for p in parts)
    return pl.pallas_call(
        functools.partial(spmm_kernel, n=n, per_row=per_row),
        grid_spec=pltpu.PrefetchScalarGridSpec(
            num_scalar_prefetch=2,
            grid=(n, inner),
            in_specs=[pl.BlockSpec(memory_space=pl.ANY)] * (1 + len(parts)),
            out_specs=[pl.BlockSpec((share, TILE), lambda i, k, me, pos: (0, 0))] * n,
            scratch_shapes=[
                pltpu.VMEM((col_rows, TILE), BF16),
                pltpu.SemaphoreType.DMA((4 * len(parts),)),
                pltpu.VMEM(adj.shape, BF16),
                pltpu.SemaphoreType.DMA((n * inner,)),
            ],
        ),
        out_shape=[shape((share, TILE), BF16)] * n,
        compiler_params=params(56),
        cost_estimate=cost(2 * row_tiles * per_row * TILE**3 * 2, 2e7),
        name="spmm",
    )(me, pos, adj, *parts)


def joined(refs):
    return jnp.concatenate([ref[...] for ref in refs], axis=1)


def dense_kernel(*refs, n):
    agg, both, (wn_ref, ws_ref), rest = refs[:n], refs[n : 2 * n], refs[2 * n : 2 * n + 2], refs[2 * n + 2 :]
    ga, (act_ref, gp_ref) = rest[:n], rest[n:]
    wn = wn_ref[...]
    v = jnp.dot(joined(agg), wn, preferred_element_type=F32) + jnp.dot(
        joined([ref.at[0] for ref in both]), ws_ref[...], preferred_element_type=F32
    )
    root = 0.7978845608028654
    square = v * v
    t = jnp.tanh(root * v * (1.0 + 0.044715 * square))
    half = 0.5 * (1.0 + t)
    slope = half + 0.5 * v * (1.0 - t * t) * (root * (1.0 + 0.134145 * square))
    gp = (joined([ref.at[1] for ref in both]).astype(F32) * slope).astype(BF16)
    act_ref[...] = (v * half).astype(BF16)
    gp_ref[...] = gp
    back = lax.dot_general(wn, gp, NT, preferred_element_type=F32).astype(BF16)
    width = back.shape[0] // n
    for q in range(n):
        ga[q][...] = back[q * width : (q + 1) * width, :]


def dense(agg, both, wn, ws):
    n = len(agg)
    rows, width = agg[0].shape
    full = n * width
    size = 256
    weight = pl.BlockSpec((full, full), lambda i: (0, 0))
    whole = pl.BlockSpec((size, full), lambda i: (i, 0))
    results = pl.pallas_call(
        functools.partial(dense_kernel, n=n),
        grid=(rows // size,),
        in_specs=[pl.BlockSpec((size, width), lambda i: (i, 0))] * n
        + [pl.BlockSpec((2, size, width), lambda i: (0, i, 0))] * n
        + [weight, weight],
        out_specs=[pl.BlockSpec((width, size), lambda i: (0, i))] * n + [whole, whole],
        out_shape=[shape((width, rows), BF16)] * n + [pltpu.HBM((rows, full), BF16)] * 2,
        compiler_params=params(24),
        cost_estimate=cost(6 * rows * full * full, 7e6, rows * full),
        name="dense",
    )(*agg, *both, wn, ws)
    return results[:n], results[n], results[n + 1]


def wgrad_kernel(me_ref, *refs, n):
    agg, both, gp_ref, outs = refs[:n], refs[n : 2 * n], refs[2 * n], refs[-n:]
    gp = gp_ref[...]
    rows = outs[0].shape[1]
    width = agg[0].shape[1]
    for j in range(n):
        for kind, left in enumerate((agg[j][...], both[j][0])):
            term = lax.dot_general(left, gp, TN, preferred_element_type=F32).astype(BF16)
            for i in range(n):
                q = lax.rem(me_ref[0] + i, n)
                for k in range(width // rows):
                    at = (kind * (width // rows) + k) * n + q
                    outs[j][at] = term[k * rows : (k + 1) * rows, i * TILE : (i + 1) * TILE]


def wgrad(me, agg, both, gp, after, dom_count):
    n = len(agg)
    rows, width = agg[0].shape
    size = 2 * width * n // dom_count
    vmem = pl.BlockSpec(memory_space=pltpu.VMEM)
    return pl.pallas_call(
        functools.partial(wgrad_kernel, n=n),
        in_specs=[pl.BlockSpec(memory_space=pltpu.SMEM)]
        + [vmem] * (2 * n + 1)
        + [pl.BlockSpec(memory_space=pl.ANY)],
        out_specs=[vmem] * n,
        out_shape=[shape((dom_count, size, TILE), BF16)] * n,
        compiler_params=params(24),
        cost_estimate=cost(1e10, 4e6),
        name="wgrad",
    )(me, *agg, *both, gp, after)


PIECES = 6


def spmm_back_kernel(me_ref, pos_ref, *refs, n, per_row):
    adj_ref, ga = refs[0], refs[1 : 1 + n]
    local_ref, away_ref, total, left_ref, stage, sems, adj, adj_sems = refs[1 + n :]
    chunk, part = pl.program_id(0), pl.program_id(1)
    inner = adj_sems.shape[0] // n
    step = chunk * inner + part
    copy_of = adj_copies(adj_ref, adj, adj_sems, inner, lambda c: lax.rem(me_ref[0] + n - c, n))
    size = BLOCKS * TILE

    @pl.when((chunk == 0) & (part == 0))
    def _():
        for k in range(adj_sems.shape[0]):
            copy_of(k).start()
        total[...] = jnp.zeros_like(total)

    for s in range(n):

        @pl.when((chunk == s) & (part == 0))
        def _():
            for k in range(left_ref.shape[0]):
                left_ref[k] = ga[s][:, k * size : (k + 1) * size]

    copy_of(step).wait()
    first = (lax.rem(me_ref[0] + n - chunk, n) * pl.num_programs(1) + part) * BLOCKS
    for r in range(BLOCKS):
        base = (first + r) * per_row
        left = left_ref[part, :, r * TILE : (r + 1) * TILE]
        for t in range(0, per_row, 2):
            right = tile_pair(adj, (step * BLOCKS + r) * per_row + t)
            both = jnp.dot(left, right, preferred_element_type=F32)
            total[pos_ref[base + t]] += both[:, :TILE]
            total[pos_ref[base + t + 1]] += both[:, TILE:]

    @pl.when((chunk == n - 1) & (part == pl.num_programs(1) - 1))
    def _():
        own = local_ref.shape[0]
        step = away_ref.shape[0] // PIECES
        copies = [pltpu.make_async_copy(total.at[pl.ds(0, own)], local_ref, sems.at[PIECES])]
        copies[0].start()
        for k in range(PIECES):
            stage[k * step : (k + 1) * step] = total[own + k * step : own + (k + 1) * step].astype(BF16)
            copies.append(
                pltpu.make_async_copy(
                    stage.at[pl.ds(k * step, step)], away_ref.at[pl.ds(k * step, step)], sems.at[k]
                )
            )
            copies[-1].start()
        for copy in copies:
            copy.wait()


def spmm_back(me, pos, adj, ga, own, away):
    n = len(ga)
    rows = ga[0].shape[1]
    row_tiles = n * rows // TILE
    per_row = pos.shape[0] // row_tiles
    inner = row_tiles // n // BLOCKS
    return pl.pallas_call(
        functools.partial(spmm_back_kernel, n=n, per_row=per_row),
        grid_spec=pltpu.PrefetchScalarGridSpec(
            num_scalar_prefetch=2,
            grid=(n, inner),
            in_specs=[pl.BlockSpec(memory_space=pl.ANY)]
            + [pl.BlockSpec((TILE, rows), lambda i, k, me, pos: (0, 0))] * n,
            out_specs=[pl.BlockSpec(memory_space=pl.ANY)] * 2,
            scratch_shapes=[
                pltpu.VMEM((own + away, TILE, TILE), F32),
                pltpu.VMEM((inner, TILE, BLOCKS * TILE), BF16),
                pltpu.VMEM((away, TILE, TILE), BF16),
                pltpu.SemaphoreType.DMA((PIECES + 1,)),
                pltpu.VMEM(adj.shape, BF16),
                pltpu.SemaphoreType.DMA((n * inner,)),
            ],
        ),
        out_shape=[pltpu.HBM((own, TILE, TILE), F32), pltpu.HBM((away, TILE, TILE), BF16)],
        compiler_params=params(56),
        cost_estimate=cost(2 * row_tiles * per_row * TILE**3 * 2, 2.2e7),
        name="spmm_back",
    )(me, pos, adj, *ga)


def late_kernel(act_ref, gp_ref, ws_ref, after_ref, *pieces):
    del after_ref
    direct = lax.dot_general(gp_ref[...], ws_ref[...], NT, preferred_element_type=F32).astype(BF16)
    for j, piece in enumerate(pieces):
        piece[0] = act_ref[:, j * TILE : (j + 1) * TILE]
        piece[1] = direct[:, j * TILE : (j + 1) * TILE]


def late(act, gp, ws, after, n):
    rows, full = act.shape
    size = 256
    share = pl.BlockSpec((size, full), lambda i: (i, 0))
    return pl.pallas_call(
        late_kernel,
        grid=(rows // size,),
        in_specs=[
            share,
            share,
            pl.BlockSpec((full, full), lambda i: (0, 0)),
            pl.BlockSpec(memory_space=pl.ANY),
        ],
        out_specs=[pl.BlockSpec((2, size, TILE), lambda i: (0, i, 0))] * n,
        out_shape=[shape((2, rows, TILE), BF16)] * n,
        compiler_params=params(24),
        cost_estimate=cost(1e10, 6e6),
        name="late",
    )(act, gp, ws, after)


def finish_kernel(me_ref, ext_ref, *refs):
    pieces, (out_ref, grad_ref) = refs[:-2], refs[-2:]
    for s, piece in enumerate(pieces):

        @pl.when(pl.program_id(0) == s)
        def _():
            out_ref[...] = piece[0]
            for k in range(ext_ref.shape[0]):
                rows = slice(k * TILE, (k + 1) * TILE)
                total = piece[1, rows, :].astype(F32) + jnp.transpose(ext_ref[k])
                grad_ref[rows, :] = total.astype(BF16)


def finish(me, ext, pieces):
    n = len(pieces)
    share = pieces[0].shape[1]
    placed = pl.BlockSpec((share, TILE), lambda i, me: (lax.rem(me[0] + n - i, n), 0))
    return pl.pallas_call(
        finish_kernel,
        grid_spec=pltpu.PrefetchScalarGridSpec(
            num_scalar_prefetch=1,
            grid=(n,),
            in_specs=[
                pl.BlockSpec(
                    (share // TILE, TILE, TILE), lambda i, me: (lax.rem(me[0] + n - i, n), 0, 0)
                )
            ]
            + [pl.BlockSpec((2, share, TILE), lambda i, me: (0, 0, 0))] * n,
            out_specs=[placed, placed],
        ),
        out_shape=[shape((n * share, TILE), BF16)] * 2,
        compiler_params=params(24),
        cost_estimate=cost(1e6, 7e6),
        name="finish",
    )(me, ext, *pieces)


def scatter_kernel(ids_ref, counts_ref, val_ref, *refs, first):
    before, out_ref = refs[:-1], refs[-1]
    groups = out_ref.shape[0] // LOW

    @pl.when(pl.program_id(0) == 0)
    def _():
        out_ref[...] = before[0][...] if before else jnp.zeros_like(out_ref)

    for p in range(0, ids_ref.shape[0], 2):
        ids = masked_ids(ids_ref, counts_ref, p, 2, first)
        onehot = low_onehot(ids)
        values = jnp.concatenate([val_ref[p * CHUNKS + k] for k in range(2 * CHUNKS)], axis=1)
        zero = jnp.zeros_like(values)
        for g in range(0, groups, 2):
            pair = [jnp.where(in_group(ids, k), values, zero) for k in (g, g + 1)]
            both = lax.dot_general(
                onehot, jnp.concatenate(pair, axis=0), NT, preferred_element_type=F32
            )
            out_ref[g * LOW : (g + 1) * LOW, :] += both[:, :TILE]
            out_ref[(g + 1) * LOW : (g + 2) * LOW, :] += both[:, TILE:]


def scatter_rows(ids, counts, values, rows, first, steps, before):
    size = 8
    whole = pl.BlockSpec((rows, TILE), lambda i: (0, 0))
    extra = [] if before is None else [before]
    return pl.pallas_call(
        functools.partial(scatter_kernel, first=first),
        grid=(steps,),
        in_specs=[
            pl.BlockSpec((size, B), lambda i: (i + first, 0)),
            pl.BlockSpec(memory_space=pltpu.SMEM),
            pl.BlockSpec((size * CHUNKS, TILE, TILE), lambda i: (i + first, 0, 0)),
        ]
        + [whole] * len(extra),
        out_specs=whole,
        out_shape=shape((rows, TILE), F32),
        compiler_params=params(56),
        cost_estimate=cost(2 * steps * size * B * rows * TILE * 4, 4e6),
        name="scatter_rows",
    )(ids, counts, values, *extra)


def add_kernel(*refs):
    terms, out_ref = refs[:-1], refs[-1]
    total = terms[0][...].astype(F32)
    for term in terms[1:]:
        total = total + term[...].astype(F32)
    out_ref[...] = total.astype(BF16)


def add_terms(terms):
    vmem = pl.BlockSpec(memory_space=pltpu.VMEM)
    return pl.pallas_call(
        add_kernel,
        in_specs=[vmem] * len(terms),
        out_specs=vmem,
        out_shape=shape(terms[0].shape, BF16),
        compiler_params=params(8),
        cost_estimate=cost(1e6, 1e6),
        name="add_terms",
    )(*terms)


def tie_kernel(value_ref, after_ref, out_ref):
    del value_ref, after_ref, out_ref


def tie(value, after):
    anywhere = pl.BlockSpec(memory_space=pl.ANY)
    return pl.pallas_call(
        tie_kernel,
        in_specs=[anywhere, anywhere],
        out_specs=anywhere,
        out_shape=shape(value.shape, value.dtype),
        input_output_aliases={0: 0},
        compiler_params=params(56),
        name="tie",
    )(value, after)


def spread_kernel(terms_ref, after_ref, out_ref):
    del after_ref
    total = jnp.sum(terms_ref[...].astype(F32), axis=0).astype(BF16)
    out_ref[...] = jnp.broadcast_to(total[None], out_ref.shape)


def spread_terms(terms, after):
    vmem = pl.BlockSpec(memory_space=pltpu.VMEM)
    return pl.pallas_call(
        spread_kernel,
        in_specs=[vmem, pl.BlockSpec(memory_space=pl.ANY)],
        out_specs=vmem,
        out_shape=shape(terms.shape, BF16),
        compiler_params=params(8),
        cost_estimate=cost(1e6, 6e5),
        name="spread_terms",
    )(terms, after)


def place_kernel(terms_ref, *outs):
    rows, width = terms_ref.shape[1:]
    n = outs[0].shape[1] // width
    for at in range(terms_ref.shape[0]):
        group, q = at // n, at % n
        per = outs[0].shape[0] // rows
        out = outs[group // per]
        first = group % per * rows
        out[first : first + rows, q * width : (q + 1) * width] = terms_ref[at].astype(F32)


def place_terms(terms, width, n):
    return pl.pallas_call(
        place_kernel,
        out_shape=[shape((width, n * width), F32)] * 2,
        compiler_params=params(8),
        cost_estimate=cost(1e5, 8e5),
        name="place_terms",
    )(terms)


def per_device(
    features, stale_features, grad_output, w_neigh, w_self, adj_tiles, tile_cols, send_idx, counts
):
    dom_count = lax.axis_size("dom")
    n = lax.axis_size("rep")
    row_count, width = features.shape
    row_tiles = row_count // TILE
    swap = functools.partial(
        lax.all_to_all, axis_name="dom", split_axis=0, concat_axis=0, tiled=True
    )
    me = lax.axis_index("rep").astype(jnp.int32).reshape(1)

    ids = send_idx[0]
    pos = tile_cols[0].reshape(-1)
    adj = adj_tiles.reshape(-1, TILE)

    packed = gather_rows(ids, counts, stale_features)
    halo = swap(packed)
    own, wn, ws, pieces = prep(me, features, grad_output, w_neigh, w_self, packed, n)
    both = relative(exchange(pieces))

    agg = relative(exchange(spmm(me, pos, adj, [own.reshape(-1, TILE), halo.reshape(-1, TILE)], n, row_tiles)))
    grad_agg, act, grad_pre = dense(agg, both, wn, ws)
    grad_agg = exchange(grad_agg)

    local, away = spmm_back(me, pos, adj, grad_agg, row_tiles, dom_count * CHUNKS)
    returned = swap(away)
    pieces = exchange(late(act, grad_pre, ws, away, n))
    out, grad_input = finish(me, local, pieces)
    terms = exchange(wgrad(me, agg, both, grad_pre, away, dom_count))

    blocks = dom_count // 8
    half = (blocks + 1) // 2
    terms = swap(tie(add_terms(terms), returned))
    grad_stale = scatter_rows(ids, counts, returned, row_count, 0, half, None)
    terms = swap(spread_terms(terms, grad_stale))
    if blocks > half:
        grad_stale = scatter_rows(
            ids, counts, returned, row_count, half, blocks - half, grad_stale
        )
    grad_neigh, grad_self = place_terms(terms, width, n)
    return (out, grad_input, grad_stale, grad_neigh, grad_self)


def solution(mesh):
    in_specs = (
        P("dom", "rep"),
        P("dom", "rep"),
        P("dom", "rep"),
        P(),
        P(),
        P("dom", None, None, None, None),
        P("dom", None, None),
        P("dom", None, None),
        P("dom", None),
    )
    out_specs = (P("dom", "rep"), P("dom", "rep"), P("dom", "rep"), P("rep", None), P("rep", None))
    return jax.shard_map(
        per_device, mesh=mesh, in_specs=in_specs, out_specs=out_specs, check_vma=False
    )
```

```python
import functools

import jax
import jax.numpy as jnp
from jax import lax
from jax.experimental import pallas as pl
from jax.experimental.pallas import tpu as pltpu
from jax.sharding import PartitionSpec as P

TILE = 128
B = 384
CHUNKS = B // TILE
LOW = 512
F32 = jnp.float32
BF16 = jnp.bfloat16
NT = (((1,), (1,)), ((), ()))
TN = (((0,), (0,)), ((), ()))


def params(mib):
    return pltpu.CompilerParams(vmem_limit_bytes=mib * 1024 * 1024)


def cost(flops, nbytes, trans=0):
    return pl.CostEstimate(flops=int(flops), bytes_accessed=int(nbytes), transcendentals=int(trans))


def shape(dims, dtype):
    return jax.ShapeDtypeStruct(dims, dtype)


def turned(block):
    return jnp.transpose(block.astype(F32))


def masked_ids(ids_ref, counts_ref, first, peers, skipped=0):
    base = (pl.program_id(0) + skipped) * ids_ref.shape[0]
    slot = lax.broadcasted_iota(jnp.int32, (1, ids_ref.shape[1]), 1)
    rows = [
        jnp.where(slot < counts_ref[0, base + p], ids_ref[p : p + 1, :], -1)
        for p in range(first, first + peers)
    ]
    return jnp.concatenate(rows, axis=1)


def low_onehot(ids):
    spot = lax.broadcasted_iota(jnp.int32, (LOW, ids.shape[1]), 0)
    return jnp.where(spot == (ids & (LOW - 1)), 1.0, 0.0).astype(BF16)


def in_group(ids, g):
    return (ids >= g * LOW) & (ids < (g + 1) * LOW)


def gather_kernel(ids_ref, counts_ref, table_ref, out_ref, flipped):
    groups = table_ref.shape[0] // LOW

    @pl.when(pl.program_id(0) == 0)
    def _():
        for g in range(groups):
            for k in range(LOW // TILE):
                block = table_ref[g * LOW + k * TILE : g * LOW + (k + 1) * TILE, :]
                flipped[g * TILE : (g + 1) * TILE, k * TILE : (k + 1) * TILE] = turned(block).astype(
                    BF16
                )

    for p in range(0, ids_ref.shape[0], 2):
        ids = masked_ids(ids_ref, counts_ref, p, 2)
        found = jnp.dot(flipped[...], low_onehot(ids), preferred_element_type=F32)
        total = jnp.zeros((TILE, ids.shape[1]), F32)
        for g in range(groups):
            total = jnp.where(in_group(ids, g), found[g * TILE : (g + 1) * TILE, :], total)
        total = total.astype(BF16)
        for k in range(2 * CHUNKS):
            out_ref[p * CHUNKS + k] = total[:, k * TILE : (k + 1) * TILE]


def gather_rows(ids, counts, table):
    peers = ids.shape[0]
    size = 8
    rows, cols = table.shape
    return pl.pallas_call(
        gather_kernel,
        grid=(peers // size,),
        in_specs=[
            pl.BlockSpec((size, B), lambda i: (i, 0)),
            pl.BlockSpec(memory_space=pltpu.SMEM),
            pl.BlockSpec((rows, cols), lambda i: (0, 0)),
        ],
        out_specs=pl.BlockSpec((size * CHUNKS, TILE, TILE), lambda i: (i, 0, 0)),
        out_shape=shape((peers * CHUNKS, TILE, TILE), BF16),
        scratch_shapes=[pltpu.VMEM((rows // LOW * TILE, LOW), BF16)],
        compiler_params=params(56),
        cost_estimate=cost(2 * ids.size * rows * cols, 4e6),
        name="gather_rows",
    )(ids, counts, table)


def exchange(pieces):
    n = len(pieces)
    return [pieces[0]] + [
        lax.ppermute(pieces[s], "rep", [(i, (i + s) % n) for i in range(n)]) for s in range(1, n)
    ]


def relative(received):
    n = len(received)
    return [received[(n - j) % n] for j in range(n)]


def prep_kernel(me_ref, feat_ref, up_ref, wn_ref, ws_ref, after_ref, own_ref, wn_out, ws_out, *pieces):
    del after_ref
    step = pl.program_id(0)
    n = len(pieces)
    for k in range(own_ref.shape[0]):
        own_ref[k] = turned(feat_ref[k * TILE : (k + 1) * TILE, :]).astype(BF16)
    for j, piece in enumerate(pieces):
        column = pl.multiple_of(lax.rem(me_ref[0] + j, n) * TILE, TILE)
        wn_out[:, j * TILE : (j + 1) * TILE] = wn_ref[:, pl.ds(column, TILE)]
        ws_out[:, j * TILE : (j + 1) * TILE] = ws_ref[:, pl.ds(column, TILE)]

        @pl.when(step == j)
        def _():
            piece[0] = feat_ref[...]
            piece[1] = up_ref[...]


def prep(me, features, upstream, wn, ws, after, n):
    rows, width = features.shape
    share = rows // n
    full = wn.shape[0]
    chunk = pl.BlockSpec((share, width), lambda i, me: (lax.rem(me[0] + i, n), 0))
    weight = pl.BlockSpec((width, full), lambda i, me: (lax.rem(me[0] + i, n), 0))
    placed = pl.BlockSpec((width, full), lambda i, me: (i, 0))
    own, wn, ws, *pieces = pl.pallas_call(
        prep_kernel,
        grid_spec=pltpu.PrefetchScalarGridSpec(
            num_scalar_prefetch=1,
            grid=(n,),
            in_specs=[chunk, chunk, weight, weight, pl.BlockSpec(memory_space=pl.ANY)],
            out_specs=[
                pl.BlockSpec(
                    (share // TILE, TILE, TILE), lambda i, me: (lax.rem(me[0] + i, n), 0, 0)
                ),
                placed,
                placed,
            ]
            + [pl.BlockSpec((2, share, width), lambda i, me: (0, 0, 0))] * n,
        ),
        out_shape=[
            pltpu.HBM((rows // TILE, TILE, TILE), BF16),
            pltpu.HBM((full, full), BF16),
            pltpu.HBM((full, full), BF16),
        ]
        + [shape((2, share, width), BF16)] * n,
        compiler_params=params(56),
        cost_estimate=cost(1e10, 6e6),
        name="prep",
    )(me, features, upstream, wn, ws, after)
    return own, wn, ws, pieces


BLOCKS = 3


SLOTS = 3 * BLOCKS


def adj_stream(adj_ref, held, sems, chunk, part, n, inner, chunk_of):
    step = chunk * inner + part

    def copy(at, r):
        source = (chunk_of(at // inner) * inner + lax.rem(at, inner)) * BLOCKS + r
        slot = lax.rem(at, 3) * BLOCKS + r
        return pltpu.make_async_copy(adj_ref.at[source], held.at[slot], sems.at[slot])

    def start(at):
        for r in range(BLOCKS):
            copy(at, r).start()

    def wait(r):
        copy(step, r).wait()

    def ahead():
        @pl.when(step + 2 < n * inner)
        def _():
            start(step + 2)

    return lax.rem(step, 3) * BLOCKS, start, wait, ahead


def spmm_kernel(me_ref, pos_ref, *refs, n):
    adj_ref, parts, outs, (ext, sems, adj, adj_sems) = (
        refs[0],
        refs[1 : -n - 4],
        refs[-n - 4 : -4],
        refs[-4:],
    )
    chunk, part = pl.program_id(0), pl.program_id(1)
    inner = pl.num_programs(1)
    per_row = adj.shape[1]
    slot, start_adj, wait_adj, ahead = adj_stream(
        adj_ref, adj, adj_sems, chunk, part, n, inner, lambda c: lax.rem(me_ref[0] + c, n)
    )

    @pl.when((chunk == 0) & (part == 0))
    def _():
        copies, start, at = [], 0, 0
        for source in parts:
            size = source.shape[0] // 4
            for k in range(4):
                copies.append(
                    pltpu.make_async_copy(
                        source.at[pl.ds(k * size, size)], ext.at[pl.ds(start, size)], sems.at[at]
                    )
                )
                start, at = start + size, at + 1
        for copy in copies:
            copy.start()
        start_adj(0)
        for copy in copies:
            copy.wait()
        start_adj(1)

    ahead()
    first = (lax.rem(me_ref[0] + chunk, n) * pl.num_programs(1) + part) * BLOCKS
    done = []
    for r in range(BLOCKS):
        base = (first + r) * per_row
        wait_adj(r)
        total = None
        for t in range(0, per_row, 2):
            left = jnp.concatenate([adj[slot + r, t], adj[slot + r, t + 1]], axis=1)
            right = jnp.concatenate([ext[pos_ref[base + t]], ext[pos_ref[base + t + 1]]], axis=1)
            term = lax.dot_general(left, right, NT, preferred_element_type=F32)
            total = term if total is None else total + term
        done.append(total.astype(BF16))
    done = jnp.concatenate(done, axis=0)
    size = BLOCKS * TILE
    place = pl.ds(pl.multiple_of(part * size, size), size)
    for j, out in enumerate(outs):

        @pl.when(chunk == j)
        def _():
            out[place, :] = done


def spmm(me, pos, adj, parts, n):
    row_tiles, per_row = adj.shape[:2]
    inner = row_tiles // n // BLOCKS
    share = row_tiles // n * TILE
    col_tiles = sum(p.shape[0] for p in parts)
    return pl.pallas_call(
        functools.partial(spmm_kernel, n=n),
        grid_spec=pltpu.PrefetchScalarGridSpec(
            num_scalar_prefetch=2,
            grid=(n, inner),
            in_specs=[pl.BlockSpec(memory_space=pl.ANY)] * (1 + len(parts)),
            out_specs=[pl.BlockSpec((share, TILE), lambda i, k, me, pos: (0, 0))] * n,
            scratch_shapes=[
                pltpu.VMEM((col_tiles, TILE, TILE), BF16),
                pltpu.SemaphoreType.DMA((4 * len(parts),)),
                pltpu.VMEM((SLOTS, *adj.shape[1:]), BF16),
                pltpu.SemaphoreType.DMA((SLOTS,)),
            ],
        ),
        out_shape=[shape((share, TILE), BF16)] * n,
        compiler_params=params(52),
        cost_estimate=cost(2 * row_tiles * per_row * TILE**3 * 2, 2e7),
        name="spmm",
    )(me, pos, adj, *parts)


def joined(refs):
    return jnp.concatenate([ref[...] for ref in refs], axis=1)


def dense_kernel(*refs, n):
    agg, both, (wn_ref, ws_ref), rest = refs[:n], refs[n : 2 * n], refs[2 * n : 2 * n + 2], refs[2 * n + 2 :]
    ga, (act_ref, gp_ref) = rest[:n], rest[n:]
    wn = wn_ref[...]
    v = jnp.dot(joined(agg), wn, preferred_element_type=F32) + jnp.dot(
        joined([ref.at[0] for ref in both]), ws_ref[...], preferred_element_type=F32
    )
    root = 0.7978845608028654
    square = v * v
    t = jnp.tanh(root * v * (1.0 + 0.044715 * square))
    half = 0.5 * (1.0 + t)
    slope = half + 0.5 * v * (1.0 - t * t) * (root * (1.0 + 0.134145 * square))
    gp = (joined([ref.at[1] for ref in both]).astype(F32) * slope).astype(BF16)
    act_ref[...] = (v * half).astype(BF16)
    gp_ref[...] = gp
    back = lax.dot_general(wn, gp, NT, preferred_element_type=F32).astype(BF16)
    width = back.shape[0] // n
    for q in range(n):
        ga[q][...] = back[q * width : (q + 1) * width, :]


def dense(agg, both, wn, ws):
    n = len(agg)
    rows, width = agg[0].shape
    full = n * width
    size = 256
    weight = pl.BlockSpec((full, full), lambda i: (0, 0))
    whole = pl.BlockSpec((size, full), lambda i: (i, 0))
    results = pl.pallas_call(
        functools.partial(dense_kernel, n=n),
        grid=(rows // size,),
        in_specs=[pl.BlockSpec((size, width), lambda i: (i, 0))] * n
        + [pl.BlockSpec((2, size, width), lambda i: (0, i, 0))] * n
        + [weight, weight],
        out_specs=[pl.BlockSpec((width, size), lambda i: (0, i))] * n + [whole, whole],
        out_shape=[shape((width, rows), BF16)] * n + [pltpu.HBM((rows, full), BF16)] * 2,
        compiler_params=params(24),
        cost_estimate=cost(6 * rows * full * full, 7e6, rows * full),
        name="dense",
    )(*agg, *both, wn, ws)
    return results[:n], results[n], results[n + 1]


def wgrad_kernel(me_ref, *refs, n):
    agg, both, gp_ref, outs = refs[:n], refs[n : 2 * n], refs[2 * n], refs[-n:]
    gp = gp_ref[...]
    rows = outs[0].shape[1]
    width = agg[0].shape[1]
    for j in range(n):
        for kind, left in enumerate((agg[j][...], both[j][0])):
            term = lax.dot_general(left, gp, TN, preferred_element_type=F32).astype(BF16)
            for i in range(n):
                q = lax.rem(me_ref[0] + i, n)
                for k in range(width // rows):
                    at = (kind * (width // rows) + k) * n + q
                    outs[j][at] = term[k * rows : (k + 1) * rows, i * TILE : (i + 1) * TILE]


def wgrad(me, agg, both, gp, after, dom_count):
    n = len(agg)
    rows, width = agg[0].shape
    size = 2 * width * n // dom_count
    vmem = pl.BlockSpec(memory_space=pltpu.VMEM)
    return pl.pallas_call(
        functools.partial(wgrad_kernel, n=n),
        in_specs=[pl.BlockSpec(memory_space=pltpu.SMEM)]
        + [vmem] * (2 * n + 1)
        + [pl.BlockSpec(memory_space=pl.ANY)],
        out_specs=[vmem] * n,
        out_shape=[shape((dom_count, size, TILE), BF16)] * n,
        compiler_params=params(24),
        cost_estimate=cost(1e10, 4e6),
        name="wgrad",
    )(me, *agg, *both, gp, after)


PIECES = 6


def spmm_back_kernel(me_ref, pos_ref, *refs, n):
    adj_ref, ga = refs[0], refs[1 : 1 + n]
    local_ref, away_ref, total, left_ref, stage, sems, adj, adj_sems = refs[1 + n :]
    chunk, part = pl.program_id(0), pl.program_id(1)
    inner = pl.num_programs(1)
    per_row = adj.shape[1]
    slot, start_adj, wait_adj, ahead = adj_stream(
        adj_ref, adj, adj_sems, chunk, part, n, inner, lambda c: lax.rem(me_ref[0] + n - c, n)
    )
    size = BLOCKS * TILE

    @pl.when((chunk == 0) & (part == 0))
    def _():
        start_adj(0)
        start_adj(1)
        total[...] = jnp.zeros_like(total)

    for s in range(n):

        @pl.when((chunk == s) & (part == 0))
        def _():
            for k in range(left_ref.shape[0]):
                left_ref[k] = ga[s][:, k * size : (k + 1) * size]

    ahead()
    first = (lax.rem(me_ref[0] + n - chunk, n) * pl.num_programs(1) + part) * BLOCKS
    for r in range(BLOCKS):
        base = (first + r) * per_row
        wait_adj(r)
        left = left_ref[part, :, r * TILE : (r + 1) * TILE]
        for t in range(0, per_row, 2):
            right = jnp.concatenate([adj[slot + r, t], adj[slot + r, t + 1]], axis=1)
            both = jnp.dot(left, right, preferred_element_type=F32)
            total[pos_ref[base + t]] += both[:, :TILE]
            total[pos_ref[base + t + 1]] += both[:, TILE:]

    @pl.when((chunk == n - 1) & (part == pl.num_programs(1) - 1))
    def _():
        own = local_ref.shape[0]
        step = away_ref.shape[0] // PIECES
        copies = [pltpu.make_async_copy(total.at[pl.ds(0, own)], local_ref, sems.at[PIECES])]
        copies[0].start()
        for k in range(PIECES):
            stage[k * step : (k + 1) * step] = total[own + k * step : own + (k + 1) * step].astype(BF16)
            copies.append(
                pltpu.make_async_copy(
                    stage.at[pl.ds(k * step, step)], away_ref.at[pl.ds(k * step, step)], sems.at[k]
                )
            )
            copies[-1].start()
        for copy in copies:
            copy.wait()


def spmm_back(me, pos, adj, ga, own, away):
    n = len(ga)
    row_tiles, per_row = adj.shape[:2]
    rows = ga[0].shape[1]
    inner = row_tiles // n // BLOCKS
    return pl.pallas_call(
        functools.partial(spmm_back_kernel, n=n),
        grid_spec=pltpu.PrefetchScalarGridSpec(
            num_scalar_prefetch=2,
            grid=(n, inner),
            in_specs=[pl.BlockSpec(memory_space=pl.ANY)]
            + [pl.BlockSpec((TILE, rows), lambda i, k, me, pos: (0, 0))] * n,
            out_specs=[pl.BlockSpec(memory_space=pl.ANY)] * 2,
            scratch_shapes=[
                pltpu.VMEM((own + away, TILE, TILE), F32),
                pltpu.VMEM((inner, TILE, BLOCKS * TILE), BF16),
                pltpu.VMEM((away, TILE, TILE), BF16),
                pltpu.SemaphoreType.DMA((PIECES + 1,)),
                pltpu.VMEM((SLOTS, *adj.shape[1:]), BF16),
                pltpu.SemaphoreType.DMA((SLOTS,)),
            ],
        ),
        out_shape=[pltpu.HBM((own, TILE, TILE), F32), pltpu.HBM((away, TILE, TILE), BF16)],
        compiler_params=params(52),
        cost_estimate=cost(2 * row_tiles * per_row * TILE**3 * 2, 2.2e7),
        name="spmm_back",
    )(me, pos, adj, *ga)


def late_kernel(act_ref, gp_ref, ws_ref, after_ref, *pieces):
    del after_ref
    direct = lax.dot_general(gp_ref[...], ws_ref[...], NT, preferred_element_type=F32).astype(BF16)
    for j, piece in enumerate(pieces):
        piece[0] = act_ref[:, j * TILE : (j + 1) * TILE]
        piece[1] = direct[:, j * TILE : (j + 1) * TILE]


def late(act, gp, ws, after, n):
    rows, full = act.shape
    size = 256
    share = pl.BlockSpec((size, full), lambda i: (i, 0))
    return pl.pallas_call(
        late_kernel,
        grid=(rows // size,),
        in_specs=[
            share,
            share,
            pl.BlockSpec((full, full), lambda i: (0, 0)),
            pl.BlockSpec(memory_space=pl.ANY),
        ],
        out_specs=[pl.BlockSpec((2, size, TILE), lambda i: (0, i, 0))] * n,
        out_shape=[shape((2, rows, TILE), BF16)] * n,
        compiler_params=params(24),
        cost_estimate=cost(1e10, 6e6),
        name="late",
    )(act, gp, ws, after)


def finish_kernel(me_ref, ext_ref, *refs):
    pieces, (out_ref, grad_ref) = refs[:-2], refs[-2:]
    for s, piece in enumerate(pieces):

        @pl.when(pl.program_id(0) == s)
        def _():
            out_ref[...] = piece[0]
            for k in range(ext_ref.shape[0]):
                rows = slice(k * TILE, (k + 1) * TILE)
                total = piece[1, rows, :].astype(F32) + jnp.transpose(ext_ref[k])
                grad_ref[rows, :] = total.astype(BF16)


def finish(me, ext, pieces):
    n = len(pieces)
    share = pieces[0].shape[1]
    placed = pl.BlockSpec((share, TILE), lambda i, me: (lax.rem(me[0] + n - i, n), 0))
    return pl.pallas_call(
        finish_kernel,
        grid_spec=pltpu.PrefetchScalarGridSpec(
            num_scalar_prefetch=1,
            grid=(n,),
            in_specs=[
                pl.BlockSpec(
                    (share // TILE, TILE, TILE), lambda i, me: (lax.rem(me[0] + n - i, n), 0, 0)
                )
            ]
            + [pl.BlockSpec((2, share, TILE), lambda i, me: (0, 0, 0))] * n,
            out_specs=[placed, placed],
        ),
        out_shape=[shape((n * share, TILE), BF16)] * 2,
        compiler_params=params(24),
        cost_estimate=cost(1e6, 7e6),
        name="finish",
    )(me, ext, *pieces)


def scatter_kernel(ids_ref, counts_ref, val_ref, *refs, first):
    before, (out_ref, mark_ref) = refs[:-2], refs[-2:]
    groups = out_ref.shape[0] // LOW

    @pl.when(pl.program_id(0) == 0)
    def _():
        out_ref[...] = before[0][...] if before else jnp.zeros_like(out_ref)
        mark_ref[...] = jnp.zeros_like(mark_ref)

    for p in range(0, ids_ref.shape[0], 2):
        ids = masked_ids(ids_ref, counts_ref, p, 2, first)
        onehot = low_onehot(ids)
        values = jnp.concatenate([val_ref[p * CHUNKS + k] for k in range(2 * CHUNKS)], axis=1)
        zero = jnp.zeros_like(values)
        for g in range(0, groups, 2):
            pair = [jnp.where(in_group(ids, k), values, zero) for k in (g, g + 1)]
            both = lax.dot_general(
                onehot, jnp.concatenate(pair, axis=0), NT, preferred_element_type=F32
            )
            out_ref[g * LOW : (g + 1) * LOW, :] += both[:, :TILE]
            out_ref[(g + 1) * LOW : (g + 2) * LOW, :] += both[:, TILE:]


def scatter_rows(ids, counts, values, rows, first, steps, before):
    size = 8
    whole = pl.BlockSpec((rows, TILE), lambda i: (0, 0))
    extra = [] if before is None else [before]
    return pl.pallas_call(
        functools.partial(scatter_kernel, first=first),
        grid=(steps,),
        in_specs=[
            pl.BlockSpec((size, B), lambda i: (i + first, 0)),
            pl.BlockSpec(memory_space=pltpu.SMEM),
            pl.BlockSpec((size * CHUNKS, TILE, TILE), lambda i: (i + first, 0, 0)),
        ]
        + [whole] * len(extra),
        out_specs=[whole, pl.BlockSpec((8, TILE), lambda i: (0, 0))],
        out_shape=[shape((rows, TILE), F32), shape((8, TILE), F32)],
        compiler_params=params(24),
        cost_estimate=cost(2 * steps * size * B * rows * TILE * 4, 4e6),
        name="scatter_rows",
    )(ids, counts, values, *extra)


def add_kernel(*refs):
    terms, out_ref = refs[:-1], refs[-1]
    total = terms[0][...].astype(F32)
    for term in terms[1:]:
        total = total + term[...].astype(F32)
    out_ref[...] = total.astype(BF16)


def add_terms(terms):
    vmem = pl.BlockSpec(memory_space=pltpu.VMEM)
    return pl.pallas_call(
        add_kernel,
        in_specs=[vmem] * len(terms),
        out_specs=vmem,
        out_shape=shape(terms[0].shape, BF16),
        compiler_params=params(8),
        cost_estimate=cost(1e6, 1e6),
        name="add_terms",
    )(*terms)


def tie_kernel(value_ref, after_ref, out_ref):
    del value_ref, after_ref, out_ref


def tie(value, after):
    anywhere = pl.BlockSpec(memory_space=pl.ANY)
    return pl.pallas_call(
        tie_kernel,
        in_specs=[anywhere, anywhere],
        out_specs=anywhere,
        out_shape=shape(value.shape, value.dtype),
        input_output_aliases={0: 0},
        compiler_params=params(8),
        name="tie",
    )(value, after)


def spread_kernel(terms_ref, after_ref, out_ref):
    del after_ref
    total = jnp.sum(terms_ref[...].astype(F32), axis=0).astype(BF16)
    out_ref[...] = jnp.broadcast_to(total[None], out_ref.shape)


def spread_terms(terms, after):
    vmem = pl.BlockSpec(memory_space=pltpu.VMEM)
    return pl.pallas_call(
        spread_kernel,
        in_specs=[vmem, pl.BlockSpec(memory_space=pl.ANY)],
        out_specs=vmem,
        out_shape=shape(terms.shape, BF16),
        compiler_params=params(8),
        cost_estimate=cost(1e6, 6e5),
        name="spread_terms",
    )(terms, after)


def place_kernel(terms_ref, *outs):
    rows, width = terms_ref.shape[1:]
    n = outs[0].shape[1] // width
    for at in range(terms_ref.shape[0]):
        group, q = at // n, at % n
        per = outs[0].shape[0] // rows
        out = outs[group // per]
        first = group % per * rows
        out[first : first + rows, q * width : (q + 1) * width] = terms_ref[at].astype(F32)


def place_terms(terms, width, n):
    return pl.pallas_call(
        place_kernel,
        out_shape=[shape((width, n * width), F32)] * 2,
        compiler_params=params(8),
        cost_estimate=cost(1e5, 8e5),
        name="place_terms",
    )(terms)


def per_device(
    features, stale_features, grad_output, w_neigh, w_self, adj_tiles, tile_cols, send_idx, counts
):
    dom_count = lax.axis_size("dom")
    n = lax.axis_size("rep")
    row_count, width = features.shape
    row_tiles = row_count // TILE
    swap = functools.partial(
        lax.all_to_all, axis_name="dom", split_axis=0, concat_axis=0, tiled=True
    )
    me = lax.axis_index("rep").astype(jnp.int32).reshape(1)

    ids = send_idx[0]
    pos = tile_cols[0].reshape(-1)
    adj = adj_tiles[0]

    packed = gather_rows(ids, counts, stale_features)
    halo = swap(packed)
    own, wn, ws, pieces = prep(me, features, grad_output, w_neigh, w_self, packed, n)
    both = relative(exchange(pieces))

    agg = relative(exchange(spmm(me, pos, adj, [own, halo], n)))
    grad_agg, act, grad_pre = dense(agg, both, wn, ws)
    grad_agg = exchange(grad_agg)

    local, away = spmm_back(me, pos, adj, grad_agg, row_tiles, dom_count * CHUNKS)
    returned = swap(away)
    pieces = exchange(late(act, grad_pre, ws, away, n))
    out, grad_input = finish(me, local, pieces)
    terms = exchange(wgrad(me, agg, both, grad_pre, away, dom_count))

    blocks = dom_count // 8
    half = (blocks + 1) // 2
    terms = swap(tie(add_terms(terms), returned[0]))
    grad_stale, mark = scatter_rows(ids, counts, returned, row_count, 0, half, None)
    terms = swap(spread_terms(terms, mark))
    if blocks > half:
        grad_stale, _ = scatter_rows(
            ids, counts, returned, row_count, half, blocks - half, grad_stale
        )
    grad_neigh, grad_self = place_terms(terms, width, n)
    return (out, grad_input, grad_stale, grad_neigh, grad_self)


def solution(mesh):
    in_specs = (
        P("dom", "rep"),
        P("dom", "rep"),
        P("dom", "rep"),
        P(),
        P(),
        P("dom", None, None, None, None),
        P("dom", None, None),
        P("dom", None, None),
        P("dom", None),
    )
    out_specs = (P("dom", "rep"), P("dom", "rep"), P("dom", "rep"), P("rep", None), P("rep", None))
    return jax.shard_map(
        per_device, mesh=mesh, in_specs=in_specs, out_specs=out_specs, check_vma=False
    )
```

```python
import functools

import jax
import jax.numpy as jnp
from jax import lax
from jax.experimental import pallas as pl
from jax.experimental.pallas import tpu as pltpu
from jax.sharding import PartitionSpec as P

TILE = 128
B = 384
CHUNKS = B // TILE
LOW = 512
F32 = jnp.float32
BF16 = jnp.bfloat16
NT = (((1,), (1,)), ((), ()))
TN = (((0,), (0,)), ((), ()))


def params(mib):
    return pltpu.CompilerParams(vmem_limit_bytes=mib * 1024 * 1024)


def cost(flops, nbytes, trans=0):
    return pl.CostEstimate(flops=int(flops), bytes_accessed=int(nbytes), transcendentals=int(trans))


def shape(dims, dtype):
    return jax.ShapeDtypeStruct(dims, dtype)


def turned(block):
    return jnp.transpose(block.astype(F32))


def masked_ids(ids_ref, counts_ref, first, peers):
    base = pl.program_id(0) * ids_ref.shape[0]
    slot = lax.broadcasted_iota(jnp.int32, (1, ids_ref.shape[1]), 1)
    rows = [
        jnp.where(slot < counts_ref[0, base + p], ids_ref[p : p + 1, :], -1)
        for p in range(first, first + peers)
    ]
    return jnp.concatenate(rows, axis=1)


def low_onehot(ids):
    spot = lax.broadcasted_iota(jnp.int32, (LOW, ids.shape[1]), 0)
    return jnp.where(spot == (ids & (LOW - 1)), 1.0, 0.0).astype(BF16)


def in_group(ids, g):
    return (ids >= g * LOW) & (ids < (g + 1) * LOW)


def gather_kernel(ids_ref, counts_ref, table_ref, out_ref, flipped):
    groups = table_ref.shape[0] // LOW

    @pl.when(pl.program_id(0) == 0)
    def _():
        for g in range(groups):
            for k in range(LOW // TILE):
                block = table_ref[g * LOW + k * TILE : g * LOW + (k + 1) * TILE, :]
                flipped[g * TILE : (g + 1) * TILE, k * TILE : (k + 1) * TILE] = turned(block).astype(
                    BF16
                )

    for p in range(0, ids_ref.shape[0], 2):
        ids = masked_ids(ids_ref, counts_ref, p, 2)
        found = jnp.dot(flipped[...], low_onehot(ids), preferred_element_type=F32)
        total = jnp.zeros((TILE, ids.shape[1]), F32)
        for g in range(groups):
            total = jnp.where(in_group(ids, g), found[g * TILE : (g + 1) * TILE, :], total)
        total = total.astype(BF16)
        for k in range(2 * CHUNKS):
            out_ref[p * CHUNKS + k] = total[:, k * TILE : (k + 1) * TILE]


def gather_rows(ids, counts, table):
    peers = ids.shape[0]
    size = 8
    rows, cols = table.shape
    return pl.pallas_call(
        gather_kernel,
        grid=(peers // size,),
        in_specs=[
            pl.BlockSpec((size, B), lambda i: (i, 0)),
            pl.BlockSpec(memory_space=pltpu.SMEM),
            pl.BlockSpec((rows, cols), lambda i: (0, 0)),
        ],
        out_specs=pl.BlockSpec((size * CHUNKS, TILE, TILE), lambda i: (i, 0, 0)),
        out_shape=shape((peers * CHUNKS, TILE, TILE), BF16),
        scratch_shapes=[pltpu.VMEM((rows // LOW * TILE, LOW), BF16)],
        compiler_params=params(56),
        cost_estimate=cost(2 * ids.size * rows * cols, 4e6),
        name="gather_rows",
    )(ids, counts, table)


def exchange(pieces):
    n = len(pieces)
    return [pieces[0]] + [
        lax.ppermute(pieces[s], "rep", [(i, (i + s) % n) for i in range(n)]) for s in range(1, n)
    ]


def relative(received):
    n = len(received)
    return [received[(n - j) % n] for j in range(n)]


def prep_kernel(me_ref, feat_ref, up_ref, wn_ref, ws_ref, after_ref, own_ref, wn_out, ws_out, *pieces):
    del after_ref
    step = pl.program_id(0)
    n = len(pieces)
    for k in range(own_ref.shape[0]):
        own_ref[k] = turned(feat_ref[k * TILE : (k + 1) * TILE, :]).astype(BF16)
    for j, piece in enumerate(pieces):
        column = pl.multiple_of(lax.rem(me_ref[0] + j, n) * TILE, TILE)
        wn_out[:, j * TILE : (j + 1) * TILE] = wn_ref[:, pl.ds(column, TILE)]
        ws_out[:, j * TILE : (j + 1) * TILE] = ws_ref[:, pl.ds(column, TILE)]

        @pl.when(step == j)
        def _():
            piece[0] = feat_ref[...]
            piece[1] = up_ref[...]


def prep(me, features, upstream, wn, ws, after, n):
    rows, width = features.shape
    share = rows // n
    full = wn.shape[0]
    chunk = pl.BlockSpec((share, width), lambda i, me: (lax.rem(me[0] + i, n), 0))
    weight = pl.BlockSpec((width, full), lambda i, me: (lax.rem(me[0] + i, n), 0))
    placed = pl.BlockSpec((width, full), lambda i, me: (i, 0))
    own, wn, ws, *pieces = pl.pallas_call(
        prep_kernel,
        grid_spec=pltpu.PrefetchScalarGridSpec(
            num_scalar_prefetch=1,
            grid=(n,),
            in_specs=[chunk, chunk, weight, weight, pl.BlockSpec(memory_space=pl.ANY)],
            out_specs=[
                pl.BlockSpec(
                    (share // TILE, TILE, TILE), lambda i, me: (lax.rem(me[0] + i, n), 0, 0)
                ),
                placed,
                placed,
            ]
            + [pl.BlockSpec((2, share, width), lambda i, me: (0, 0, 0))] * n,
        ),
        out_shape=[
            pltpu.HBM((rows // TILE, TILE, TILE), BF16),
            pltpu.HBM((full, full), BF16),
            pltpu.HBM((full, full), BF16),
        ]
        + [shape((2, share, width), BF16)] * n,
        compiler_params=params(56),
        cost_estimate=cost(1e10, 6e6),
        name="prep",
    )(me, features, upstream, wn, ws, after)
    return own, wn, ws, pieces


BLOCKS = 3


def adj_copies(adj_ref, held, sems, inner, chunk_of):
    def copy(step):
        first = (chunk_of(step // inner) * inner + lax.rem(step, inner)) * BLOCKS
        return pltpu.make_async_copy(
            adj_ref.at[pl.ds(first, BLOCKS)], held.at[pl.ds(step * BLOCKS, BLOCKS)], sems.at[step]
        )

    return copy


def spmm_kernel(me_ref, pos_ref, *refs, n, start_chunk, extras):
    adj_ref, parts, outs, (ext, sems, adj, adj_sems) = (
        refs[0],
        refs[1 : 3],
        refs[3 + extras : -4],
        refs[-4:],
    )
    chunk, part = pl.program_id(0), pl.program_id(1)
    inner = adj_sems.shape[0] // len(outs)
    step = chunk * inner + part
    per_row = adj.shape[1]
    copy_of = adj_copies(
        adj_ref, adj, adj_sems, inner, lambda c: lax.rem(me_ref[0] + start_chunk + c, n)
    )

    @pl.when((chunk == 0) & (part == 0))
    def _():
        copies, start, at = [], 0, 0
        for source in parts:
            size = source.shape[0] // 4
            for k in range(4):
                copies.append(
                    pltpu.make_async_copy(
                        source.at[pl.ds(k * size, size)], ext.at[pl.ds(start, size)], sems.at[at]
                    )
                )
                start, at = start + size, at + 1
        for copy in copies:
            copy.start()
        copy_of(0).start()
        for copy in copies:
            copy.wait()
        for k in range(1, adj_sems.shape[0]):
            copy_of(k).start()

    copy_of(step).wait()
    first = (lax.rem(me_ref[0] + start_chunk + chunk, n) * inner + part) * BLOCKS
    done = []
    for r in range(BLOCKS):
        base = (first + r) * per_row
        total = None
        for t in range(0, per_row, 2):
            left = jnp.concatenate([adj[step * BLOCKS + r, t], adj[step * BLOCKS + r, t + 1]], axis=1)
            right = jnp.concatenate([ext[pos_ref[base + t]], ext[pos_ref[base + t + 1]]], axis=1)
            term = lax.dot_general(left, right, NT, preferred_element_type=F32)
            total = term if total is None else total + term
        done.append(total.astype(BF16))
    done = jnp.concatenate(done, axis=0)
    size = BLOCKS * TILE
    place = pl.ds(pl.multiple_of(part * size, size), size)
    for j, out in enumerate(outs):

        @pl.when(chunk == j)
        def _():
            out[place, :] = done


def spmm(me, pos, adj, parts, n, start_chunk, count, after):
    row_tiles, per_row = adj.shape[:2]
    inner = row_tiles // n // BLOCKS
    share = row_tiles // n * TILE
    col_tiles = sum(p.shape[0] for p in parts)
    return pl.pallas_call(
        functools.partial(spmm_kernel, n=n, start_chunk=start_chunk, extras=len(after)),
        grid_spec=pltpu.PrefetchScalarGridSpec(
            num_scalar_prefetch=2,
            grid=(count, inner),
            in_specs=[pl.BlockSpec(memory_space=pl.ANY)] * (1 + len(parts) + len(after)),
            out_specs=[pl.BlockSpec((share, TILE), lambda i, k, me, pos: (0, 0))] * count,
            scratch_shapes=[
                pltpu.VMEM((col_tiles, TILE, TILE), BF16),
                pltpu.SemaphoreType.DMA((4 * len(parts),)),
                pltpu.VMEM((count * inner * BLOCKS, *adj.shape[1:]), BF16),
                pltpu.SemaphoreType.DMA((count * inner,)),
            ],
        ),
        out_shape=[shape((share, TILE), BF16)] * count,
        compiler_params=params(52),
        cost_estimate=cost(2 * count * share * per_row * TILE**2 * 8, 1e7),
        name="spmm",
    )(me, pos, adj, *parts, *after)


def joined(refs):
    return jnp.concatenate([ref[...] for ref in refs], axis=1)


def dense_kernel(*refs, n):
    agg, both, (wn_ref, ws_ref), rest = refs[:n], refs[n : 2 * n], refs[2 * n : 2 * n + 2], refs[2 * n + 2 :]
    ga, (act_ref, gp_ref) = rest[:n], rest[n:]
    wn = wn_ref[...]
    v = jnp.dot(joined(agg), wn, preferred_element_type=F32) + jnp.dot(
        joined([ref.at[0] for ref in both]), ws_ref[...], preferred_element_type=F32
    )
    root = 0.7978845608028654
    square = v * v
    t = jnp.tanh(root * v * (1.0 + 0.044715 * square))
    half = 0.5 * (1.0 + t)
    slope = half + 0.5 * v * (1.0 - t * t) * (root * (1.0 + 0.134145 * square))
    gp = (joined([ref.at[1] for ref in both]).astype(F32) * slope).astype(BF16)
    act_ref[...] = (v * half).astype(BF16)
    gp_ref[...] = gp
    back = lax.dot_general(wn, gp, NT, preferred_element_type=F32).astype(BF16)
    width = back.shape[0] // n
    for q in range(n):
        ga[q][...] = back[q * width : (q + 1) * width, :]


def dense(agg, both, wn, ws):
    n = len(agg)
    rows, width = agg[0].shape
    full = n * width
    size = 256
    weight = pl.BlockSpec((full, full), lambda i: (0, 0))
    whole = pl.BlockSpec((size, full), lambda i: (i, 0))
    results = pl.pallas_call(
        functools.partial(dense_kernel, n=n),
        grid=(rows // size,),
        in_specs=[pl.BlockSpec((size, width), lambda i: (i, 0))] * n
        + [pl.BlockSpec((2, size, width), lambda i: (0, i, 0))] * n
        + [weight, weight],
        out_specs=[pl.BlockSpec((width, size), lambda i: (0, i))] * n + [whole, whole],
        out_shape=[shape((width, rows), BF16)] * n + [pltpu.HBM((rows, full), BF16)] * 2,
        compiler_params=params(24),
        cost_estimate=cost(6 * rows * full * full, 7e6, rows * full),
        name="dense",
    )(*agg, *both, wn, ws)
    return results[:n], results[n], results[n + 1]


def wgrad_kernel(me_ref, *refs, n):
    agg, both, gp_ref, out_ref = refs[:n], refs[n : 2 * n], refs[2 * n], refs[-1]
    gp = gp_ref[...]
    rows = out_ref.shape[2]
    width = agg[0].shape[1]
    for j in range(n):
        for kind, left in enumerate((agg[j][...], both[j][0])):
            term = lax.dot_general(left, gp, TN, preferred_element_type=F32).astype(BF16)
            for i in range(n):
                q = lax.rem(me_ref[0] + i, n)
                for k in range(width // rows):
                    at = (kind * (width // rows) + k) * n + q
                    out_ref[at, j] = term[k * rows : (k + 1) * rows, i * TILE : (i + 1) * TILE]


def wgrad(me, agg, both, gp, dom_count):
    n = len(agg)
    rows, width = agg[0].shape
    size = 2 * width * n // dom_count
    vmem = pl.BlockSpec(memory_space=pltpu.VMEM)
    return pl.pallas_call(
        functools.partial(wgrad_kernel, n=n),
        in_specs=[pl.BlockSpec(memory_space=pltpu.SMEM)]
        + [vmem] * (2 * n + 1),
        out_specs=vmem,
        out_shape=shape((dom_count, n, size, TILE), BF16),
        compiler_params=params(24),
        cost_estimate=cost(1e10, 4e6),
        name="wgrad",
    )(me, *agg, *both, gp)


PIECES = 6


def spmm_back_kernel(me_ref, pos_ref, *refs, n):
    adj_ref, ga = refs[0], refs[1 : 1 + n]
    local_ref, away_ref, total, left_ref, stage, sems, adj, adj_sems = refs[1 + n :]
    chunk, part = pl.program_id(0), pl.program_id(1)
    inner = adj_sems.shape[0] // n
    step = chunk * inner + part
    per_row = adj.shape[1]
    copy_of = adj_copies(adj_ref, adj, adj_sems, inner, lambda c: lax.rem(me_ref[0] + n - c, n))
    size = BLOCKS * TILE

    @pl.when((chunk == 0) & (part == 0))
    def _():
        for k in range(adj_sems.shape[0]):
            copy_of(k).start()
        total[...] = jnp.zeros_like(total)

    for s in range(n):

        @pl.when((chunk == s) & (part == 0))
        def _():
            for k in range(left_ref.shape[0]):
                left_ref[k] = ga[s][:, k * size : (k + 1) * size]

    copy_of(step).wait()
    first = (lax.rem(me_ref[0] + n - chunk, n) * pl.num_programs(1) + part) * BLOCKS
    for r in range(BLOCKS):
        base = (first + r) * per_row
        left = left_ref[part, :, r * TILE : (r + 1) * TILE]
        for t in range(0, per_row, 2):
            right = jnp.concatenate([adj[step * BLOCKS + r, t], adj[step * BLOCKS + r, t + 1]], axis=1)
            both = jnp.dot(left, right, preferred_element_type=F32)
            total[pos_ref[base + t]] += both[:, :TILE]
            total[pos_ref[base + t + 1]] += both[:, TILE:]

    @pl.when((chunk == n - 1) & (part == pl.num_programs(1) - 1))
    def _():
        own = local_ref.shape[0]
        step = away_ref.shape[0] // PIECES
        copies = [pltpu.make_async_copy(total.at[pl.ds(0, own)], local_ref, sems.at[PIECES])]
        copies[0].start()
        for k in range(PIECES):
            stage[k * step : (k + 1) * step] = total[own + k * step : own + (k + 1) * step].astype(BF16)
            copies.append(
                pltpu.make_async_copy(
                    stage.at[pl.ds(k * step, step)], away_ref.at[pl.ds(k * step, step)], sems.at[k]
                )
            )
            copies[-1].start()
        for copy in copies:
            copy.wait()


def spmm_back(me, pos, adj, ga, own, away):
    n = len(ga)
    row_tiles, per_row = adj.shape[:2]
    rows = ga[0].shape[1]
    inner = row_tiles // n // BLOCKS
    return pl.pallas_call(
        functools.partial(spmm_back_kernel, n=n),
        grid_spec=pltpu.PrefetchScalarGridSpec(
            num_scalar_prefetch=2,
            grid=(n, inner),
            in_specs=[pl.BlockSpec(memory_space=pl.ANY)]
            + [pl.BlockSpec((TILE, rows), lambda i, k, me, pos: (0, 0))] * n,
            out_specs=[pl.BlockSpec(memory_space=pl.ANY)] * 2,
            scratch_shapes=[
                pltpu.VMEM((own + away, TILE, TILE), F32),
                pltpu.VMEM((inner, TILE, BLOCKS * TILE), BF16),
                pltpu.VMEM((away, TILE, TILE), BF16),
                pltpu.SemaphoreType.DMA((PIECES + 1,)),
                pltpu.VMEM(adj.shape, BF16),
                pltpu.SemaphoreType.DMA((n * inner,)),
            ],
        ),
        out_shape=[pltpu.HBM((own, TILE, TILE), F32), pltpu.HBM((away, TILE, TILE), BF16)],
        compiler_params=params(52),
        cost_estimate=cost(2 * row_tiles * per_row * TILE**3 * 2, 2.2e7),
        name="spmm_back",
    )(me, pos, adj, *ga)


def late_kernel(act_ref, gp_ref, ws_ref, after_ref, *pieces):
    del after_ref
    direct = lax.dot_general(gp_ref[...], ws_ref[...], NT, preferred_element_type=F32).astype(BF16)
    for j, piece in enumerate(pieces):
        piece[0] = act_ref[:, j * TILE : (j + 1) * TILE]
        piece[1] = direct[:, j * TILE : (j + 1) * TILE]


def late(act, gp, ws, after, n):
    rows, full = act.shape
    size = 256
    share = pl.BlockSpec((size, full), lambda i: (i, 0))
    return pl.pallas_call(
        late_kernel,
        grid=(rows // size,),
        in_specs=[
            share,
            share,
            pl.BlockSpec((full, full), lambda i: (0, 0)),
            pl.BlockSpec(memory_space=pl.ANY),
        ],
        out_specs=[pl.BlockSpec((2, size, TILE), lambda i: (0, i, 0))] * n,
        out_shape=[shape((2, rows, TILE), BF16)] * n,
        compiler_params=params(24),
        cost_estimate=cost(1e10, 6e6),
        name="late",
    )(act, gp, ws, after)


def finish_kernel(me_ref, ext_ref, *refs):
    pieces, (out_ref, grad_ref) = refs[:-2], refs[-2:]
    for s, piece in enumerate(pieces):

        @pl.when(pl.program_id(0) == s)
        def _():
            out_ref[...] = piece[0]
            for k in range(ext_ref.shape[0]):
                rows = slice(k * TILE, (k + 1) * TILE)
                total = piece[1, rows, :].astype(F32) + jnp.transpose(ext_ref[k])
                grad_ref[rows, :] = total.astype(BF16)


def finish(me, ext, pieces):
    n = len(pieces)
    share = pieces[0].shape[1]
    placed = pl.BlockSpec((share, TILE), lambda i, me: (lax.rem(me[0] + n - i, n), 0))
    return pl.pallas_call(
        finish_kernel,
        grid_spec=pltpu.PrefetchScalarGridSpec(
            num_scalar_prefetch=1,
            grid=(n,),
            in_specs=[
                pl.BlockSpec(
                    (share // TILE, TILE, TILE), lambda i, me: (lax.rem(me[0] + n - i, n), 0, 0)
                )
            ]
            + [pl.BlockSpec((2, share, TILE), lambda i, me: (0, 0, 0))] * n,
            out_specs=[placed, placed],
        ),
        out_shape=[shape((n * share, TILE), BF16)] * 2,
        compiler_params=params(24),
        cost_estimate=cost(1e6, 7e6),
        name="finish",
    )(me, ext, *pieces)


def scatter_kernel(ids_ref, counts_ref, val_ref, out_ref):
    groups = out_ref.shape[0] // LOW

    @pl.when(pl.program_id(0) == 0)
    def _():
        out_ref[...] = jnp.zeros_like(out_ref)

    for p in range(0, ids_ref.shape[0], 2):
        ids = masked_ids(ids_ref, counts_ref, p, 2)
        onehot = low_onehot(ids)
        values = jnp.concatenate([val_ref[p * CHUNKS + k] for k in range(2 * CHUNKS)], axis=1)
        zero = jnp.zeros_like(values)
        for g in range(0, groups, 2):
            pair = [jnp.where(in_group(ids, k), values, zero) for k in (g, g + 1)]
            both = lax.dot_general(
                onehot, jnp.concatenate(pair, axis=0), NT, preferred_element_type=F32
            )
            out_ref[g * LOW : (g + 1) * LOW, :] += both[:, :TILE]
            out_ref[(g + 1) * LOW : (g + 2) * LOW, :] += both[:, TILE:]


def scatter_rows(ids, counts, values, rows):
    peers = ids.shape[0]
    size = 8
    return pl.pallas_call(
        scatter_kernel,
        grid=(peers // size,),
        in_specs=[
            pl.BlockSpec((size, B), lambda i: (i, 0)),
            pl.BlockSpec(memory_space=pltpu.SMEM),
            pl.BlockSpec((size * CHUNKS, TILE, TILE), lambda i: (i, 0, 0)),
        ],
        out_specs=pl.BlockSpec((rows, TILE), lambda i: (0, 0)),
        out_shape=shape((rows, TILE), F32),
        compiler_params=params(40),
        cost_estimate=cost(8 * ids.size * rows * TILE, 4e6),
        name="scatter_rows",
    )(ids, counts, values)


def sum_kernel(terms_ref, after_ref, *outs):
    del after_ref
    total = jnp.sum(terms_ref[...].astype(F32), axis=0).astype(BF16)
    for j, out in enumerate(outs):
        out[...] = total[j]


def sum_terms(terms, after):
    n = terms.shape[1]
    return pl.pallas_call(
        sum_kernel,
        in_specs=[pl.BlockSpec(memory_space=pltpu.VMEM), pl.BlockSpec(memory_space=pl.ANY)],
        out_specs=[pl.BlockSpec(memory_space=pltpu.VMEM)] * n,
        out_shape=[shape(terms.shape[2:], BF16)] * n,
        compiler_params=params(16),
        cost_estimate=cost(1e9, 1e6),
        name="sum_terms",
    )(terms, after)


def spread_kernel(*refs):
    terms, out_ref = refs[:-2], refs[-1]
    total = terms[0][...].astype(F32)
    for term in terms[1:]:
        total = total + term[...].astype(F32)
    out_ref[...] = jnp.broadcast_to(total.astype(BF16)[None], out_ref.shape)


def spread_terms(terms, after, dom_count):
    return pl.pallas_call(
        spread_kernel,
        in_specs=[pl.BlockSpec(memory_space=pltpu.VMEM)] * len(terms)
        + [pl.BlockSpec(memory_space=pl.ANY)],
        out_specs=pl.BlockSpec(memory_space=pltpu.VMEM),
        out_shape=shape((dom_count, *terms[0].shape), BF16),
        compiler_params=params(8),
        cost_estimate=cost(1e5, 3e5),
        name="spread_terms",
    )(*terms, after)


def place_kernel(terms_ref, *outs):
    rows, width = terms_ref.shape[1:]
    n = outs[0].shape[1] // width
    for at in range(terms_ref.shape[0]):
        group, q = at // n, at % n
        per = outs[0].shape[0] // rows
        out = outs[group // per]
        first = group % per * rows
        out[first : first + rows, q * width : (q + 1) * width] = terms_ref[at].astype(F32)


def place_terms(terms, width, n):
    return pl.pallas_call(
        place_kernel,
        out_shape=[shape((width, n * width), F32)] * 2,
        compiler_params=params(8),
        cost_estimate=cost(1e5, 8e5),
        name="place_terms",
    )(terms)


def per_device(
    features, stale_features, grad_output, w_neigh, w_self, adj_tiles, tile_cols, send_idx, counts
):
    dom_count = lax.axis_size("dom")
    n = lax.axis_size("rep")
    row_count, width = features.shape
    row_tiles = row_count // TILE
    swap = functools.partial(
        lax.all_to_all, axis_name="dom", split_axis=0, concat_axis=0, tiled=True
    )
    me = lax.axis_index("rep").astype(jnp.int32).reshape(1)

    ids = send_idx[0]
    pos = tile_cols[0].reshape(-1)
    adj = adj_tiles[0]

    packed = gather_rows(ids, counts, stale_features)
    halo = swap(packed)
    own, wn, ws, pieces = prep(me, features, grad_output, w_neigh, w_self, packed, n)
    both = relative(exchange(pieces))

    half = n // 2
    early = spmm(me, pos, adj, [own, halo], n, 1, half, [])
    rest = spmm(me, pos, adj, [own, halo], n, 1 + half, n - half, [early[-1]])
    agg = relative(exchange([rest[-1], *early, *rest[:-1]]))
    grad_agg, act, grad_pre = dense(agg, both, wn, ws)
    grad_agg = exchange(grad_agg)
    terms = swap(wgrad(me, agg, both, grad_pre, dom_count))

    local, away = spmm_back(me, pos, adj, grad_agg, row_tiles, dom_count * CHUNKS)
    returned = swap(away)
    pieces = exchange(late(act, grad_pre, ws, away, n))
    out, grad_input = finish(me, local, pieces)
    terms = exchange(sum_terms(terms, away))

    terms = swap(spread_terms(terms, returned[0], dom_count))
    grad_stale = scatter_rows(ids, counts, returned, row_count)
    grad_neigh, grad_self = place_terms(terms, width, n)
    return (out, grad_input, grad_stale, grad_neigh, grad_self)


def solution(mesh):
    in_specs = (
        P("dom", "rep"),
        P("dom", "rep"),
        P("dom", "rep"),
        P(),
        P(),
        P("dom", None, None, None, None),
        P("dom", None, None),
        P("dom", None, None),
        P("dom", None),
    )
    out_specs = (P("dom", "rep"), P("dom", "rep"), P("dom", "rep"), P("rep", None), P("rep", None))
    return jax.shard_map(
        per_device, mesh=mesh, in_specs=in_specs, out_specs=out_specs, check_vma=False
    )
```

```python
import functools

import jax
import jax.numpy as jnp
from jax import lax
from jax.experimental import pallas as pl
from jax.experimental.pallas import tpu as pltpu
from jax.sharding import PartitionSpec as P

TILE = 128
B = 384
CHUNKS = B // TILE
LOW_BITS = 9
LOW = 1 << LOW_BITS
F32 = jnp.float32
BF16 = jnp.bfloat16
NT = (((1,), (1,)), ((), ()))
TN = (((0,), (0,)), ((), ()))


def params(mib):
    return pltpu.CompilerParams(vmem_limit_bytes=mib * 1024 * 1024)


def cost(flops, nbytes, trans=0):
    return pl.CostEstimate(flops=int(flops), bytes_accessed=int(nbytes), transcendentals=int(trans))


def shape(dims, dtype):
    return jax.ShapeDtypeStruct(dims, dtype)


def turned(block):
    return jnp.transpose(block.astype(F32))


def masked_ids(ids_ref, counts_ref, first, peers):
    base = pl.program_id(0) * ids_ref.shape[0]
    slot = lax.broadcasted_iota(jnp.int32, (1, ids_ref.shape[1]), 1)
    rows = [
        jnp.where(slot < counts_ref[0, base + p], ids_ref[p : p + 1, :], -1)
        for p in range(first, first + peers)
    ]
    return jnp.concatenate(rows, axis=1)


def low_onehot(ids):
    spot = lax.broadcasted_iota(jnp.int32, (LOW, ids.shape[1]), 0).astype(jnp.int16)
    low = jnp.broadcast_to((ids & (LOW - 1)).astype(jnp.int16), spot.shape)
    return jnp.where(spot == low, jnp.ones(spot.shape, BF16), jnp.zeros(spot.shape, BF16))


def in_group(ids, g):
    return (ids >= g * LOW) & (ids < (g + 1) * LOW)


def gather_kernel(ids_ref, counts_ref, table_ref, out_ref, flipped):
    groups = table_ref.shape[0] // LOW

    @pl.when(pl.program_id(0) == 0)
    def _():
        for g in range(groups):
            for k in range(LOW // TILE):
                block = table_ref[g * LOW + k * TILE : g * LOW + (k + 1) * TILE, :]
                flipped[g * TILE : (g + 1) * TILE, k * TILE : (k + 1) * TILE] = turned(block).astype(
                    BF16
                )

    for p in range(0, ids_ref.shape[0], 2):
        ids = masked_ids(ids_ref, counts_ref, p, 2)
        found = jnp.dot(flipped[...], low_onehot(ids), preferred_element_type=F32)
        total = jnp.zeros((TILE, ids.shape[1]), F32)
        for g in range(groups):
            total = jnp.where(in_group(ids, g), found[g * TILE : (g + 1) * TILE, :], total)
        total = total.astype(BF16)
        for k in range(2 * CHUNKS):
            out_ref[p * CHUNKS + k] = total[:, k * TILE : (k + 1) * TILE]


def gather_rows(ids, counts, table):
    peers = ids.shape[0]
    size = 8
    rows, cols = table.shape
    return pl.pallas_call(
        gather_kernel,
        grid=(peers // size,),
        in_specs=[
            pl.BlockSpec((size, B), lambda i: (i, 0)),
            pl.BlockSpec(memory_space=pltpu.SMEM),
            pl.BlockSpec((rows, cols), lambda i: (0, 0)),
        ],
        out_specs=pl.BlockSpec((size * CHUNKS, TILE, TILE), lambda i: (i, 0, 0)),
        out_shape=shape((peers * CHUNKS, TILE, TILE), BF16),
        scratch_shapes=[pltpu.VMEM((rows // LOW * TILE, LOW), BF16)],
        compiler_params=params(56),
        cost_estimate=cost(2 * ids.size * rows * cols, 4e6),
        name="gather_rows",
    )(ids, counts, table)


def exchange(pieces):
    n = len(pieces)
    return [pieces[0]] + [
        lax.ppermute(pieces[s], "rep", [(i, (i + s) % n) for i in range(n)]) for s in range(1, n)
    ]


def relative(received):
    n = len(received)
    return [received[(n - j) % n] for j in range(n)]


def prep_kernel(me_ref, feat_ref, up_ref, wn_ref, ws_ref, after_ref, own_ref, wn_out, ws_out, *pieces):
    del after_ref
    step = pl.program_id(0)
    n = len(pieces)
    for k in range(own_ref.shape[0]):
        own_ref[k] = turned(feat_ref[k * TILE : (k + 1) * TILE, :]).astype(BF16)
    for j, piece in enumerate(pieces):
        column = pl.multiple_of(lax.rem(me_ref[0] + j, n) * TILE, TILE)
        wn_out[:, j * TILE : (j + 1) * TILE] = wn_ref[:, pl.ds(column, TILE)]
        ws_out[:, j * TILE : (j + 1) * TILE] = ws_ref[:, pl.ds(column, TILE)]

        @pl.when(step == j)
        def _():
            piece[0] = feat_ref[...]
            piece[1] = up_ref[...]


def prep(me, features, upstream, wn, ws, after, n):
    rows, width = features.shape
    share = rows // n
    full = wn.shape[0]
    chunk = pl.BlockSpec((share, width), lambda i, me: (lax.rem(me[0] + i, n), 0))
    weight = pl.BlockSpec((width, full), lambda i, me: (lax.rem(me[0] + i, n), 0))
    placed = pl.BlockSpec((width, full), lambda i, me: (i, 0))
    own, wn, ws, *pieces = pl.pallas_call(
        prep_kernel,
        grid_spec=pltpu.PrefetchScalarGridSpec(
            num_scalar_prefetch=1,
            grid=(n,),
            in_specs=[chunk, chunk, weight, weight, pl.BlockSpec(memory_space=pl.ANY)],
            out_specs=[
                pl.BlockSpec(
                    (share // TILE, TILE, TILE), lambda i, me: (lax.rem(me[0] + i, n), 0, 0)
                ),
                placed,
                placed,
            ]
            + [pl.BlockSpec((2, share, width), lambda i, me: (0, 0, 0))] * n,
        ),
        out_shape=[
            pltpu.HBM((rows // TILE, TILE, TILE), BF16),
            pltpu.HBM((full, full), BF16),
            pltpu.HBM((full, full), BF16),
        ]
        + [shape((2, share, width), BF16)] * n,
        compiler_params=params(56),
        cost_estimate=cost(1e10, 6e6),
        name="prep",
    )(me, features, upstream, wn, ws, after)
    return own, wn, ws, pieces


BLOCKS = 3


def adj_copies(adj_ref, held, sems, inner, chunk_of):
    def copy(step):
        first = (chunk_of(step // inner) * inner + lax.rem(step, inner)) * BLOCKS
        return pltpu.make_async_copy(
            adj_ref.at[pl.ds(first, BLOCKS)], held.at[pl.ds(step * BLOCKS, BLOCKS)], sems.at[step]
        )

    return copy


def spmm_kernel(me_ref, pos_ref, *refs, n, start_chunk, extras):
    adj_ref, parts, outs, (ext, sems, adj, adj_sems) = (
        refs[0],
        refs[1 : 3],
        refs[3 + extras : -4],
        refs[-4:],
    )
    chunk, part = pl.program_id(0), pl.program_id(1)
    inner = adj_sems.shape[0] // len(outs)
    step = chunk * inner + part
    per_row = adj.shape[1]
    copy_of = adj_copies(
        adj_ref, adj, adj_sems, inner, lambda c: lax.rem(me_ref[0] + start_chunk + c, n)
    )

    @pl.when((chunk == 0) & (part == 0))
    def _():
        copies, start, at = [], 0, 0
        for source in parts:
            size = source.shape[0] // 4
            for k in range(4):
                copies.append(
                    pltpu.make_async_copy(
                        source.at[pl.ds(k * size, size)], ext.at[pl.ds(start, size)], sems.at[at]
                    )
                )
                start, at = start + size, at + 1
        for copy in copies:
            copy.start()
        copy_of(0).start()
        for copy in copies:
            copy.wait()
        for k in range(1, adj_sems.shape[0]):
            copy_of(k).start()

    copy_of(step).wait()
    first = (lax.rem(me_ref[0] + start_chunk + chunk, n) * inner + part) * BLOCKS
    done = []
    for r in range(BLOCKS):
        base = (first + r) * per_row
        total = None
        for t in range(0, per_row, 2):
            left = jnp.concatenate([adj[step * BLOCKS + r, t], adj[step * BLOCKS + r, t + 1]], axis=1)
            right = jnp.concatenate([ext[pos_ref[base + t]], ext[pos_ref[base + t + 1]]], axis=1)
            term = lax.dot_general(left, right, NT, preferred_element_type=F32)
            total = term if total is None else total + term
        done.append(total.astype(BF16))
    done = jnp.concatenate(done, axis=0)
    size = BLOCKS * TILE
    place = pl.ds(pl.multiple_of(part * size, size), size)
    for j, out in enumerate(outs):

        @pl.when(chunk == j)
        def _():
            out[place, :] = done


def spmm(me, pos, adj, parts, n, start_chunk, count, after):
    row_tiles, per_row = adj.shape[:2]
    inner = row_tiles // n // BLOCKS
    share = row_tiles // n * TILE
    col_tiles = sum(p.shape[0] for p in parts)
    return pl.pallas_call(
        functools.partial(spmm_kernel, n=n, start_chunk=start_chunk, extras=len(after)),
        grid_spec=pltpu.PrefetchScalarGridSpec(
            num_scalar_prefetch=2,
            grid=(count, inner),
            in_specs=[pl.BlockSpec(memory_space=pl.ANY)] * (1 + len(parts) + len(after)),
            out_specs=[pl.BlockSpec((share, TILE), lambda i, k, me, pos: (0, 0))] * count,
            scratch_shapes=[
                pltpu.VMEM((col_tiles, TILE, TILE), BF16),
                pltpu.SemaphoreType.DMA((4 * len(parts),)),
                pltpu.VMEM((count * inner * BLOCKS, *adj.shape[1:]), BF16),
                pltpu.SemaphoreType.DMA((count * inner,)),
            ],
        ),
        out_shape=[shape((share, TILE), BF16)] * count,
        compiler_params=params(56),
        cost_estimate=cost(2 * count * share * per_row * TILE**2 * 8, 1e7),
        name="spmm",
    )(me, pos, adj, *parts, *after)


def joined(refs):
    return jnp.concatenate([ref[...] for ref in refs], axis=1)


def dense_kernel(me_ref, *refs, n):
    agg, both, (wn_ref, ws_ref), rest = refs[:n], refs[n : 2 * n], refs[2 * n : 2 * n + 2], refs[2 * n + 2 :]
    ga, (act_ref, gp_ref, terms_ref, total) = rest[:n], rest[n:]
    step = pl.program_id(0)
    wn = wn_ref[...]
    feat = [ref[0] for ref in both]
    v = jnp.dot(joined(agg), wn, preferred_element_type=F32) + jnp.dot(
        jnp.concatenate(feat, axis=1), ws_ref[...], preferred_element_type=F32
    )
    root = 0.7978845608028654
    square = v * v
    t = jnp.tanh(root * v * (1.0 + 0.044715 * square))
    half = 0.5 * (1.0 + t)
    slope = half + 0.5 * v * (1.0 - t * t) * (root * (1.0 + 0.134145 * square))
    gp = (joined([ref.at[1] for ref in both]).astype(F32) * slope).astype(BF16)
    act_ref[...] = (v * half).astype(BF16)
    gp_ref[...] = gp
    back = lax.dot_general(wn, gp, NT, preferred_element_type=F32).astype(BF16)
    width = back.shape[0] // n
    for q in range(n):
        ga[q][...] = back[q * width : (q + 1) * width, :]

    @pl.when(step == 0)
    def _():
        total[...] = jnp.zeros_like(total)

    for j in range(n):
        for kind, left in enumerate((agg[j][...], feat[j])):
            total[2 * j + kind] += lax.dot_general(left, gp, TN, preferred_element_type=F32)

    @pl.when(step == pl.num_programs(0) - 1)
    def _():
        rows = terms_ref.shape[2]
        for j in range(n):
            for kind in range(2):
                term = total[2 * j + kind].astype(BF16)
                for i in range(n):
                    q = lax.rem(me_ref[0] + i, n)
                    for k in range(width // rows):
                        at = (kind * (width // rows) + k) * n + q
                        terms_ref[at, j] = term[k * rows : (k + 1) * rows, i * width : (i + 1) * width]


def dense(me, agg, both, wn, ws, dom_count):
    n = len(agg)
    rows, width = agg[0].shape
    full = n * width
    size = 256
    piece = (dom_count, n, 2 * width * n // dom_count, width)
    weight = pl.BlockSpec((full, full), lambda i, me: (0, 0))
    whole = pl.BlockSpec((size, full), lambda i, me: (i, 0))
    results = pl.pallas_call(
        functools.partial(dense_kernel, n=n),
        grid_spec=pltpu.PrefetchScalarGridSpec(
            num_scalar_prefetch=1,
            grid=(rows // size,),
            in_specs=[pl.BlockSpec((size, width), lambda i, me: (i, 0))] * n
            + [pl.BlockSpec((2, size, width), lambda i, me: (0, i, 0))] * n
            + [weight, weight],
            out_specs=[pl.BlockSpec((width, size), lambda i, me: (0, i))] * n
            + [whole, whole, pl.BlockSpec(piece, lambda i, me: (0, 0, 0, 0))],
            scratch_shapes=[pltpu.VMEM((2 * n, width, full), F32)],
        ),
        out_shape=[shape((width, rows), BF16)] * n
        + [pltpu.HBM((rows, full), BF16)] * 2
        + [pltpu.HBM(piece, BF16)],
        compiler_params=params(24),
        cost_estimate=cost(10 * rows * full * full, 9e6, rows * full),
        name="dense",
    )(me, *agg, *both, wn, ws)
    return results[:n], *results[n:]


PIECES = 6


def spmm_back_kernel(me_ref, pos_ref, *refs, n):
    adj_ref, ga = refs[0], refs[1 : 1 + n]
    local_ref, away_ref, total, left_ref, stage, sems, adj, adj_sems = refs[1 + n :]
    chunk, part = pl.program_id(0), pl.program_id(1)
    inner = adj_sems.shape[0] // n
    step = chunk * inner + part
    per_row = adj.shape[1]
    copy_of = adj_copies(adj_ref, adj, adj_sems, inner, lambda c: lax.rem(me_ref[0] + n - c, n))
    size = BLOCKS * TILE

    @pl.when((chunk == 0) & (part == 0))
    def _():
        for k in range(adj_sems.shape[0]):
            copy_of(k).start()
        total[...] = jnp.zeros_like(total)

    for s in range(n):

        @pl.when((chunk == s) & (part == 0))
        def _():
            for k in range(left_ref.shape[0]):
                left_ref[k] = ga[s][:, k * size : (k + 1) * size]

    copy_of(step).wait()
    first = (lax.rem(me_ref[0] + n - chunk, n) * pl.num_programs(1) + part) * BLOCKS
    for r in range(BLOCKS):
        base = (first + r) * per_row
        left = left_ref[part, :, r * TILE : (r + 1) * TILE]
        for t in range(0, per_row, 2):
            right = jnp.concatenate([adj[step * BLOCKS + r, t], adj[step * BLOCKS + r, t + 1]], axis=1)
            both = jnp.dot(left, right, preferred_element_type=F32)
            total[pos_ref[base + t]] += both[:, :TILE]
            total[pos_ref[base + t + 1]] += both[:, TILE:]

    @pl.when((chunk == n - 1) & (part == pl.num_programs(1) - 1))
    def _():
        own = local_ref.shape[0]
        step = away_ref.shape[0] // PIECES
        copies = [pltpu.make_async_copy(total.at[pl.ds(0, own)], local_ref, sems.at[PIECES])]
        copies[0].start()
        for k in range(PIECES):
            stage[k * step : (k + 1) * step] = total[own + k * step : own + (k + 1) * step].astype(BF16)
            copies.append(
                pltpu.make_async_copy(
                    stage.at[pl.ds(k * step, step)], away_ref.at[pl.ds(k * step, step)], sems.at[k]
                )
            )
            copies[-1].start()
        for copy in copies:
            copy.wait()


def spmm_back(me, pos, adj, ga, own, away):
    n = len(ga)
    row_tiles, per_row = adj.shape[:2]
    rows = ga[0].shape[1]
    inner = row_tiles // n // BLOCKS
    return pl.pallas_call(
        functools.partial(spmm_back_kernel, n=n),
        grid_spec=pltpu.PrefetchScalarGridSpec(
            num_scalar_prefetch=2,
            grid=(n, inner),
            in_specs=[pl.BlockSpec(memory_space=pl.ANY)]
            + [pl.BlockSpec((TILE, rows), lambda i, k, me, pos: (0, 0))] * n,
            out_specs=[pl.BlockSpec(memory_space=pl.ANY)] * 2,
            scratch_shapes=[
                pltpu.VMEM((own + away, TILE, TILE), F32),
                pltpu.VMEM((inner, TILE, BLOCKS * TILE), BF16),
                pltpu.VMEM((away, TILE, TILE), BF16),
                pltpu.SemaphoreType.DMA((PIECES + 1,)),
                pltpu.VMEM(adj.shape, BF16),
                pltpu.SemaphoreType.DMA((n * inner,)),
            ],
        ),
        out_shape=[pltpu.HBM((own, TILE, TILE), F32), pltpu.HBM((away, TILE, TILE), BF16)],
        compiler_params=params(52),
        cost_estimate=cost(2 * row_tiles * per_row * TILE**3 * 2, 2.2e7),
        name="spmm_back",
    )(me, pos, adj, *ga)


def late_kernel(act_ref, gp_ref, ws_ref, after_ref, *pieces):
    del after_ref
    direct = lax.dot_general(gp_ref[...], ws_ref[...], NT, preferred_element_type=F32).astype(BF16)
    for j, piece in enumerate(pieces):
        piece[0] = act_ref[:, j * TILE : (j + 1) * TILE]
        piece[1] = direct[:, j * TILE : (j + 1) * TILE]


def late(act, gp, ws, after, n):
    rows, full = act.shape
    size = 256
    share = pl.BlockSpec((size, full), lambda i: (i, 0))
    return pl.pallas_call(
        late_kernel,
        grid=(rows // size,),
        in_specs=[
            share,
            share,
            pl.BlockSpec((full, full), lambda i: (0, 0)),
            pl.BlockSpec(memory_space=pl.ANY),
        ],
        out_specs=[pl.BlockSpec((2, size, TILE), lambda i: (0, i, 0))] * n,
        out_shape=[shape((2, rows, TILE), BF16)] * n,
        compiler_params=params(24),
        cost_estimate=cost(1e10, 6e6),
        name="late",
    )(act, gp, ws, after)


def finish_kernel(me_ref, ext_ref, *refs):
    pieces, (out_ref, grad_ref) = refs[:-2], refs[-2:]
    for s, piece in enumerate(pieces):

        @pl.when(pl.program_id(0) == s)
        def _():
            out_ref[...] = piece[0]
            for k in range(ext_ref.shape[0]):
                rows = slice(k * TILE, (k + 1) * TILE)
                total = piece[1, rows, :].astype(F32) + jnp.transpose(ext_ref[k])
                grad_ref[rows, :] = total.astype(BF16)


def finish(me, ext, pieces):
    n = len(pieces)
    share = pieces[0].shape[1]
    placed = pl.BlockSpec((share, TILE), lambda i, me: (lax.rem(me[0] + n - i, n), 0))
    return pl.pallas_call(
        finish_kernel,
        grid_spec=pltpu.PrefetchScalarGridSpec(
            num_scalar_prefetch=1,
            grid=(n,),
            in_specs=[
                pl.BlockSpec(
                    (share // TILE, TILE, TILE), lambda i, me: (lax.rem(me[0] + n - i, n), 0, 0)
                )
            ]
            + [pl.BlockSpec((2, share, TILE), lambda i, me: (0, 0, 0))] * n,
            out_specs=[placed, placed],
        ),
        out_shape=[shape((n * share, TILE), BF16)] * 2,
        compiler_params=params(24),
        cost_estimate=cost(1e6, 7e6),
        name="finish",
    )(me, ext, *pieces)


def scatter_kernel(ids_ref, counts_ref, val_ref, out_ref):
    groups = out_ref.shape[0] // LOW

    @pl.when(pl.program_id(0) == 0)
    def _():
        out_ref[...] = jnp.zeros_like(out_ref)

    for p in range(0, ids_ref.shape[0], 2):
        ids = masked_ids(ids_ref, counts_ref, p, 2)
        onehot = low_onehot(ids)
        values = jnp.concatenate([val_ref[p * CHUNKS + k] for k in range(2 * CHUNKS)], axis=1)
        zero = jnp.zeros_like(values)
        which = jnp.broadcast_to((ids >> LOW_BITS).astype(jnp.int16), values.shape)
        for g in range(0, groups, 2):
            pair = [jnp.where(which == jnp.int16(k), values, zero) for k in (g, g + 1)]
            both = lax.dot_general(
                onehot, jnp.concatenate(pair, axis=0), NT, preferred_element_type=F32
            )
            out_ref[g * LOW : (g + 1) * LOW, :] += both[:, :TILE]
            out_ref[(g + 1) * LOW : (g + 2) * LOW, :] += both[:, TILE:]


def scatter_rows(ids, counts, values, rows):
    peers = ids.shape[0]
    size = 8
    return pl.pallas_call(
        scatter_kernel,
        grid=(peers // size,),
        in_specs=[
            pl.BlockSpec((size, B), lambda i: (i, 0)),
            pl.BlockSpec(memory_space=pltpu.SMEM),
            pl.BlockSpec((size * CHUNKS, TILE, TILE), lambda i: (i, 0, 0)),
        ],
        out_specs=pl.BlockSpec((rows, TILE), lambda i: (0, 0)),
        out_shape=shape((rows, TILE), F32),
        compiler_params=params(40),
        cost_estimate=cost(8 * ids.size * rows * TILE, 4e6),
        name="scatter_rows",
    )(ids, counts, values)


def sum_kernel(terms_ref, after_ref, *outs):
    del after_ref
    total = jnp.sum(terms_ref[...].astype(F32), axis=0).astype(BF16)
    for j, out in enumerate(outs):
        out[...] = total[j]


def sum_terms(terms, after):
    n = terms.shape[1]
    return pl.pallas_call(
        sum_kernel,
        in_specs=[pl.BlockSpec(memory_space=pltpu.VMEM), pl.BlockSpec(memory_space=pl.ANY)],
        out_specs=[pl.BlockSpec(memory_space=pltpu.VMEM)] * n,
        out_shape=[shape(terms.shape[2:], BF16)] * n,
        compiler_params=params(16),
        cost_estimate=cost(1e9, 1e6),
        name="sum_terms",
    )(terms, after)


def spread_kernel(*refs):
    terms, out_ref = refs[:-1], refs[-1]
    total = terms[0][...].astype(F32)
    for term in terms[1:]:
        total = total + term[...].astype(F32)
    out_ref[...] = jnp.broadcast_to(total.astype(BF16)[None], out_ref.shape)


def spread_terms(terms, dom_count):
    vmem = pl.BlockSpec(memory_space=pltpu.VMEM)
    return pl.pallas_call(
        spread_kernel,
        in_specs=[vmem] * len(terms),
        out_specs=vmem,
        out_shape=shape((dom_count, *terms[0].shape), BF16),
        compiler_params=params(8),
        cost_estimate=cost(1e5, 3e5),
        name="spread_terms",
    )(*terms)


def tie_kernel(value_ref, after_ref, out_ref):
    del value_ref, after_ref, out_ref


def tie(value, after):
    anywhere = pl.BlockSpec(memory_space=pl.ANY)
    return pl.pallas_call(
        tie_kernel,
        in_specs=[anywhere, anywhere],
        out_specs=anywhere,
        out_shape=shape(value.shape, value.dtype),
        input_output_aliases={0: 0},
        compiler_params=params(8),
        name="tie",
    )(value, after)


def place_kernel(terms_ref, *outs):
    rows, width = terms_ref.shape[1:]
    n = outs[0].shape[1] // width
    for at in range(terms_ref.shape[0]):
        group, q = at // n, at % n
        per = outs[0].shape[0] // rows
        out = outs[group // per]
        first = group % per * rows
        out[first : first + rows, q * width : (q + 1) * width] = terms_ref[at].astype(F32)


def place_terms(terms, width, n):
    return pl.pallas_call(
        place_kernel,
        out_shape=[shape((width, n * width), F32)] * 2,
        compiler_params=params(8),
        cost_estimate=cost(1e5, 8e5),
        name="place_terms",
    )(terms)


def per_device(
    features, stale_features, grad_output, w_neigh, w_self, adj_tiles, tile_cols, send_idx, counts
):
    dom_count = lax.axis_size("dom")
    n = lax.axis_size("rep")
    row_count, width = features.shape
    row_tiles = row_count // TILE
    swap = functools.partial(
        lax.all_to_all, axis_name="dom", split_axis=0, concat_axis=0, tiled=True
    )
    me = lax.axis_index("rep").astype(jnp.int32).reshape(1)

    ids = send_idx[0]
    pos = tile_cols[0].reshape(-1)
    adj = adj_tiles[0]

    packed = gather_rows(ids, counts, stale_features)
    halo = swap(packed)
    own, wn, ws, pieces = prep(me, features, grad_output, w_neigh, w_self, packed, n)
    both = relative(exchange(pieces))

    agg = relative(exchange(spmm(me, pos, adj, [own, halo], n, 0, n, [])))
    grad_agg, act, grad_pre, terms = dense(me, agg, both, wn, ws, dom_count)
    grad_agg = exchange(grad_agg)
    terms = swap(terms)

    local, away = spmm_back(me, pos, adj, grad_agg, row_tiles, dom_count * CHUNKS)
    returned = swap(away)
    pieces = exchange(late(act, grad_pre, ws, away, n))
    out, grad_input = finish(me, local, pieces)
    terms = exchange(sum_terms(terms, away))

    terms = swap(tie(spread_terms(terms, dom_count), returned[0, :16]))
    grad_stale = scatter_rows(ids, counts, returned, row_count)
    grad_neigh, grad_self = place_terms(terms, width, n)
    return (out, grad_input, grad_stale, grad_neigh, grad_self)


def solution(mesh):
    in_specs = (
        P("dom", "rep"),
        P("dom", "rep"),
        P("dom", "rep"),
        P(),
        P(),
        P("dom", None, None, None, None),
        P("dom", None, None),
        P("dom", None, None),
        P("dom", None),
    )
    out_specs = (P("dom", "rep"), P("dom", "rep"), P("dom", "rep"), P("rep", None), P("rep", None))
    return jax.shard_map(
        per_device, mesh=mesh, in_specs=in_specs, out_specs=out_specs, check_vma=False
    )
```

```python
import functools

import jax
import jax.numpy as jnp
from jax import lax
from jax.experimental import pallas as pl
from jax.experimental.pallas import tpu as pltpu
from jax.sharding import PartitionSpec as P

TILE = 128
B = 384
CHUNKS = B // TILE
LOW_BITS = 9
LOW = 1 << LOW_BITS
F32 = jnp.float32
BF16 = jnp.bfloat16
NT = (((1,), (1,)), ((), ()))
TN = (((0,), (0,)), ((), ()))


def params(mib):
    return pltpu.CompilerParams(vmem_limit_bytes=mib * 1024 * 1024)


def cost(flops, nbytes, trans=0):
    return pl.CostEstimate(flops=int(flops), bytes_accessed=int(nbytes), transcendentals=int(trans))


def shape(dims, dtype):
    return jax.ShapeDtypeStruct(dims, dtype)


def turned(block):
    return jnp.transpose(block.astype(F32))


def masked_ids(ids_ref, counts_ref, first, peers):
    base = pl.program_id(0) * ids_ref.shape[0]
    slot = lax.broadcasted_iota(jnp.int32, (1, ids_ref.shape[1]), 1)
    rows = [
        jnp.where(slot < counts_ref[0, base + p], ids_ref[p : p + 1, :], -1)
        for p in range(first, first + peers)
    ]
    return jnp.concatenate(rows, axis=1)


def low_onehot(ids):
    spot = lax.broadcasted_iota(jnp.int32, (LOW, ids.shape[1]), 0).astype(jnp.int16)
    low = jnp.broadcast_to((ids & (LOW - 1)).astype(jnp.int16), spot.shape)
    return jnp.where(spot == low, jnp.ones(spot.shape, BF16), jnp.zeros(spot.shape, BF16))


def in_group(ids, g):
    return (ids >= g * LOW) & (ids < (g + 1) * LOW)


def gather_kernel(ids_ref, counts_ref, table_ref, out_ref, flipped):
    groups = table_ref.shape[0] // LOW

    @pl.when(pl.program_id(0) == 0)
    def _():
        for g in range(groups):
            for k in range(LOW // TILE):
                block = table_ref[g * LOW + k * TILE : g * LOW + (k + 1) * TILE, :]
                flipped[g * TILE : (g + 1) * TILE, k * TILE : (k + 1) * TILE] = turned(block).astype(
                    BF16
                )

    for p in range(0, ids_ref.shape[0], 2):
        ids = masked_ids(ids_ref, counts_ref, p, 2)
        found = jnp.dot(flipped[...], low_onehot(ids), preferred_element_type=F32)
        total = jnp.zeros((TILE, ids.shape[1]), F32)
        for g in range(groups):
            total = jnp.where(in_group(ids, g), found[g * TILE : (g + 1) * TILE, :], total)
        total = total.astype(BF16)
        for k in range(2 * CHUNKS):
            out_ref[p * CHUNKS + k] = total[:, k * TILE : (k + 1) * TILE]


def gather_rows(ids, counts, table):
    peers = ids.shape[0]
    size = 8
    rows, cols = table.shape
    return pl.pallas_call(
        gather_kernel,
        grid=(peers // size,),
        in_specs=[
            pl.BlockSpec((size, B), lambda i: (i, 0)),
            pl.BlockSpec(memory_space=pltpu.SMEM),
            pl.BlockSpec((rows, cols), lambda i: (0, 0)),
        ],
        out_specs=pl.BlockSpec((size * CHUNKS, TILE, TILE), lambda i: (i, 0, 0)),
        out_shape=shape((peers * CHUNKS, TILE, TILE), BF16),
        scratch_shapes=[pltpu.VMEM((rows // LOW * TILE, LOW), BF16)],
        compiler_params=params(56),
        cost_estimate=cost(2 * ids.size * rows * cols, 4e6),
        name="gather_rows",
    )(ids, counts, table)


def exchange(pieces):
    n = len(pieces)
    return [pieces[0]] + [
        lax.ppermute(pieces[s], "rep", [(i, (i + s) % n) for i in range(n)]) for s in range(1, n)
    ]


def relative(received):
    n = len(received)
    return [received[(n - j) % n] for j in range(n)]


def prep_kernel(me_ref, feat_ref, up_ref, wn_ref, ws_ref, after_ref, own_ref, wn_out, ws_out, *pieces):
    del after_ref
    step = pl.program_id(0)
    n = len(pieces)
    for k in range(own_ref.shape[0]):
        own_ref[k] = turned(feat_ref[k * TILE : (k + 1) * TILE, :]).astype(BF16)
    for j, piece in enumerate(pieces):
        column = pl.multiple_of(lax.rem(me_ref[0] + j, n) * TILE, TILE)
        wn_out[:, j * TILE : (j + 1) * TILE] = wn_ref[:, pl.ds(column, TILE)]
        ws_out[:, j * TILE : (j + 1) * TILE] = ws_ref[:, pl.ds(column, TILE)]

        @pl.when(step == j)
        def _():
            piece[0] = feat_ref[...]
            piece[1] = up_ref[...]


def prep(me, features, upstream, wn, ws, after, n):
    rows, width = features.shape
    share = rows // n
    full = wn.shape[0]
    chunk = pl.BlockSpec((share, width), lambda i, me: (lax.rem(me[0] + i, n), 0))
    weight = pl.BlockSpec((width, full), lambda i, me: (lax.rem(me[0] + i, n), 0))
    placed = pl.BlockSpec((width, full), lambda i, me: (i, 0))
    own, wn, ws, *pieces = pl.pallas_call(
        prep_kernel,
        grid_spec=pltpu.PrefetchScalarGridSpec(
            num_scalar_prefetch=1,
            grid=(n,),
            in_specs=[chunk, chunk, weight, weight, pl.BlockSpec(memory_space=pl.ANY)],
            out_specs=[
                pl.BlockSpec(
                    (share // TILE, TILE, TILE), lambda i, me: (lax.rem(me[0] + i, n), 0, 0)
                ),
                placed,
                placed,
            ]
            + [pl.BlockSpec((2, share, width), lambda i, me: (0, 0, 0))] * n,
        ),
        out_shape=[
            pltpu.HBM((rows // TILE, TILE, TILE), BF16),
            pltpu.HBM((full, full), BF16),
            pltpu.HBM((full, full), BF16),
        ]
        + [shape((2, share, width), BF16)] * n,
        compiler_params=params(56),
        cost_estimate=cost(1e10, 6e6),
        name="prep",
    )(me, features, upstream, wn, ws, after)
    return own, wn, ws, pieces


BLOCKS = 3
AHEAD = 4


def adj_copies(adj_ref, held, sems, inner, chunk_of):
    def copy(step):
        first = (chunk_of(step // inner) * inner + lax.rem(step, inner)) * BLOCKS
        return pltpu.make_async_copy(
            adj_ref.at[pl.ds(first, BLOCKS)], held.at[pl.ds(step * BLOCKS, BLOCKS)], sems.at[step]
        )

    return copy


def spmm_kernel(me_ref, pos_ref, *refs, n, start_chunk, extras):
    adj_ref, parts, outs, (ext, sems, adj, adj_sems) = (
        refs[0],
        refs[1 : 3],
        refs[3 + extras : -4],
        refs[-4:],
    )
    chunk, part = pl.program_id(0), pl.program_id(1)
    inner = adj_sems.shape[0] // len(outs)
    step = chunk * inner + part
    per_row = adj.shape[1]
    copy_of = adj_copies(
        adj_ref, adj, adj_sems, inner, lambda c: lax.rem(me_ref[0] + start_chunk + c, n)
    )

    @pl.when((chunk == 0) & (part == 0))
    def _():
        copies, start, at = [], 0, 0
        for source in parts:
            size = source.shape[0] // 4
            for k in range(4):
                copies.append(
                    pltpu.make_async_copy(
                        source.at[pl.ds(k * size, size)], ext.at[pl.ds(start, size)], sems.at[at]
                    )
                )
                start, at = start + size, at + 1
        for copy in copies:
            copy.start()
        copy_of(0).start()
        for copy in copies:
            copy.wait()
        for k in range(1, AHEAD):
            copy_of(k).start()

    @pl.when(step + AHEAD < adj_sems.shape[0])
    def _():
        copy_of(step + AHEAD).start()

    copy_of(step).wait()
    first = (lax.rem(me_ref[0] + start_chunk + chunk, n) * inner + part) * BLOCKS
    done = []
    for r in range(BLOCKS):
        base = (first + r) * per_row
        total = None
        for t in range(0, per_row, 2):
            left = jnp.concatenate([adj[step * BLOCKS + r, t], adj[step * BLOCKS + r, t + 1]], axis=1)
            right = jnp.concatenate([ext[pos_ref[base + t]], ext[pos_ref[base + t + 1]]], axis=1)
            term = lax.dot_general(left, right, NT, preferred_element_type=F32)
            total = term if total is None else total + term
        done.append(total.astype(BF16))
    done = jnp.concatenate(done, axis=0)
    size = BLOCKS * TILE
    place = pl.ds(pl.multiple_of(part * size, size), size)
    for j, out in enumerate(outs):

        @pl.when(chunk == j)
        def _():
            out[place, :] = done


def spmm(me, pos, adj, parts, n, start_chunk, count, after):
    row_tiles, per_row = adj.shape[:2]
    inner = row_tiles // n // BLOCKS
    share = row_tiles // n * TILE
    col_tiles = sum(p.shape[0] for p in parts)
    return pl.pallas_call(
        functools.partial(spmm_kernel, n=n, start_chunk=start_chunk, extras=len(after)),
        grid_spec=pltpu.PrefetchScalarGridSpec(
            num_scalar_prefetch=2,
            grid=(count, inner),
            in_specs=[pl.BlockSpec(memory_space=pl.ANY)] * (1 + len(parts) + len(after)),
            out_specs=[pl.BlockSpec((share, TILE), lambda i, k, me, pos: (0, 0))] * count,
            scratch_shapes=[
                pltpu.VMEM((col_tiles, TILE, TILE), BF16),
                pltpu.SemaphoreType.DMA((4 * len(parts),)),
                pltpu.VMEM((count * inner * BLOCKS, *adj.shape[1:]), BF16),
                pltpu.SemaphoreType.DMA((count * inner,)),
            ],
        ),
        out_shape=[shape((share, TILE), BF16)] * count,
        compiler_params=params(56),
        cost_estimate=cost(2 * count * share * per_row * TILE**2 * 8, 1e7),
        name="spmm",
    )(me, pos, adj, *parts, *after)


def joined(refs):
    return jnp.concatenate([ref[...] for ref in refs], axis=1)


def dense_kernel(me_ref, *refs, n):
    agg, both, (wn_ref, ws_ref), rest = refs[:n], refs[n : 2 * n], refs[2 * n : 2 * n + 2], refs[2 * n + 2 :]
    ga, (act_ref, gp_ref, terms_ref, total) = rest[:n], rest[n:]
    step = pl.program_id(0)
    wn = wn_ref[...]
    feat = [ref[0] for ref in both]
    v = jnp.dot(joined(agg), wn, preferred_element_type=F32) + jnp.dot(
        jnp.concatenate(feat, axis=1), ws_ref[...], preferred_element_type=F32
    )
    root = 0.7978845608028654
    square = v * v
    t = jnp.tanh(root * v * (1.0 + 0.044715 * square))
    half = 0.5 * (1.0 + t)
    slope = half + 0.5 * v * (1.0 - t * t) * (root * (1.0 + 0.134145 * square))
    gp = (joined([ref.at[1] for ref in both]).astype(F32) * slope).astype(BF16)
    act_ref[...] = (v * half).astype(BF16)
    gp_ref[...] = gp
    back = lax.dot_general(wn, gp, NT, preferred_element_type=F32).astype(BF16)
    width = back.shape[0] // n
    for q in range(n):
        ga[q][...] = back[q * width : (q + 1) * width, :]

    terms = [
        lax.dot_general(left, gp, TN, preferred_element_type=F32)
        for j in range(n)
        for left in (agg[j][...], feat[j])
    ]

    @pl.when(step == 0)
    def _():
        for k, term in enumerate(terms):
            total[k] = term

    @pl.when(step > 0)
    def _():
        for k, term in enumerate(terms):
            total[k] += term

    @pl.when(step == pl.num_programs(0) - 1)
    def _():
        rows = terms_ref.shape[2]
        for j in range(n):
            for kind in range(2):
                term = total[2 * j + kind].astype(BF16)
                for i in range(n):
                    q = lax.rem(me_ref[0] + i, n)
                    for k in range(width // rows):
                        at = (kind * (width // rows) + k) * n + q
                        terms_ref[at, j] = term[k * rows : (k + 1) * rows, i * width : (i + 1) * width]


def dense(me, agg, both, wn, ws, dom_count):
    n = len(agg)
    rows, width = agg[0].shape
    full = n * width
    size = 256
    piece = (dom_count, n, 2 * width * n // dom_count, width)
    weight = pl.BlockSpec((full, full), lambda i, me: (0, 0))
    whole = pl.BlockSpec((size, full), lambda i, me: (i, 0))
    results = pl.pallas_call(
        functools.partial(dense_kernel, n=n),
        grid_spec=pltpu.PrefetchScalarGridSpec(
            num_scalar_prefetch=1,
            grid=(rows // size,),
            in_specs=[pl.BlockSpec((size, width), lambda i, me: (i, 0))] * n
            + [pl.BlockSpec((2, size, width), lambda i, me: (0, i, 0))] * n
            + [weight, weight],
            out_specs=[pl.BlockSpec((width, size), lambda i, me: (0, i))] * n
            + [whole, whole, pl.BlockSpec(piece, lambda i, me: (0, 0, 0, 0))],
            scratch_shapes=[pltpu.VMEM((2 * n, width, full), F32)],
        ),
        out_shape=[shape((width, rows), BF16)] * n
        + [pltpu.HBM((rows, full), BF16)] * 2
        + [pltpu.HBM(piece, BF16)],
        compiler_params=params(24),
        cost_estimate=cost(10 * rows * full * full, 9e6, rows * full),
        name="dense",
    )(me, *agg, *both, wn, ws)
    return results[:n], *results[n:]


PIECES = 6


def spmm_back_kernel(me_ref, pos_ref, *refs, n):
    adj_ref, ga = refs[0], refs[1 : 1 + n]
    local_ref, away_ref, total, left_ref, stage, sems, adj, adj_sems = refs[1 + n :]
    chunk, part = pl.program_id(0), pl.program_id(1)
    inner = adj_sems.shape[0] // n
    step = chunk * inner + part
    per_row = adj.shape[1]
    copy_of = adj_copies(adj_ref, adj, adj_sems, inner, lambda c: lax.rem(me_ref[0] + n - c, n))
    size = BLOCKS * TILE

    @pl.when((chunk == 0) & (part == 0))
    def _():
        copy_of(0).start()
        copy_of(1).start()
        total[...] = jnp.zeros_like(total)
        for k in range(2, AHEAD):
            copy_of(k).start()

    for s in range(n):

        @pl.when((chunk == s) & (part == 0))
        def _():
            for k in range(left_ref.shape[0]):
                left_ref[k] = ga[s][:, k * size : (k + 1) * size]

    @pl.when(step + AHEAD < adj_sems.shape[0])
    def _():
        copy_of(step + AHEAD).start()

    copy_of(step).wait()
    first = (lax.rem(me_ref[0] + n - chunk, n) * pl.num_programs(1) + part) * BLOCKS
    for r in range(BLOCKS):
        base = (first + r) * per_row
        left = left_ref[part, :, r * TILE : (r + 1) * TILE]
        for t in range(0, per_row, 2):
            right = jnp.concatenate([adj[step * BLOCKS + r, t], adj[step * BLOCKS + r, t + 1]], axis=1)
            both = jnp.dot(left, right, preferred_element_type=F32)
            total[pos_ref[base + t]] += both[:, :TILE]
            total[pos_ref[base + t + 1]] += both[:, TILE:]

    @pl.when((chunk == n - 1) & (part == pl.num_programs(1) - 1))
    def _():
        own = local_ref.shape[0]
        step = away_ref.shape[0] // PIECES
        copies = [pltpu.make_async_copy(total.at[pl.ds(0, own)], local_ref, sems.at[PIECES])]
        copies[0].start()
        for k in range(PIECES):
            stage[k * step : (k + 1) * step] = total[own + k * step : own + (k + 1) * step].astype(BF16)
            copies.append(
                pltpu.make_async_copy(
                    stage.at[pl.ds(k * step, step)], away_ref.at[pl.ds(k * step, step)], sems.at[k]
                )
            )
            copies[-1].start()
        for copy in copies:
            copy.wait()


def spmm_back(me, pos, adj, ga, own, away):
    n = len(ga)
    row_tiles, per_row = adj.shape[:2]
    rows = ga[0].shape[1]
    inner = row_tiles // n // BLOCKS
    return pl.pallas_call(
        functools.partial(spmm_back_kernel, n=n),
        grid_spec=pltpu.PrefetchScalarGridSpec(
            num_scalar_prefetch=2,
            grid=(n, inner),
            in_specs=[pl.BlockSpec(memory_space=pl.ANY)]
            + [pl.BlockSpec((TILE, rows), lambda i, k, me, pos: (0, 0))] * n,
            out_specs=[pl.BlockSpec(memory_space=pl.ANY)] * 2,
            scratch_shapes=[
                pltpu.VMEM((own + away, TILE, TILE), F32),
                pltpu.VMEM((inner, TILE, BLOCKS * TILE), BF16),
                pltpu.VMEM((away, TILE, TILE), BF16),
                pltpu.SemaphoreType.DMA((PIECES + 1,)),
                pltpu.VMEM(adj.shape, BF16),
                pltpu.SemaphoreType.DMA((n * inner,)),
            ],
        ),
        out_shape=[pltpu.HBM((own, TILE, TILE), F32), pltpu.HBM((away, TILE, TILE), BF16)],
        compiler_params=params(52),
        cost_estimate=cost(2 * row_tiles * per_row * TILE**3 * 2, 2.2e7),
        name="spmm_back",
    )(me, pos, adj, *ga)


def late_kernel(act_ref, gp_ref, ws_ref, after_ref, *pieces):
    del after_ref
    direct = lax.dot_general(gp_ref[...], ws_ref[...], NT, preferred_element_type=F32).astype(BF16)
    for j, piece in enumerate(pieces):
        piece[0] = act_ref[:, j * TILE : (j + 1) * TILE]
        piece[1] = direct[:, j * TILE : (j + 1) * TILE]


def late(act, gp, ws, after, n):
    rows, full = act.shape
    size = 256
    share = pl.BlockSpec((size, full), lambda i: (i, 0))
    return pl.pallas_call(
        late_kernel,
        grid=(rows // size,),
        in_specs=[
            share,
            share,
            pl.BlockSpec((full, full), lambda i: (0, 0)),
            pl.BlockSpec(memory_space=pl.ANY),
        ],
        out_specs=[pl.BlockSpec((2, size, TILE), lambda i: (0, i, 0))] * n,
        out_shape=[shape((2, rows, TILE), BF16)] * n,
        compiler_params=params(24),
        cost_estimate=cost(1e10, 6e6),
        name="late",
    )(act, gp, ws, after)


def finish_kernel(me_ref, ext_ref, *refs):
    pieces, (out_ref, grad_ref) = refs[:-2], refs[-2:]
    for s, piece in enumerate(pieces):

        @pl.when(pl.program_id(0) == s)
        def _():
            out_ref[...] = piece[0]
            for k in range(ext_ref.shape[0]):
                rows = slice(k * TILE, (k + 1) * TILE)
                total = piece[1, rows, :].astype(F32) + jnp.transpose(ext_ref[k])
                grad_ref[rows, :] = total.astype(BF16)


def finish(me, ext, pieces):
    n = len(pieces)
    share = pieces[0].shape[1]
    placed = pl.BlockSpec((share, TILE), lambda i, me: (lax.rem(me[0] + n - i, n), 0))
    return pl.pallas_call(
        finish_kernel,
        grid_spec=pltpu.PrefetchScalarGridSpec(
            num_scalar_prefetch=1,
            grid=(n,),
            in_specs=[
                pl.BlockSpec(
                    (share // TILE, TILE, TILE), lambda i, me: (lax.rem(me[0] + n - i, n), 0, 0)
                )
            ]
            + [pl.BlockSpec((2, share, TILE), lambda i, me: (0, 0, 0))] * n,
            out_specs=[placed, placed],
        ),
        out_shape=[shape((n * share, TILE), BF16)] * 2,
        compiler_params=params(24),
        cost_estimate=cost(1e6, 7e6),
        name="finish",
    )(me, ext, *pieces)


def scatter_kernel(ids_ref, counts_ref, val_ref, out_ref):
    groups = out_ref.shape[0] // LOW

    @pl.when(pl.program_id(0) == 0)
    def _():
        out_ref[...] = jnp.zeros_like(out_ref)

    for p in range(0, ids_ref.shape[0], 2):
        ids = masked_ids(ids_ref, counts_ref, p, 2)
        onehot = low_onehot(ids)
        values = jnp.concatenate([val_ref[p * CHUNKS + k] for k in range(2 * CHUNKS)], axis=1)
        zero = jnp.zeros_like(values)
        which = jnp.broadcast_to((ids >> LOW_BITS).astype(jnp.int16), values.shape)
        for g in range(0, groups, 2):
            pair = [jnp.where(which == jnp.int16(k), values, zero) for k in (g, g + 1)]
            both = lax.dot_general(
                onehot, jnp.concatenate(pair, axis=0), NT, preferred_element_type=F32
            )
            out_ref[g * LOW : (g + 1) * LOW, :] += both[:, :TILE]
            out_ref[(g + 1) * LOW : (g + 2) * LOW, :] += both[:, TILE:]


def scatter_rows(ids, counts, values, rows):
    peers = ids.shape[0]
    size = 8
    return pl.pallas_call(
        scatter_kernel,
        grid=(peers // size,),
        in_specs=[
            pl.BlockSpec((size, B), lambda i: (i, 0)),
            pl.BlockSpec(memory_space=pltpu.SMEM),
            pl.BlockSpec((size * CHUNKS, TILE, TILE), lambda i: (i, 0, 0)),
        ],
        out_specs=pl.BlockSpec((rows, TILE), lambda i: (0, 0)),
        out_shape=shape((rows, TILE), F32),
        compiler_params=params(40),
        cost_estimate=cost(8 * ids.size * rows * TILE, 4e6),
        name="scatter_rows",
    )(ids, counts, values)


def sum_kernel(terms_ref, after_ref, *outs):
    del after_ref
    total = jnp.sum(terms_ref[...].astype(F32), axis=0).astype(BF16)
    for j, out in enumerate(outs):
        out[...] = total[j]


def sum_terms(terms, after):
    n = terms.shape[1]
    return pl.pallas_call(
        sum_kernel,
        in_specs=[pl.BlockSpec(memory_space=pltpu.VMEM), pl.BlockSpec(memory_space=pl.ANY)],
        out_specs=[pl.BlockSpec(memory_space=pltpu.VMEM)] * n,
        out_shape=[shape(terms.shape[2:], BF16)] * n,
        compiler_params=params(16),
        cost_estimate=cost(1e9, 1e6),
        name="sum_terms",
    )(terms, after)


def spread_kernel(*refs):
    terms, out_ref = refs[:-1], refs[-1]
    total = terms[0][...].astype(F32)
    for term in terms[1:]:
        total = total + term[...].astype(F32)
    out_ref[...] = jnp.broadcast_to(total.astype(BF16)[None], out_ref.shape)


def spread_terms(terms, dom_count):
    vmem = pl.BlockSpec(memory_space=pltpu.VMEM)
    return pl.pallas_call(
        spread_kernel,
        in_specs=[vmem] * len(terms),
        out_specs=vmem,
        out_shape=shape((dom_count, *terms[0].shape), BF16),
        compiler_params=params(8),
        cost_estimate=cost(1e5, 3e5),
        name="spread_terms",
    )(*terms)


def tie_kernel(value_ref, after_ref, out_ref):
    del value_ref, after_ref, out_ref


def tie(value, after):
    anywhere = pl.BlockSpec(memory_space=pl.ANY)
    return pl.pallas_call(
        tie_kernel,
        in_specs=[anywhere, anywhere],
        out_specs=anywhere,
        out_shape=shape(value.shape, value.dtype),
        input_output_aliases={0: 0},
        compiler_params=params(8),
        name="tie",
    )(value, after)


def place_kernel(terms_ref, *outs):
    rows, width = terms_ref.shape[1:]
    n = outs[0].shape[1] // width
    for at in range(terms_ref.shape[0]):
        group, q = at // n, at % n
        per = outs[0].shape[0] // rows
        out = outs[group // per]
        first = group % per * rows
        out[first : first + rows, q * width : (q + 1) * width] = terms_ref[at].astype(F32)


def place_terms(terms, width, n):
    return pl.pallas_call(
        place_kernel,
        out_shape=[shape((width, n * width), F32)] * 2,
        compiler_params=params(8),
        cost_estimate=cost(1e5, 8e5),
        name="place_terms",
    )(terms)


def per_device(
    features, stale_features, grad_output, w_neigh, w_self, adj_tiles, tile_cols, send_idx, counts
):
    dom_count = lax.axis_size("dom")
    n = lax.axis_size("rep")
    row_count, width = features.shape
    row_tiles = row_count // TILE
    swap = functools.partial(
        lax.all_to_all, axis_name="dom", split_axis=0, concat_axis=0, tiled=True
    )
    me = lax.axis_index("rep").astype(jnp.int32).reshape(1)

    ids = send_idx[0]
    pos = tile_cols[0].reshape(-1)
    adj = adj_tiles[0]

    packed = gather_rows(ids, counts, stale_features)
    halo = swap(packed)
    own, wn, ws, pieces = prep(me, features, grad_output, w_neigh, w_self, packed, n)
    both = relative(exchange(pieces))

    agg = relative(exchange(spmm(me, pos, adj, [own, halo], n, 0, n, [])))
    grad_agg, act, grad_pre, terms = dense(me, agg, both, wn, ws, dom_count)
    grad_agg = exchange(grad_agg)
    terms = swap(terms)

    local, away = spmm_back(me, pos, adj, grad_agg, row_tiles, dom_count * CHUNKS)
    returned = swap(away)
    pieces = exchange(late(act, grad_pre, ws, away, n))
    out, grad_input = finish(me, local, pieces)
    terms = exchange(sum_terms(terms, away))

    terms = swap(tie(spread_terms(terms, dom_count), returned))
    grad_stale = scatter_rows(ids, counts, returned, row_count)
    grad_neigh, grad_self = place_terms(terms, width, n)
    return (out, grad_input, grad_stale, grad_neigh, grad_self)


def solution(mesh):
    in_specs = (
        P("dom", "rep"),
        P("dom", "rep"),
        P("dom", "rep"),
        P(),
        P(),
        P("dom", None, None, None, None),
        P("dom", None, None),
        P("dom", None, None),
        P("dom", None),
    )
    out_specs = (P("dom", "rep"), P("dom", "rep"), P("dom", "rep"), P("rep", None), P("rep", None))
    return jax.shard_map(
        per_device, mesh=mesh, in_specs=in_specs, out_specs=out_specs, check_vma=False
    )
```

```python
import functools

import jax
import jax.numpy as jnp
from jax import lax
from jax.experimental import pallas as pl
from jax.experimental.pallas import tpu as pltpu
from jax.sharding import PartitionSpec as P

TILE = 128
B = 384
CHUNKS = B // TILE
LOW_BITS = 9
LOW = 1 << LOW_BITS
F32 = jnp.float32
BF16 = jnp.bfloat16
NT = (((1,), (1,)), ((), ()))
TN = (((0,), (0,)), ((), ()))


def params(mib):
    return pltpu.CompilerParams(vmem_limit_bytes=mib * 1024 * 1024)


def cost(flops, nbytes, trans=0):
    return pl.CostEstimate(flops=int(flops), bytes_accessed=int(nbytes), transcendentals=int(trans))


def shape(dims, dtype):
    return jax.ShapeDtypeStruct(dims, dtype)


def turned(block):
    return jnp.transpose(block.astype(F32))


def masked_ids(ids_ref, counts_ref, first, peers):
    base = pl.program_id(0) * ids_ref.shape[0]
    slot = lax.broadcasted_iota(jnp.int32, (1, ids_ref.shape[1]), 1)
    rows = [
        jnp.where(slot < counts_ref[0, base + p], ids_ref[p : p + 1, :], -1)
        for p in range(first, first + peers)
    ]
    return jnp.concatenate(rows, axis=1)


def low_onehot(ids):
    spot = lax.broadcasted_iota(jnp.int32, (LOW, ids.shape[1]), 0).astype(jnp.int16)
    low = jnp.broadcast_to((ids & (LOW - 1)).astype(jnp.int16), spot.shape)
    return jnp.where(spot == low, jnp.ones(spot.shape, BF16), jnp.zeros(spot.shape, BF16))


def in_group(ids, g):
    return (ids >= g * LOW) & (ids < (g + 1) * LOW)


def gather_kernel(ids_ref, counts_ref, table_ref, out_ref, flipped):
    groups = table_ref.shape[0] // LOW

    @pl.when(pl.program_id(0) == 0)
    def _():
        for g in range(groups):
            for k in range(LOW // TILE):
                block = table_ref[g * LOW + k * TILE : g * LOW + (k + 1) * TILE, :]
                flipped[g * TILE : (g + 1) * TILE, k * TILE : (k + 1) * TILE] = turned(block).astype(
                    BF16
                )

    for p in range(0, ids_ref.shape[0], 2):
        ids = masked_ids(ids_ref, counts_ref, p, 2)
        found = jnp.dot(flipped[...], low_onehot(ids), preferred_element_type=F32)
        total = jnp.zeros((TILE, ids.shape[1]), F32)
        for g in range(groups):
            total = jnp.where(in_group(ids, g), found[g * TILE : (g + 1) * TILE, :], total)
        total = total.astype(BF16)
        for k in range(2 * CHUNKS):
            out_ref[p * CHUNKS + k] = total[:, k * TILE : (k + 1) * TILE]


def gather_rows(ids, counts, table):
    peers = ids.shape[0]
    size = 8
    rows, cols = table.shape
    return pl.pallas_call(
        gather_kernel,
        grid=(peers // size,),
        in_specs=[
            pl.BlockSpec((size, B), lambda i: (i, 0)),
            pl.BlockSpec(memory_space=pltpu.SMEM),
            pl.BlockSpec((rows, cols), lambda i: (0, 0)),
        ],
        out_specs=pl.BlockSpec((size * CHUNKS, TILE, TILE), lambda i: (i, 0, 0)),
        out_shape=shape((peers * CHUNKS, TILE, TILE), BF16),
        scratch_shapes=[pltpu.VMEM((rows // LOW * TILE, LOW), BF16)],
        compiler_params=params(56),
        cost_estimate=cost(2 * ids.size * rows * cols, 4e6),
        name="gather_rows",
    )(ids, counts, table)


def exchange(pieces):
    n = len(pieces)
    return [pieces[0]] + [
        lax.ppermute(pieces[s], "rep", [(i, (i + s) % n) for i in range(n)]) for s in range(1, n)
    ]


def relative(received):
    n = len(received)
    return [received[(n - j) % n] for j in range(n)]


def prep_kernel(me_ref, feat_ref, up_ref, wn_ref, ws_ref, after_ref, own_ref, wn_out, ws_out, *pieces):
    del after_ref
    step = pl.program_id(0)
    n = len(pieces)
    for k in range(own_ref.shape[0]):
        own_ref[k] = turned(feat_ref[k * TILE : (k + 1) * TILE, :]).astype(BF16)
    for j, piece in enumerate(pieces):
        column = pl.multiple_of(lax.rem(me_ref[0] + j, n) * TILE, TILE)
        wn_out[:, j * TILE : (j + 1) * TILE] = wn_ref[:, pl.ds(column, TILE)]
        ws_out[:, j * TILE : (j + 1) * TILE] = ws_ref[:, pl.ds(column, TILE)]

        @pl.when(step == j)
        def _():
            piece[0] = feat_ref[...]
            piece[1] = up_ref[...]


def prep(me, features, upstream, wn, ws, after, n):
    rows, width = features.shape
    share = rows // n
    full = wn.shape[0]
    chunk = pl.BlockSpec((share, width), lambda i, me: (lax.rem(me[0] + i, n), 0))
    weight = pl.BlockSpec((width, full), lambda i, me: (lax.rem(me[0] + i, n), 0))
    placed = pl.BlockSpec((width, full), lambda i, me: (i, 0))
    own, wn, ws, *pieces = pl.pallas_call(
        prep_kernel,
        grid_spec=pltpu.PrefetchScalarGridSpec(
            num_scalar_prefetch=1,
            grid=(n,),
            in_specs=[chunk, chunk, weight, weight, pl.BlockSpec(memory_space=pl.ANY)],
            out_specs=[
                pl.BlockSpec(
                    (share // TILE, TILE, TILE), lambda i, me: (lax.rem(me[0] + i, n), 0, 0)
                ),
                placed,
                placed,
            ]
            + [pl.BlockSpec((2, share, width), lambda i, me: (0, 0, 0))] * n,
        ),
        out_shape=[
            pltpu.HBM((rows // TILE, TILE, TILE), BF16),
            pltpu.HBM((full, full), BF16),
            pltpu.HBM((full, full), BF16),
        ]
        + [shape((2, share, width), BF16)] * n,
        compiler_params=params(56),
        cost_estimate=cost(1e10, 6e6),
        name="prep",
    )(me, features, upstream, wn, ws, after)
    return own, wn, ws, pieces


BLOCKS = 3


def adj_copies(adj_ref, held, sems, inner, chunk_of):
    def copy(step):
        first = (chunk_of(step // inner) * inner + lax.rem(step, inner)) * BLOCKS
        return pltpu.make_async_copy(
            adj_ref.at[pl.ds(first, BLOCKS)], held.at[pl.ds(step * BLOCKS, BLOCKS)], sems.at[step]
        )

    return copy


def spmm_kernel(me_ref, pos_ref, *refs, n, start_chunk, extras):
    adj_ref, parts, outs, (ext, sems, adj, adj_sems) = (
        refs[0],
        refs[1 : 3],
        refs[3 + extras : -4],
        refs[-4:],
    )
    chunk, part = pl.program_id(0), pl.program_id(1)
    inner = adj_sems.shape[0] // len(outs)
    step = chunk * inner + part
    per_row = adj.shape[1]
    copy_of = adj_copies(
        adj_ref, adj, adj_sems, inner, lambda c: lax.rem(me_ref[0] + start_chunk + c, n)
    )

    @pl.when((chunk == 0) & (part == 0))
    def _():
        copies, start, at = [], 0, 0
        for source in parts:
            size = source.shape[0] // 4
            for k in range(4):
                copies.append(
                    pltpu.make_async_copy(
                        source.at[pl.ds(k * size, size)], ext.at[pl.ds(start, size)], sems.at[at]
                    )
                )
                start, at = start + size, at + 1
        for copy in copies:
            copy.start()
        copy_of(0).start()
        for copy in copies:
            copy.wait()
        for k in range(1, adj_sems.shape[0]):
            copy_of(k).start()

    copy_of(step).wait()
    first = (lax.rem(me_ref[0] + start_chunk + chunk, n) * inner + part) * BLOCKS
    done = []
    for r in range(BLOCKS):
        base = (first + r) * per_row
        total = None
        for t in range(0, per_row, 2):
            left = jnp.concatenate([adj[step * BLOCKS + r, t], adj[step * BLOCKS + r, t + 1]], axis=1)
            right = jnp.concatenate([ext[pos_ref[base + t]], ext[pos_ref[base + t + 1]]], axis=1)
            term = lax.dot_general(left, right, NT, preferred_element_type=F32)
            total = term if total is None else total + term
        done.append(total.astype(BF16))
    done = jnp.concatenate(done, axis=0)
    size = BLOCKS * TILE
    place = pl.ds(pl.multiple_of(part * size, size), size)
    for j, out in enumerate(outs):

        @pl.when(chunk == j)
        def _():
            out[place, :] = done


def spmm(me, pos, adj, parts, n, start_chunk, count, after):
    row_tiles, per_row = adj.shape[:2]
    inner = row_tiles // n // BLOCKS
    share = row_tiles // n * TILE
    col_tiles = sum(p.shape[0] for p in parts)
    return pl.pallas_call(
        functools.partial(spmm_kernel, n=n, start_chunk=start_chunk, extras=len(after)),
        grid_spec=pltpu.PrefetchScalarGridSpec(
            num_scalar_prefetch=2,
            grid=(count, inner),
            in_specs=[pl.BlockSpec(memory_space=pl.ANY)] * (1 + len(parts) + len(after)),
            out_specs=[pl.BlockSpec((share, TILE), lambda i, k, me, pos: (0, 0))] * count,
            scratch_shapes=[
                pltpu.VMEM((col_tiles, TILE, TILE), BF16),
                pltpu.SemaphoreType.DMA((4 * len(parts),)),
                pltpu.VMEM((count * inner * BLOCKS, *adj.shape[1:]), BF16),
                pltpu.SemaphoreType.DMA((count * inner,)),
            ],
        ),
        out_shape=[shape((share, TILE), BF16)] * count,
        compiler_params=params(56),
        cost_estimate=cost(2 * count * share * per_row * TILE**2 * 8, 1e7),
        name="spmm",
    )(me, pos, adj, *parts, *after)


def joined(refs):
    return jnp.concatenate([ref[...] for ref in refs], axis=1)


def dense_kernel(me_ref, *refs, n):
    agg, both, (wn_ref, ws_ref), rest = refs[:n], refs[n : 2 * n], refs[2 * n : 2 * n + 2], refs[2 * n + 2 :]
    ga, (act_ref, gp_ref, terms_ref, total) = rest[:n], rest[n:]
    step = pl.program_id(0)
    wn = wn_ref[...]
    feat = [ref[0] for ref in both]
    v = jnp.dot(joined(agg), wn, preferred_element_type=F32) + jnp.dot(
        jnp.concatenate(feat, axis=1), ws_ref[...], preferred_element_type=F32
    )
    root = 0.7978845608028654
    square = v * v
    t = jnp.tanh(root * v * (1.0 + 0.044715 * square))
    half = 0.5 * (1.0 + t)
    slope = half + 0.5 * v * (1.0 - t * t) * (root * (1.0 + 0.134145 * square))
    gp = (joined([ref.at[1] for ref in both]).astype(F32) * slope).astype(BF16)
    act_ref[...] = (v * half).astype(BF16)
    gp_ref[...] = gp
    back = lax.dot_general(wn, gp, NT, preferred_element_type=F32).astype(BF16)
    width = back.shape[0] // n
    for q in range(n):
        ga[q][...] = back[q * width : (q + 1) * width, :]

    terms = [
        lax.dot_general(left, gp, TN, preferred_element_type=F32)
        for j in range(n)
        for left in (agg[j][...], feat[j])
    ]

    @pl.when(step == 0)
    def _():
        for k, term in enumerate(terms):
            total[k] = term

    @pl.when(step > 0)
    def _():
        for k, term in enumerate(terms):
            total[k] += term

    @pl.when(step == pl.num_programs(0) - 1)
    def _():
        rows = terms_ref.shape[2]
        for j in range(n):
            for kind in range(2):
                term = total[2 * j + kind].astype(BF16)
                for i in range(n):
                    q = lax.rem(me_ref[0] + i, n)
                    for k in range(width // rows):
                        at = (kind * (width // rows) + k) * n + q
                        terms_ref[at, j] = term[k * rows : (k + 1) * rows, i * width : (i + 1) * width]


def dense(me, agg, both, wn, ws, dom_count):
    n = len(agg)
    rows, width = agg[0].shape
    full = n * width
    size = 256
    piece = (dom_count, n, 2 * width * n // dom_count, width)
    weight = pl.BlockSpec((full, full), lambda i, me: (0, 0))
    whole = pl.BlockSpec((size, full), lambda i, me: (i, 0))
    results = pl.pallas_call(
        functools.partial(dense_kernel, n=n),
        grid_spec=pltpu.PrefetchScalarGridSpec(
            num_scalar_prefetch=1,
            grid=(rows // size,),
            in_specs=[pl.BlockSpec((size, width), lambda i, me: (i, 0))] * n
            + [pl.BlockSpec((2, size, width), lambda i, me: (0, i, 0))] * n
            + [weight, weight],
            out_specs=[pl.BlockSpec((width, size), lambda i, me: (0, i))] * n
            + [whole, whole, pl.BlockSpec(piece, lambda i, me: (0, 0, 0, 0))],
            scratch_shapes=[pltpu.VMEM((2 * n, width, full), F32)],
        ),
        out_shape=[shape((width, rows), BF16)] * n
        + [pltpu.HBM((rows, full), BF16)] * 2
        + [pltpu.HBM(piece, BF16)],
        compiler_params=params(24),
        cost_estimate=cost(10 * rows * full * full, 9e6, rows * full),
        name="dense",
    )(me, *agg, *both, wn, ws)
    return results[:n], *results[n:]


PIECES = 6


def spmm_back_kernel(me_ref, pos_ref, *refs, n):
    adj_ref, ga = refs[0], refs[1 : 1 + n]
    local_ref, away_ref, total, left_ref, stage, sems, adj, adj_sems = refs[1 + n :]
    chunk, part = pl.program_id(0), pl.program_id(1)
    inner = adj_sems.shape[0] // n
    step = chunk * inner + part
    per_row = adj.shape[1]
    copy_of = adj_copies(adj_ref, adj, adj_sems, inner, lambda c: lax.rem(me_ref[0] + n - c, n))
    size = BLOCKS * TILE

    @pl.when((chunk == 0) & (part == 0))
    def _():
        for k in range(adj_sems.shape[0]):
            copy_of(k).start()
        total[...] = jnp.zeros_like(total)

    for s in range(n):

        @pl.when((chunk == s) & (part == 0))
        def _():
            for k in range(left_ref.shape[0]):
                left_ref[k] = ga[s][:, k * size : (k + 1) * size]

    copy_of(step).wait()
    first = (lax.rem(me_ref[0] + n - chunk, n) * pl.num_programs(1) + part) * BLOCKS
    for r in range(BLOCKS):
        base = (first + r) * per_row
        left = left_ref[part, :, r * TILE : (r + 1) * TILE]
        for t in range(0, per_row, 2):
            right = jnp.concatenate([adj[step * BLOCKS + r, t], adj[step * BLOCKS + r, t + 1]], axis=1)
            both = jnp.dot(left, right, preferred_element_type=F32)
            total[pos_ref[base + t]] += both[:, :TILE]
            total[pos_ref[base + t + 1]] += both[:, TILE:]

    @pl.when((chunk == n - 1) & (part == pl.num_programs(1) - 1))
    def _():
        own = local_ref.shape[0]
        step = away_ref.shape[0] // PIECES
        copies = [pltpu.make_async_copy(total.at[pl.ds(0, own)], local_ref, sems.at[PIECES])]
        copies[0].start()
        for k in range(PIECES):
            stage[k * step : (k + 1) * step] = total[own + k * step : own + (k + 1) * step].astype(BF16)
            copies.append(
                pltpu.make_async_copy(
                    stage.at[pl.ds(k * step, step)], away_ref.at[pl.ds(k * step, step)], sems.at[k]
                )
            )
            copies[-1].start()
        for copy in copies:
            copy.wait()


def spmm_back(me, pos, adj, ga, own, away):
    n = len(ga)
    row_tiles, per_row = adj.shape[:2]
    rows = ga[0].shape[1]
    inner = row_tiles // n // BLOCKS
    return pl.pallas_call(
        functools.partial(spmm_back_kernel, n=n),
        grid_spec=pltpu.PrefetchScalarGridSpec(
            num_scalar_prefetch=2,
            grid=(n, inner),
            in_specs=[pl.BlockSpec(memory_space=pl.ANY)]
            + [pl.BlockSpec((TILE, rows), lambda i, k, me, pos: (0, 0))] * n,
            out_specs=[pl.BlockSpec(memory_space=pl.ANY)] * 2,
            scratch_shapes=[
                pltpu.VMEM((own + away, TILE, TILE), F32),
                pltpu.VMEM((inner, TILE, BLOCKS * TILE), BF16),
                pltpu.VMEM((away, TILE, TILE), BF16),
                pltpu.SemaphoreType.DMA((PIECES + 1,)),
                pltpu.VMEM(adj.shape, BF16),
                pltpu.SemaphoreType.DMA((n * inner,)),
            ],
        ),
        out_shape=[pltpu.HBM((own, TILE, TILE), F32), pltpu.HBM((away, TILE, TILE), BF16)],
        compiler_params=params(52),
        cost_estimate=cost(24 * row_tiles * per_row * TILE**3, 2.2e7),
        name="spmm_back",
    )(me, pos, adj, *ga)


def late_kernel(act_ref, gp_ref, ws_ref, after_ref, *pieces):
    del after_ref
    direct = lax.dot_general(gp_ref[...], ws_ref[...], NT, preferred_element_type=F32).astype(BF16)
    for j, piece in enumerate(pieces):
        piece[0] = act_ref[:, j * TILE : (j + 1) * TILE]
        piece[1] = direct[:, j * TILE : (j + 1) * TILE]


def late(act, gp, ws, after, n):
    rows, full = act.shape
    size = 256
    share = pl.BlockSpec((size, full), lambda i: (i, 0))
    return pl.pallas_call(
        late_kernel,
        grid=(rows // size,),
        in_specs=[
            share,
            share,
            pl.BlockSpec((full, full), lambda i: (0, 0)),
            pl.BlockSpec(memory_space=pl.ANY),
        ],
        out_specs=[pl.BlockSpec((2, size, TILE), lambda i: (0, i, 0))] * n,
        out_shape=[shape((2, rows, TILE), BF16)] * n,
        compiler_params=params(24),
        cost_estimate=cost(1e10, 6e6),
        name="late",
    )(act, gp, ws, after)


def finish_kernel(me_ref, ext_ref, *refs):
    pieces, (out_ref, grad_ref) = refs[:-2], refs[-2:]
    for s, piece in enumerate(pieces):

        @pl.when(pl.program_id(0) == s)
        def _():
            out_ref[...] = piece[0]
            for k in range(ext_ref.shape[0]):
                rows = slice(k * TILE, (k + 1) * TILE)
                total = piece[1, rows, :].astype(F32) + jnp.transpose(ext_ref[k])
                grad_ref[rows, :] = total.astype(BF16)


def finish(me, ext, pieces):
    n = len(pieces)
    share = pieces[0].shape[1]
    placed = pl.BlockSpec((share, TILE), lambda i, me: (lax.rem(me[0] + n - i, n), 0))
    return pl.pallas_call(
        finish_kernel,
        grid_spec=pltpu.PrefetchScalarGridSpec(
            num_scalar_prefetch=1,
            grid=(n,),
            in_specs=[
                pl.BlockSpec(
                    (share // TILE, TILE, TILE), lambda i, me: (lax.rem(me[0] + n - i, n), 0, 0)
                )
            ]
            + [pl.BlockSpec((2, share, TILE), lambda i, me: (0, 0, 0))] * n,
            out_specs=[placed, placed],
        ),
        out_shape=[shape((n * share, TILE), BF16)] * 2,
        compiler_params=params(24),
        cost_estimate=cost(1e6, 7e6),
        name="finish",
    )(me, ext, *pieces)


def scatter_kernel(ids_ref, counts_ref, val_ref, out_ref):
    groups = out_ref.shape[0] // LOW

    @pl.when(pl.program_id(0) == 0)
    def _():
        out_ref[...] = jnp.zeros_like(out_ref)

    for p in range(0, ids_ref.shape[0], 2):
        ids = masked_ids(ids_ref, counts_ref, p, 2)
        onehot = low_onehot(ids)
        values = jnp.concatenate([val_ref[p * CHUNKS + k] for k in range(2 * CHUNKS)], axis=1)
        zero = jnp.zeros_like(values)
        which = jnp.broadcast_to((ids >> LOW_BITS).astype(jnp.int16), values.shape)
        for g in range(0, groups, 2):
            pair = [jnp.where(which == jnp.int16(k), values, zero) for k in (g, g + 1)]
            both = lax.dot_general(
                onehot, jnp.concatenate(pair, axis=0), NT, preferred_element_type=F32
            )
            out_ref[g * LOW : (g + 1) * LOW, :] += both[:, :TILE]
            out_ref[(g + 1) * LOW : (g + 2) * LOW, :] += both[:, TILE:]


def scatter_rows(ids, counts, values, rows):
    peers = ids.shape[0]
    size = 8
    return pl.pallas_call(
        scatter_kernel,
        grid=(peers // size,),
        in_specs=[
            pl.BlockSpec((size, B), lambda i: (i, 0)),
            pl.BlockSpec(memory_space=pltpu.SMEM),
            pl.BlockSpec((size * CHUNKS, TILE, TILE), lambda i: (i, 0, 0)),
        ],
        out_specs=pl.BlockSpec((rows, TILE), lambda i: (0, 0)),
        out_shape=shape((rows, TILE), F32),
        compiler_params=params(40),
        cost_estimate=cost(8 * ids.size * rows * TILE, 4e6),
        name="scatter_rows",
    )(ids, counts, values)


def sum_kernel(terms_ref, after_ref, *outs):
    del after_ref
    total = jnp.sum(terms_ref[...].astype(F32), axis=0).astype(BF16)
    for j, out in enumerate(outs):
        out[...] = total[j]


def sum_terms(terms, after):
    n = terms.shape[1]
    return pl.pallas_call(
        sum_kernel,
        in_specs=[pl.BlockSpec(memory_space=pltpu.VMEM), pl.BlockSpec(memory_space=pl.ANY)],
        out_specs=[pl.BlockSpec(memory_space=pltpu.VMEM)] * n,
        out_shape=[shape(terms.shape[2:], BF16)] * n,
        compiler_params=params(16),
        cost_estimate=cost(1e9, 1e6),
        name="sum_terms",
    )(terms, after)


def spread_kernel(*refs):
    terms, out_ref = refs[:-1], refs[-1]
    total = terms[0][...].astype(F32)
    for term in terms[1:]:
        total = total + term[...].astype(F32)
    out_ref[...] = jnp.broadcast_to(total.astype(BF16)[None], out_ref.shape)


def spread_terms(terms, dom_count):
    vmem = pl.BlockSpec(memory_space=pltpu.VMEM)
    return pl.pallas_call(
        spread_kernel,
        in_specs=[vmem] * len(terms),
        out_specs=vmem,
        out_shape=shape((dom_count, *terms[0].shape), BF16),
        compiler_params=params(8),
        cost_estimate=cost(1e5, 3e5),
        name="spread_terms",
    )(*terms)


def tie_kernel(value_ref, after_ref, out_ref):
    del value_ref, after_ref, out_ref


def tie(value, after):
    anywhere = pl.BlockSpec(memory_space=pl.ANY)
    return pl.pallas_call(
        tie_kernel,
        in_specs=[anywhere, anywhere],
        out_specs=anywhere,
        out_shape=shape(value.shape, value.dtype),
        input_output_aliases={0: 0},
        compiler_params=params(8),
        name="tie",
    )(value, after)


def place_kernel(terms_ref, *outs):
    rows, width = terms_ref.shape[1:]
    n = outs[0].shape[1] // width
    for at in range(terms_ref.shape[0]):
        group, q = at // n, at % n
        per = outs[0].shape[0] // rows
        out = outs[group // per]
        first = group % per * rows
        out[first : first + rows, q * width : (q + 1) * width] = terms_ref[at].astype(F32)


def place_terms(terms, width, n):
    return pl.pallas_call(
        place_kernel,
        out_shape=[shape((width, n * width), F32)] * 2,
        compiler_params=params(8),
        cost_estimate=cost(1e5, 8e5),
        name="place_terms",
    )(terms)


def per_device(
    features, stale_features, grad_output, w_neigh, w_self, adj_tiles, tile_cols, send_idx, counts
):
    dom_count = lax.axis_size("dom")
    n = lax.axis_size("rep")
    row_count, width = features.shape
    row_tiles = row_count // TILE
    swap = functools.partial(
        lax.all_to_all, axis_name="dom", split_axis=0, concat_axis=0, tiled=True
    )
    me = lax.axis_index("rep").astype(jnp.int32).reshape(1)

    ids = send_idx[0]
    pos = tile_cols[0].reshape(-1)
    adj = adj_tiles[0]

    packed = gather_rows(ids, counts, stale_features)
    halo = swap(packed)
    own, wn, ws, pieces = prep(me, features, grad_output, w_neigh, w_self, packed, n)
    both = relative(exchange(pieces))

    agg = relative(exchange(spmm(me, pos, adj, [own, halo], n, 0, n, [])))
    grad_agg, act, grad_pre, terms = dense(me, agg, both, wn, ws, dom_count)
    grad_agg = exchange(grad_agg)
    terms = swap(terms)

    local, away = spmm_back(me, pos, adj, grad_agg, row_tiles, dom_count * CHUNKS)
    returned = swap(away)
    pieces = exchange(late(act, grad_pre, ws, away, n))
    out, grad_input = finish(me, local, pieces)
    terms = exchange(sum_terms(terms, away))

    terms = swap(tie(spread_terms(terms, dom_count), returned))
    grad_stale = scatter_rows(ids, counts, returned, row_count)
    grad_neigh, grad_self = place_terms(terms, width, n)
    return (out, grad_input, grad_stale, grad_neigh, grad_self)


def solution(mesh):
    in_specs = (
        P("dom", "rep"),
        P("dom", "rep"),
        P("dom", "rep"),
        P(),
        P(),
        P("dom", None, None, None, None),
        P("dom", None, None),
        P("dom", None, None),
        P("dom", None),
    )
    out_specs = (P("dom", "rep"), P("dom", "rep"), P("dom", "rep"), P("rep", None), P("rep", None))
    return jax.shard_map(
        per_device, mesh=mesh, in_specs=in_specs, out_specs=out_specs, check_vma=False
    )
```

```python
import functools

import jax
import jax.numpy as jnp
from jax import lax
from jax.experimental import pallas as pl
from jax.experimental.pallas import tpu as pltpu
from jax.sharding import PartitionSpec as P

TILE = 128
B = 384
CHUNKS = B // TILE
LOW_BITS = 9
LOW = 1 << LOW_BITS
F32 = jnp.float32
BF16 = jnp.bfloat16
NT = (((1,), (1,)), ((), ()))
TN = (((0,), (0,)), ((), ()))


def params(mib):
    return pltpu.CompilerParams(vmem_limit_bytes=mib * 1024 * 1024)


def cost(flops, nbytes, trans=0):
    return pl.CostEstimate(flops=int(flops), bytes_accessed=int(nbytes), transcendentals=int(trans))


def shape(dims, dtype):
    return jax.ShapeDtypeStruct(dims, dtype)


def turned(block):
    return jnp.transpose(block.astype(F32))


def masked_ids(ids_ref, counts_ref, first, peers):
    base = pl.program_id(0) * ids_ref.shape[0]
    slot = lax.broadcasted_iota(jnp.int32, (1, ids_ref.shape[1]), 1)
    rows = [
        jnp.where(slot < counts_ref[0, base + p], ids_ref[p : p + 1, :], -1)
        for p in range(first, first + peers)
    ]
    return jnp.concatenate(rows, axis=1)


def low_onehot(ids):
    spot = lax.broadcasted_iota(jnp.int32, (LOW, ids.shape[1]), 0).astype(jnp.int16)
    low = jnp.broadcast_to((ids & (LOW - 1)).astype(jnp.int16), spot.shape)
    return jnp.where(spot == low, jnp.ones(spot.shape, BF16), jnp.zeros(spot.shape, BF16))


def in_group(ids, g):
    return (ids >= g * LOW) & (ids < (g + 1) * LOW)


def gather_kernel(ids_ref, counts_ref, table_ref, out_ref, flipped):
    groups = table_ref.shape[0] // LOW

    @pl.when(pl.program_id(0) == 0)
    def _():
        for g in range(groups):
            for k in range(LOW // TILE):
                block = table_ref[g * LOW + k * TILE : g * LOW + (k + 1) * TILE, :]
                flipped[g * TILE : (g + 1) * TILE, k * TILE : (k + 1) * TILE] = turned(block).astype(
                    BF16
                )

    for p in range(0, ids_ref.shape[0], 2):
        ids = masked_ids(ids_ref, counts_ref, p, 2)
        found = jnp.dot(flipped[...], low_onehot(ids), preferred_element_type=F32)
        total = jnp.zeros((TILE, ids.shape[1]), F32)
        for g in range(groups):
            total = jnp.where(in_group(ids, g), found[g * TILE : (g + 1) * TILE, :], total)
        total = total.astype(BF16)
        for k in range(2 * CHUNKS):
            out_ref[p * CHUNKS + k] = total[:, k * TILE : (k + 1) * TILE]


def gather_rows(ids, counts, table):
    peers = ids.shape[0]
    size = 8
    rows, cols = table.shape
    return pl.pallas_call(
        gather_kernel,
        grid=(peers // size,),
        in_specs=[
            pl.BlockSpec((size, B), lambda i: (i, 0)),
            pl.BlockSpec(memory_space=pltpu.SMEM),
            pl.BlockSpec((rows, cols), lambda i: (0, 0)),
        ],
        out_specs=pl.BlockSpec((size * CHUNKS, TILE, TILE), lambda i: (i, 0, 0)),
        out_shape=shape((peers * CHUNKS, TILE, TILE), BF16),
        scratch_shapes=[pltpu.VMEM((rows // LOW * TILE, LOW), BF16)],
        compiler_params=params(56),
        cost_estimate=cost(2 * ids.size * rows * cols, 4e6),
        name="gather_rows",
    )(ids, counts, table)


def exchange(pieces):
    n = len(pieces)
    return [pieces[0]] + [
        lax.ppermute(pieces[s], "rep", [(i, (i + s) % n) for i in range(n)]) for s in range(1, n)
    ]


def relative(received):
    n = len(received)
    return [received[(n - j) % n] for j in range(n)]


def prep_kernel(me_ref, feat_ref, up_ref, wn_ref, ws_ref, after_ref, own_ref, wn_out, ws_out, *pieces):
    del after_ref
    step = pl.program_id(0)
    n = len(pieces)
    for k in range(own_ref.shape[0]):
        own_ref[k] = turned(feat_ref[k * TILE : (k + 1) * TILE, :]).astype(BF16)
    for j, piece in enumerate(pieces):
        column = pl.multiple_of(lax.rem(me_ref[0] + j, n) * TILE, TILE)
        wn_out[:, j * TILE : (j + 1) * TILE] = wn_ref[:, pl.ds(column, TILE)]
        ws_out[:, j * TILE : (j + 1) * TILE] = ws_ref[:, pl.ds(column, TILE)]

        @pl.when(step == j)
        def _():
            piece[0] = feat_ref[...]
            piece[1] = up_ref[...]


def prep(me, features, upstream, wn, ws, after, n):
    rows, width = features.shape
    share = rows // n
    full = wn.shape[0]
    chunk = pl.BlockSpec((share, width), lambda i, me: (lax.rem(me[0] + i, n), 0))
    weight = pl.BlockSpec((width, full), lambda i, me: (lax.rem(me[0] + i, n), 0))
    placed = pl.BlockSpec((width, full), lambda i, me: (i, 0))
    own, wn, ws, *pieces = pl.pallas_call(
        prep_kernel,
        grid_spec=pltpu.PrefetchScalarGridSpec(
            num_scalar_prefetch=1,
            grid=(n,),
            in_specs=[chunk, chunk, weight, weight, pl.BlockSpec(memory_space=pl.ANY)],
            out_specs=[
                pl.BlockSpec(
                    (share // TILE, TILE, TILE), lambda i, me: (lax.rem(me[0] + i, n), 0, 0)
                ),
                placed,
                placed,
            ]
            + [pl.BlockSpec((2, share, width), lambda i, me: (0, 0, 0))] * n,
        ),
        out_shape=[
            pltpu.HBM((rows // TILE, TILE, TILE), BF16),
            pltpu.HBM((full, full), BF16),
            pltpu.HBM((full, full), BF16),
        ]
        + [shape((2, share, width), BF16)] * n,
        compiler_params=params(56),
        cost_estimate=cost(1e10, 6e6),
        name="prep",
    )(me, features, upstream, wn, ws, after)
    return own, wn, ws, pieces


BLOCKS = 3


def adj_copies(adj_ref, held, sems, inner, chunk_of):
    def copy(step):
        first = (chunk_of(step // inner) * inner + lax.rem(step, inner)) * BLOCKS
        return pltpu.make_async_copy(
            adj_ref.at[pl.ds(first, BLOCKS)], held.at[pl.ds(step * BLOCKS, BLOCKS)], sems.at[step]
        )

    return copy


def spmm_kernel(me_ref, pos_ref, *refs, n, start_chunk, extras):
    adj_ref, parts, outs, (ext, sems, adj, adj_sems) = (
        refs[0],
        refs[1 : 3],
        refs[3 + extras : -4],
        refs[-4:],
    )
    chunk, part = pl.program_id(0), pl.program_id(1)
    inner = adj_sems.shape[0] // len(outs)
    step = chunk * inner + part
    per_row = adj.shape[1]
    copy_of = adj_copies(
        adj_ref, adj, adj_sems, inner, lambda c: lax.rem(me_ref[0] + start_chunk + c, n)
    )

    @pl.when((chunk == 0) & (part == 0))
    def _():
        copies, start, at = [], 0, 0
        for source in parts:
            size = source.shape[0] // 4
            for k in range(4):
                copies.append(
                    pltpu.make_async_copy(
                        source.at[pl.ds(k * size, size)], ext.at[pl.ds(start, size)], sems.at[at]
                    )
                )
                start, at = start + size, at + 1
        for copy in copies:
            copy.start()
        copy_of(0).start()
        for copy in copies:
            copy.wait()
        for k in range(1, adj_sems.shape[0]):
            copy_of(k).start()

    copy_of(step).wait()
    first = (lax.rem(me_ref[0] + start_chunk + chunk, n) * inner + part) * BLOCKS
    done = []
    for r in range(BLOCKS):
        base = (first + r) * per_row
        total = None
        for t in range(0, per_row, 2):
            left = jnp.concatenate([adj[step * BLOCKS + r, t], adj[step * BLOCKS + r, t + 1]], axis=1)
            right = jnp.concatenate([ext[pos_ref[base + t]], ext[pos_ref[base + t + 1]]], axis=1)
            term = lax.dot_general(left, right, NT, preferred_element_type=F32)
            total = term if total is None else total + term
        done.append(total.astype(BF16))
    done = jnp.concatenate(done, axis=0)
    size = BLOCKS * TILE
    place = pl.ds(pl.multiple_of(part * size, size), size)
    for j, out in enumerate(outs):

        @pl.when(chunk == j)
        def _():
            out[place, :] = done


def spmm(me, pos, adj, parts, n, start_chunk, count, after):
    row_tiles, per_row = adj.shape[:2]
    inner = row_tiles // n // BLOCKS
    share = row_tiles // n * TILE
    col_tiles = sum(p.shape[0] for p in parts)
    return pl.pallas_call(
        functools.partial(spmm_kernel, n=n, start_chunk=start_chunk, extras=len(after)),
        grid_spec=pltpu.PrefetchScalarGridSpec(
            num_scalar_prefetch=2,
            grid=(count, inner),
            in_specs=[pl.BlockSpec(memory_space=pl.ANY)] * (1 + len(parts) + len(after)),
            out_specs=[pl.BlockSpec((share, TILE), lambda i, k, me, pos: (0, 0))] * count,
            scratch_shapes=[
                pltpu.VMEM((col_tiles, TILE, TILE), BF16),
                pltpu.SemaphoreType.DMA((4 * len(parts),)),
                pltpu.VMEM((count * inner * BLOCKS, *adj.shape[1:]), BF16),
                pltpu.SemaphoreType.DMA((count * inner,)),
            ],
        ),
        out_shape=[shape((share, TILE), BF16)] * count,
        compiler_params=params(56),
        cost_estimate=cost(2 * count * share * per_row * TILE**2 * 8, 1e7),
        name="spmm",
    )(me, pos, adj, *parts, *after)


def joined(refs):
    return jnp.concatenate([ref[...] for ref in refs], axis=1)


def dense_kernel(me_ref, *refs, n):
    agg, both, (wn_ref, ws_ref), rest = refs[:n], refs[n : 2 * n], refs[2 * n : 2 * n + 2], refs[2 * n + 2 :]
    ga, (act_ref, gp_ref, terms_ref, total) = rest[:n], rest[n:]
    step = pl.program_id(0)
    wn = wn_ref[...]
    feat = [ref[0] for ref in both]
    v = jnp.dot(joined(agg), wn, preferred_element_type=F32) + jnp.dot(
        jnp.concatenate(feat, axis=1), ws_ref[...], preferred_element_type=F32
    )
    root = 0.7978845608028654
    square = v * v
    t = jnp.tanh(root * v * (1.0 + 0.044715 * square))
    half = 0.5 * (1.0 + t)
    slope = half + 0.5 * v * (1.0 - t * t) * (root * (1.0 + 0.134145 * square))
    gp = (joined([ref.at[1] for ref in both]).astype(F32) * slope).astype(BF16)
    act_ref[...] = (v * half).astype(BF16)
    gp_ref[...] = gp
    back = lax.dot_general(wn, gp, NT, preferred_element_type=F32).astype(BF16)
    width = back.shape[0] // n
    for q in range(n):
        ga[q][...] = back[q * width : (q + 1) * width, :]

    terms = [
        lax.dot_general(left, gp, TN, preferred_element_type=F32)
        for j in range(n)
        for left in (agg[j][...], feat[j])
    ]

    @pl.when(step == 0)
    def _():
        for k, term in enumerate(terms):
            total[k] = term

    @pl.when(step > 0)
    def _():
        for k, term in enumerate(terms):
            total[k] += term

    @pl.when(step == pl.num_programs(0) - 1)
    def _():
        rows = terms_ref.shape[2]
        for j in range(n):
            for kind in range(2):
                term = total[2 * j + kind].astype(BF16)
                for i in range(n):
                    q = lax.rem(me_ref[0] + i, n)
                    for k in range(width // rows):
                        at = (kind * (width // rows) + k) * n + q
                        terms_ref[at, j] = term[k * rows : (k + 1) * rows, i * width : (i + 1) * width]


def dense(me, agg, both, wn, ws, dom_count):
    n = len(agg)
    rows, width = agg[0].shape
    full = n * width
    size = 256
    piece = (dom_count, n, 2 * width * n // dom_count, width)
    weight = pl.BlockSpec((full, full), lambda i, me: (0, 0))
    whole = pl.BlockSpec((size, full), lambda i, me: (i, 0))
    results = pl.pallas_call(
        functools.partial(dense_kernel, n=n),
        grid_spec=pltpu.PrefetchScalarGridSpec(
            num_scalar_prefetch=1,
            grid=(rows // size,),
            in_specs=[pl.BlockSpec((size, width), lambda i, me: (i, 0))] * n
            + [pl.BlockSpec((2, size, width), lambda i, me: (0, i, 0))] * n
            + [weight, weight],
            out_specs=[pl.BlockSpec((width, size), lambda i, me: (0, i))] * n
            + [whole, whole, pl.BlockSpec(piece, lambda i, me: (0, 0, 0, 0))],
            scratch_shapes=[pltpu.VMEM((2 * n, width, full), F32)],
        ),
        out_shape=[shape((width, rows), BF16)] * n
        + [pltpu.HBM((rows, full), BF16)] * 2
        + [pltpu.HBM(piece, BF16)],
        compiler_params=params(52),
        cost_estimate=cost(10 * rows * full * full, 9e6, rows * full),
        name="dense",
    )(me, *agg, *both, wn, ws)
    return results[:n], *results[n:]


PIECES = 6


def spmm_back_kernel(me_ref, pos_ref, *refs, n):
    adj_ref, ga = refs[0], refs[1 : 1 + n]
    local_ref, away_ref, total, left_ref, stage, sems, adj, adj_sems = refs[1 + n :]
    chunk, part = pl.program_id(0), pl.program_id(1)
    inner = adj_sems.shape[0] // n
    step = chunk * inner + part
    per_row = adj.shape[1]
    copy_of = adj_copies(adj_ref, adj, adj_sems, inner, lambda c: lax.rem(me_ref[0] + n - c, n))
    size = BLOCKS * TILE

    @pl.when((chunk == 0) & (part == 0))
    def _():
        for k in range(adj_sems.shape[0]):
            copy_of(k).start()
        total[...] = jnp.zeros_like(total)

    for s in range(n):

        @pl.when((chunk == s) & (part == 0))
        def _():
            for k in range(left_ref.shape[0]):
                left_ref[k] = ga[s][:, k * size : (k + 1) * size]

    copy_of(step).wait()
    first = (lax.rem(me_ref[0] + n - chunk, n) * pl.num_programs(1) + part) * BLOCKS
    for r in range(BLOCKS):
        base = (first + r) * per_row
        left = left_ref[part, :, r * TILE : (r + 1) * TILE]
        for t in range(0, per_row, 2):
            right = jnp.concatenate([adj[step * BLOCKS + r, t], adj[step * BLOCKS + r, t + 1]], axis=1)
            both = jnp.dot(left, right, preferred_element_type=F32)
            total[pos_ref[base + t]] += both[:, :TILE]
            total[pos_ref[base + t + 1]] += both[:, TILE:]

    @pl.when((chunk == n - 1) & (part == pl.num_programs(1) - 1))
    def _():
        own = local_ref.shape[0]
        step = away_ref.shape[0] // PIECES
        copies = [pltpu.make_async_copy(total.at[pl.ds(0, own)], local_ref, sems.at[PIECES])]
        copies[0].start()
        for k in range(PIECES):
            stage[k * step : (k + 1) * step] = total[own + k * step : own + (k + 1) * step].astype(BF16)
            copies.append(
                pltpu.make_async_copy(
                    stage.at[pl.ds(k * step, step)], away_ref.at[pl.ds(k * step, step)], sems.at[k]
                )
            )
            copies[-1].start()
        for copy in copies:
            copy.wait()


def spmm_back(me, pos, adj, ga, own, away):
    n = len(ga)
    row_tiles, per_row = adj.shape[:2]
    rows = ga[0].shape[1]
    inner = row_tiles // n // BLOCKS
    return pl.pallas_call(
        functools.partial(spmm_back_kernel, n=n),
        grid_spec=pltpu.PrefetchScalarGridSpec(
            num_scalar_prefetch=2,
            grid=(n, inner),
            in_specs=[pl.BlockSpec(memory_space=pl.ANY)]
            + [pl.BlockSpec((TILE, rows), lambda i, k, me, pos: (0, 0))] * n,
            out_specs=[pl.BlockSpec(memory_space=pl.ANY)] * 2,
            scratch_shapes=[
                pltpu.VMEM((own + away, TILE, TILE), F32),
                pltpu.VMEM((inner, TILE, BLOCKS * TILE), BF16),
                pltpu.VMEM((away, TILE, TILE), BF16),
                pltpu.SemaphoreType.DMA((PIECES + 1,)),
                pltpu.VMEM(adj.shape, BF16),
                pltpu.SemaphoreType.DMA((n * inner,)),
            ],
        ),
        out_shape=[pltpu.HBM((own, TILE, TILE), F32), pltpu.HBM((away, TILE, TILE), BF16)],
        compiler_params=params(52),
        cost_estimate=cost(24 * row_tiles * per_row * TILE**3, 2.2e7),
        name="spmm_back",
    )(me, pos, adj, *ga)


def late_kernel(act_ref, gp_ref, ws_ref, after_ref, *pieces):
    del after_ref
    direct = lax.dot_general(gp_ref[...], ws_ref[...], NT, preferred_element_type=F32).astype(BF16)
    for j, piece in enumerate(pieces):
        piece[0] = act_ref[:, j * TILE : (j + 1) * TILE]
        piece[1] = direct[:, j * TILE : (j + 1) * TILE]


def late(act, gp, ws, after, n):
    rows, full = act.shape
    size = 256
    share = pl.BlockSpec((size, full), lambda i: (i, 0))
    return pl.pallas_call(
        late_kernel,
        grid=(rows // size,),
        in_specs=[
            share,
            share,
            pl.BlockSpec((full, full), lambda i: (0, 0)),
            pl.BlockSpec(memory_space=pl.ANY),
        ],
        out_specs=[pl.BlockSpec((2, size, TILE), lambda i: (0, i, 0))] * n,
        out_shape=[shape((2, rows, TILE), BF16)] * n,
        compiler_params=params(24),
        cost_estimate=cost(1e10, 6e6),
        name="late",
    )(act, gp, ws, after)


def finish_kernel(me_ref, ext_ref, *refs):
    pieces, (out_ref, grad_ref) = refs[:-2], refs[-2:]
    for s, piece in enumerate(pieces):

        @pl.when(pl.program_id(0) == s)
        def _():
            out_ref[...] = piece[0]
            for k in range(ext_ref.shape[0]):
                rows = slice(k * TILE, (k + 1) * TILE)
                total = piece[1, rows, :].astype(F32) + jnp.transpose(ext_ref[k])
                grad_ref[rows, :] = total.astype(BF16)


def finish(me, ext, pieces):
    n = len(pieces)
    share = pieces[0].shape[1]
    placed = pl.BlockSpec((share, TILE), lambda i, me: (lax.rem(me[0] + n - i, n), 0))
    return pl.pallas_call(
        finish_kernel,
        grid_spec=pltpu.PrefetchScalarGridSpec(
            num_scalar_prefetch=1,
            grid=(n,),
            in_specs=[
                pl.BlockSpec(
                    (share // TILE, TILE, TILE), lambda i, me: (lax.rem(me[0] + n - i, n), 0, 0)
                )
            ]
            + [pl.BlockSpec((2, share, TILE), lambda i, me: (0, 0, 0))] * n,
            out_specs=[placed, placed],
        ),
        out_shape=[shape((n * share, TILE), BF16)] * 2,
        compiler_params=params(24),
        cost_estimate=cost(1e6, 7e6),
        name="finish",
    )(me, ext, *pieces)


def scatter_kernel(ids_ref, counts_ref, val_ref, out_ref):
    groups = out_ref.shape[0] // LOW

    @pl.when(pl.program_id(0) == 0)
    def _():
        out_ref[...] = jnp.zeros_like(out_ref)

    for p in range(0, ids_ref.shape[0], 2):
        ids = masked_ids(ids_ref, counts_ref, p, 2)
        onehot = low_onehot(ids)
        values = jnp.concatenate([val_ref[p * CHUNKS + k] for k in range(2 * CHUNKS)], axis=1)
        zero = jnp.zeros_like(values)
        which = jnp.broadcast_to((ids >> LOW_BITS).astype(jnp.int16), values.shape)
        for g in range(0, groups, 2):
            pair = [jnp.where(which == jnp.int16(k), values, zero) for k in (g, g + 1)]
            both = lax.dot_general(
                onehot, jnp.concatenate(pair, axis=0), NT, preferred_element_type=F32
            )
            out_ref[g * LOW : (g + 1) * LOW, :] += both[:, :TILE]
            out_ref[(g + 1) * LOW : (g + 2) * LOW, :] += both[:, TILE:]


def scatter_rows(ids, counts, values, rows):
    peers = ids.shape[0]
    size = 8
    return pl.pallas_call(
        scatter_kernel,
        grid=(peers // size,),
        in_specs=[
            pl.BlockSpec((size, B), lambda i: (i, 0)),
            pl.BlockSpec(memory_space=pltpu.SMEM),
            pl.BlockSpec((size * CHUNKS, TILE, TILE), lambda i: (i, 0, 0)),
        ],
        out_specs=pl.BlockSpec((rows, TILE), lambda i: (0, 0)),
        out_shape=shape((rows, TILE), F32),
        compiler_params=params(40),
        cost_estimate=cost(8 * ids.size * rows * TILE, 4e6),
        name="scatter_rows",
    )(ids, counts, values)


def sum_kernel(terms_ref, after_ref, *outs):
    del after_ref
    total = jnp.sum(terms_ref[...].astype(F32), axis=0).astype(BF16)
    for j, out in enumerate(outs):
        out[...] = total[j]


def sum_terms(terms, after):
    n = terms.shape[1]
    return pl.pallas_call(
        sum_kernel,
        in_specs=[pl.BlockSpec(memory_space=pltpu.VMEM), pl.BlockSpec(memory_space=pl.ANY)],
        out_specs=[pl.BlockSpec(memory_space=pltpu.VMEM)] * n,
        out_shape=[shape(terms.shape[2:], BF16)] * n,
        compiler_params=params(16),
        cost_estimate=cost(1e9, 1e6),
        name="sum_terms",
    )(terms, after)


def spread_kernel(*refs):
    terms, out_ref = refs[:-1], refs[-1]
    total = terms[0][...].astype(F32)
    for term in terms[1:]:
        total = total + term[...].astype(F32)
    out_ref[...] = jnp.broadcast_to(total.astype(BF16)[None], out_ref.shape)


def spread_terms(terms, dom_count):
    vmem = pl.BlockSpec(memory_space=pltpu.VMEM)
    return pl.pallas_call(
        spread_kernel,
        in_specs=[vmem] * len(terms),
        out_specs=vmem,
        out_shape=shape((dom_count, *terms[0].shape), BF16),
        compiler_params=params(8),
        cost_estimate=cost(1e5, 3e5),
        name="spread_terms",
    )(*terms)


def tie_kernel(value_ref, after_ref, out_ref):
    del value_ref, after_ref, out_ref


def tie(value, after):
    anywhere = pl.BlockSpec(memory_space=pl.ANY)
    return pl.pallas_call(
        tie_kernel,
        in_specs=[anywhere, anywhere],
        out_specs=anywhere,
        out_shape=shape(value.shape, value.dtype),
        input_output_aliases={0: 0},
        compiler_params=params(8),
        name="tie",
    )(value, after)


def place_kernel(terms_ref, *outs):
    rows, width = terms_ref.shape[1:]
    n = outs[0].shape[1] // width
    for at in range(terms_ref.shape[0]):
        group, q = at // n, at % n
        per = outs[0].shape[0] // rows
        out = outs[group // per]
        first = group % per * rows
        out[first : first + rows, q * width : (q + 1) * width] = terms_ref[at].astype(F32)


def place_terms(terms, width, n):
    return pl.pallas_call(
        place_kernel,
        out_shape=[shape((width, n * width), F32)] * 2,
        compiler_params=params(8),
        cost_estimate=cost(1e5, 8e5),
        name="place_terms",
    )(terms)


def per_device(
    features, stale_features, grad_output, w_neigh, w_self, adj_tiles, tile_cols, send_idx, counts
):
    dom_count = lax.axis_size("dom")
    n = lax.axis_size("rep")
    row_count, width = features.shape
    row_tiles = row_count // TILE
    swap = functools.partial(
        lax.all_to_all, axis_name="dom", split_axis=0, concat_axis=0, tiled=True
    )
    me = lax.axis_index("rep").astype(jnp.int32).reshape(1)

    ids = send_idx[0]
    pos = tile_cols[0].reshape(-1)
    adj = adj_tiles[0]

    packed = gather_rows(ids, counts, stale_features)
    halo = swap(packed)
    own, wn, ws, pieces = prep(me, features, grad_output, w_neigh, w_self, packed, n)
    both = relative(exchange(pieces))

    agg = relative(exchange(spmm(me, pos, adj, [own, halo], n, 0, n, [])))
    grad_agg, act, grad_pre, terms = dense(me, agg, both, wn, ws, dom_count)
    grad_agg = exchange(grad_agg)
    terms = swap(terms)

    local, away = spmm_back(me, pos, adj, grad_agg, row_tiles, dom_count * CHUNKS)
    returned = swap(away)
    pieces = exchange(late(act, grad_pre, ws, away, n))
    out, grad_input = finish(me, local, pieces)
    terms = exchange(sum_terms(terms, away))

    terms = swap(tie(spread_terms(terms, dom_count), returned))
    grad_stale = scatter_rows(ids, counts, returned, row_count)
    grad_neigh, grad_self = place_terms(terms, width, n)
    return (out, grad_input, grad_stale, grad_neigh, grad_self)


def solution(mesh):
    in_specs = (
        P("dom", "rep"),
        P("dom", "rep"),
        P("dom", "rep"),
        P(),
        P(),
        P("dom", None, None, None, None),
        P("dom", None, None),
        P("dom", None, None),
        P("dom", None),
    )
    out_specs = (P("dom", "rep"), P("dom", "rep"), P("dom", "rep"), P("rep", None), P("rep", None))
    return jax.shard_map(
        per_device, mesh=mesh, in_specs=in_specs, out_specs=out_specs, check_vma=False
    )
```
